32 devices in a mesh: seq: 8 (over z, x), chan: 4 (over y, core).
Axes of the slice: x: 2, y: 2, z: 4, core: 2. Of those that a mesh axis runs over, the one named last changes fastest.
Arguments:
- block_in: float32 [2, 1024, 1024], P(None, 'seq', 'chan'), may hold values from -6 to 6
- doc_lengths: int32 [2, 16], replicated, may hold values from 0 to 1024, as said below
- out_grad: float32 [2, 1024, 1024], P(None, 'seq', 'chan'), may hold values from -6 to 6
- first_gain: float32 [1024], P('chan'), may hold values from 0.5 to 1.5
- decay_rate: float32 [1024, 64], P('chan'), may hold values from 1.9073486e-05 to 0.05
- turn_angle: float32 [1024, 64], P('chan'), may hold values from -1 to 1
- out_real: float32 [1024, 64], P('chan'), may hold values from -0.75 to 0.75
- out_imag: float32 [1024, 64], P('chan'), may hold values from -0.75 to 0.75
- skip_gain: float32 [1024], P('chan'), may hold values from -4 to 4
- glu_value: bfloat16 [1024, 1024], P(None, 'chan'), may hold values from -0.5 to 0.5
- glu_gate: bfloat16 [1024, 1024], P(None, 'chan'), may hold values from -0.5 to 0.5
- second_gain: float32 [1024], P('chan'), may hold values from 0.5 to 1.5
- ffn_in: bfloat16 [1024, 4096], P(None, 'chan'), may hold values from -0.1875 to 0.1875
- ffn_out: bfloat16 [4096, 1024], P('chan'), may hold values from -0.1875 to 0.1875
Outputs:
- block_out: float32 [2, 1024, 1024], P(None, 'seq', 'chan')
- in_grad: float32 [2, 1024, 1024], P(None, 'seq', 'chan')
- first_gain_grad: float32 [1024], P('chan')
- decay_rate_grad: float32 [1024, 64], P('chan')
- turn_angle_grad: float32 [1024, 64], P('chan')
- out_real_grad: float32 [1024, 64], P('chan')
- out_imag_grad: float32 [1024, 64], P('chan')
- skip_gain_grad: float32 [1024], P('chan')
- glu_value_grad: float32 [1024, 1024], P(None, 'chan')
- glu_gate_grad: float32 [1024, 1024], P(None, 'chan')
- second_gain_grad: float32 [1024], P('chan')
- ffn_in_grad: float32 [1024, 4096], P(None, 'chan')
- ffn_out_grad: float32 [4096, 1024], P('chan')
The draws below stay inside these ranges and needn't reach their ends.
Inputs may be any that keep to these rules, and one draw needn't show every extreme that they name: `doc_lengths`: in every stream the lengths add up to 1024 or less; the positions after them are padding; documents may be empty.
All inputs are finite; a program needn't handle non-finite values.
Results may differ from the reference program's by a relative error of at most 0.0066.
Values may be sent and summed in bfloat16 or wider, within the bound.
A program may use at most 192 MiB of HBM per device.

```python
import math
import jax
import jax.numpy as jnp
from jax import lax

D = 1024
NS = 64
FF = 4096
STREAMS = 2
LC = 128
NDOC = 16
SLEN = 1024


def draw_doc_lengths(key, part):
    subkeys = jax.random.split(key, 3)
    spanning = jax.random.randint(subkeys[0], (), 0, STREAMS)
    padding = jax.random.randint(subkeys[1], (STREAMS,), 0, LC)
    exponents = jax.random.randint(subkeys[2], (STREAMS, NDOC), 0, 8)
    weights = jnp.left_shift(jnp.ones((STREAMS, NDOC), jnp.int32), exponents)
    stream_total = SLEN - padding
    spread = stream_total[:, None] * weights // jnp.sum(weights, axis=1, keepdims=True)
    spread = spread.at[:, -1].add(stream_total - jnp.sum(spread, axis=1))
    slot = jnp.arange(NDOC, dtype=jnp.int32)
    span_row = jnp.where(slot == 1, SLEN, 0).astype(jnp.int32)
    chosen = (jnp.arange(STREAMS) == spanning)[:, None]
    return jnp.where(chosen, span_row[None, :], spread).astype(jnp.int32)


def levels(own_key, dims, cuts, low, largest):
    loudness, own = 1.0, jax.random.fold_in(own_key, 6)
    for axis_at, shards_of in cuts:
        steps = jnp.exp(jax.random.uniform(jax.random.fold_in(own, axis_at), (shards_of,), jnp.float32, low / len(cuts), largest / len(cuts)))
        loudness = loudness * jnp.repeat(steps, dims[axis_at] // shards_of).reshape([-1 if axis == axis_at else 1 for axis in range(len(dims))])
    return loudness


def noise(own_key, shape, scale, most, cuts=(), kind=jnp.bfloat16):
    factor_of = levels(own_key, shape, cuts, -0.22, 0.18) if cuts else 1.0
    values = jax.random.normal(own_key, shape, jnp.float32) * scale * factor_of
    return jnp.minimum(jnp.maximum(values, -most), most).astype(kind)


def setup_inputs(seed: int = 0) -> dict:
    keys = jax.random.split(jax.random.key(seed), 15)
    return {
        "block_in": noise(keys[0], (STREAMS, SLEN, D), 1.0, 6.0, ((1, 8), (2, 4)), jnp.float32),
        "doc_lengths": draw_doc_lengths(jax.random.fold_in(keys[14], 71), 0),
        "out_grad": noise(keys[2], (STREAMS, SLEN, D), 1.0, 6.0, ((1, 8), (2, 4)), jnp.float32),
        "first_gain": jnp.clip(1.0 + 0.1 * jax.random.normal(keys[3], (D,), jnp.float32), 0.5, 1.5),
        "decay_rate": jnp.clip(jnp.exp(math.log(0.05) - 7.871479 * jax.random.uniform(keys[4], (D, NS), jnp.float32) ** levels(keys[4], (D, NS), ((0, 4),), -0.2, 0.2)), 1.9073486328125e-05, 0.05),
        "turn_angle": jnp.clip(jax.random.uniform(keys[5], (D, NS), jnp.float32, -1.0, 1.0) * levels(keys[5], (D, NS), ((0, 4),), -0.4, 0.0), -1.0, 1.0),
        "out_real": noise(keys[6], (D, NS), NS ** -0.5, 0.75, ((0, 4),), jnp.float32),
        "out_imag": noise(keys[7], (D, NS), NS ** -0.5, 0.75, ((0, 4),), jnp.float32),
        "skip_gain": noise(keys[8], (D,), 1.0, 4.0, ((0, 4),), jnp.float32),
        "glu_value": noise(keys[9], (D, D), (D // 8) ** -0.5, 0.5, ((1, 4),)),
        "glu_gate": noise(keys[10], (D, D), (D // 8) ** -0.5, 0.5, ((1, 4),)),
        "second_gain": jnp.clip(1.0 + 0.1 * jax.random.normal(keys[11], (D,), jnp.float32), 0.5, 1.5),
        "ffn_in": noise(keys[12], (D, FF), D ** -0.5, 0.1875, ((1, 4),)),
        "ffn_out": noise(keys[13], (FF, D), (FF // 4) ** -0.5, 0.1875, ((0, 4),)),
    }


epsilon = 1e-05
highest = lax.Precision.HIGHEST

@jax.custom_vjp
def low(v):
    return lax.optimization_barrier(v.astype(jnp.bfloat16)).astype(jnp.float32)

@jax.custom_vjp
def low_back(v):
    return v

def low_keep(v):
    return (low(v), None)

def low_pass(kept, grad):
    return (grad,)

def back_keep(v):
    return (v, None)

def back_low(kept, grad):
    return (low(grad),)
low.defvjp(low_keep, low_pass)
low_back.defvjp(back_keep, back_low)

def powers(decay, angle, count):
    steps = jnp.arange(count, dtype=jnp.float32)
    magnitude = jnp.exp(-decay[..., None] * steps)
    phase = angle[..., None] * steps
    return (magnitude * jnp.cos(phase), magnitude * jnp.sin(phase))

def weights_of(decay, real_part, imag_part):
    factor = jnp.sqrt(-jnp.expm1(-2.0 * decay))
    return (real_part * factor, imag_part * factor)

def layer_norm(values, gain):
    average = lax.optimization_barrier(jnp.mean(values, axis=-1, keepdims=True))
    spread = lax.optimization_barrier(jnp.mean(values * values, axis=-1, keepdims=True)) - average * average
    return (values - average) * lax.rsqrt(spread + epsilon) * gain

def matmul(left, right_side):
    return jnp.dot(left, right_side, preferred_element_type=jnp.float32, precision=highest)

def mix_stream(inputs, segment, decay, angle, real_part, imag_part, skip):
    total = inputs.shape[0]
    width = inputs.shape[1]
    block = min(128, LC)
    count = total // block
    coef_re, coef_im = weights_of(decay, real_part, imag_part)
    pow_re, pow_im = powers(decay, angle, block + 1)
    kernel = jnp.einsum('dn,dnk->dk', coef_re, pow_re[..., :block], precision=highest) - jnp.einsum('dn,dnk->dk', coef_im, pow_im[..., :block], precision=highest)
    index = jnp.arange(block, dtype=jnp.int32)
    lags = jnp.maximum(index[:, None] - index[None, :], 0)
    causal = index[:, None] >= index[None, :]
    toeplitz = kernel[:, lags]
    carry_re = coef_re[..., None] * pow_re[..., 1:] - coef_im[..., None] * pow_im[..., 1:]
    carry_im = coef_re[..., None] * pow_im[..., 1:] + coef_im[..., None] * pow_re[..., 1:]
    rev_re = pow_re[..., block - 1::-1]
    rev_im = pow_im[..., block - 1::-1]
    seg_blocks = segment.reshape(count, block)
    previous = jnp.concatenate([jnp.full((1,), -1, jnp.int32), seg_blocks[:-1, -1].astype(jnp.int32)])

    def step(state, items):
        state_re, state_im = state
        block_in, block_seg, block_prev = items
        same = ((block_seg[:, None] == block_seg[None, :]) & causal).astype(jnp.float32)
        local_out = jnp.einsum('dts,sd->td', toeplitz * same[None], block_in, precision=highest)
        keep_mask = (block_seg == block_prev).astype(jnp.float32)
        carried = jnp.einsum('dnt,dn->td', carry_re, state_re, precision=highest) - jnp.einsum('dnt,dn->td', carry_im, state_im, precision=highest)
        last_mask = (block_seg == block_seg[-1]).astype(jnp.float32)
        tail_in = block_in * last_mask[:, None]
        end_re = jnp.einsum('dns,sd->dn', rev_re, tail_in, precision=highest)
        end_im = jnp.einsum('dns,sd->dn', rev_im, tail_in, precision=highest)
        decay_re = keep_mask[-1] * pow_re[..., block]
        decay_im = keep_mask[-1] * pow_im[..., block]
        new_re = decay_re * state_re - decay_im * state_im + end_re
        new_im = decay_re * state_im + decay_im * state_re + end_im
        return ((new_re, new_im), local_out + keep_mask[:, None] * carried + skip * block_in)
    start_state = (jnp.zeros((width, decay.shape[1]), jnp.float32), jnp.zeros((width, decay.shape[1]), jnp.float32))
    unused, outputs = lax.scan(jax.checkpoint(step), start_state, (inputs.reshape(count, block, width), seg_blocks, previous))
    return outputs.reshape(total, width)

def stream_block(rows_in, segment, valid_mask, params):
    first_gain, decay, angle, real_part, imag_part, skip, glu_value, glu_gate, second_gain, ffn_in, ffn_out = params
    mixer_in = layer_norm(rows_in, first_gain) * valid_mask[:, None]
    mixer_out = mix_stream(mixer_in, segment, decay, angle, real_part, imag_part, skip)
    activated = low(jax.nn.gelu(mixer_out))
    value_pre = low_back(matmul(activated, glu_value))
    gate_pre = low_back(matmul(activated, glu_gate))
    resid = rows_in + value_pre * jax.nn.sigmoid(gate_pre)
    middle = low(layer_norm(resid, second_gain))
    hidden = low(jax.nn.gelu(low_back(matmul(middle, ffn_in))))
    return resid + low_back(matmul(hidden, ffn_out))

def reference(block_in, doc_lengths, out_grad, first_gain, decay_rate, turn_angle, out_real, out_imag, skip_gain, glu_value, glu_gate, second_gain, ffn_in, ffn_out):
    params = (first_gain, decay_rate, turn_angle, out_real, out_imag, skip_gain, glu_value.astype(jnp.float32), glu_gate.astype(jnp.float32), second_gain, ffn_in.astype(jnp.float32), ffn_out.astype(jnp.float32))
    positions = jnp.arange(SLEN, dtype=jnp.int32)

    def one_stream(totals, stream_items):
        rows_in, lengths_row, grad_row = stream_items
        doc_ends = jnp.cumsum(lengths_row).astype(jnp.int32)
        segment = lax.optimization_barrier(jnp.sum((doc_ends[None, :] <= positions[:, None]).astype(jnp.int32), axis=1)).astype(jnp.int32)
        valid_mask = (positions < doc_ends[-1]).astype(jnp.float32)

        def forward(values, weights):
            return stream_block(values, segment, valid_mask, weights)
        result, pullback = jax.vjp(forward, rows_in, params)
        row_grad, weight_grads = pullback(grad_row)
        totals = jax.tree.map(lambda summed, addend: summed + addend, totals, weight_grads)
        return (totals, (result, row_grad))
    start_totals = jax.tree.map(jnp.zeros_like, params)
    totals, outputs = lax.scan(one_stream, start_totals, (block_in, doc_lengths, out_grad))
    return (outputs[0], outputs[1], totals[0], totals[1], totals[2], totals[3], totals[4], totals[5], totals[6], totals[7], totals[8], totals[9], totals[10])
```

```python
import functools

import jax
import jax.numpy as jnp
from jax import lax
from jax.experimental import pallas as pl
from jax.experimental.pallas import tpu as pltpu
from jax.sharding import PartitionSpec as P

epsilon = 1e-05
LANES = 128
VM = pl.BlockSpec(memory_space=pltpu.VMEM)
GELU_A = 0.7978845608028654
GELU_B = 0.044715


def gelu_parts(x):
    inner = GELU_A * (x + GELU_B * (x * x * x))
    t = jnp.tanh(inner)
    half = 0.5 * (1.0 + t)
    slope = half + 0.5 * x * (1.0 - t * t) * (GELU_A * (1.0 + 3.0 * GELU_B * (x * x)))
    return x * half, slope


def row(ref, b, p):
    return jnp.broadcast_to(ref[b, pl.ds(p, 1), :], (8, LANES))


def tile(ref, lead, rows, cols):
    return ref[(*lead, rows, cols)].reshape(-1, 8, LANES)


def cmul(ar, ai, br, bi):
    return ar * br - ai * bi, ar * bi + ai * br


def edge_kernel(x_ref, mask_ref, lam_ref, out_ref, row_ref, *, reverse, states_at_once):
    streams, length, width = x_ref.shape
    states = lam_ref.shape[1]
    for c in range(width // LANES):
        cols = pl.ds(c * LANES, LANES)
        row_ref[...] = x_ref[:, :, cols] * mask_ref[...]
        for h in range(states // states_at_once):
            rows = pl.ds(h * states_at_once, states_at_once)
            l1r = tile(lam_ref, (0,), rows, cols)
            l1i = tile(lam_ref, (1,), rows, cols)
            l1i = -l1i if reverse else l1i
            l2r, l2i = cmul(l1r, l1i, l1r, l1i)
            l3r, l3i = cmul(l2r, l2i, l1r, l1i)
            l4r, l4i = cmul(l2r, l2i, l2r, l2i)

            def step(i, carry):
                new = []
                for b in range(streams):
                    sr, si = carry[2 * b], carry[2 * b + 1]
                    base = length - 4 - 4 * i if reverse else 4 * i
                    u = []
                    for j in range(4):
                        u.append(row(row_ref, b, base + (3 - j if reverse else j)))
                    nr = (l4r * sr - l4i * si) + (l3r * u[0] + l2r * u[1]) + (l1r * u[2] + u[3])
                    ni = (l4r * si + l4i * sr) + (l3i * u[0] + l2i * u[1]) + l1i * u[2]
                    new += [nr, ni]
                return tuple(new)

            zero = jnp.zeros((states_at_once // 8, 8, LANES), jnp.float32)
            final = lax.fori_loop(0, length // 4, step, (zero,) * (2 * streams))
            for b in range(streams):
                out_ref[b, 0, rows, cols] = final[2 * b].reshape(-1, LANES)
                out_ref[b, 1, rows, cols] = final[2 * b + 1].reshape(-1, LANES)


def edge_states(values, mask, lam, reverse):
    streams, length, width = values.shape
    states = lam.shape[1]
    return pl.pallas_call(
        functools.partial(edge_kernel, reverse=reverse, states_at_once=min(32, states)),
        out_shape=jax.ShapeDtypeStruct((streams, 2, states, width), jnp.float32),
        in_specs=[VM] * 3,
        out_specs=VM,
        scratch_shapes=[pltpu.VMEM((streams, length, LANES), jnp.float32)],
        compiler_params=pltpu.CompilerParams(vmem_limit_bytes=32 * 1024 * 1024),
    )(values, mask, lam)


def forward_kernel(u_ref, keep_ref, init_ref, lam_ref, coef_ref, skip_ref, y_ref, act_ref, row_ref, part_ref):
    streams, length, width = u_ref.shape
    states = lam_ref.shape[1]
    for c in range(width // LANES):
        cols = pl.ds(c * LANES, LANES)
        every = pl.ds(0, states)
        lr, li = tile(lam_ref, (0,), every, cols), tile(lam_ref, (1,), every, cols)
        cr, ci = tile(coef_ref, (0,), every, cols), tile(coef_ref, (1,), every, cols)
        row_ref[...] = u_ref[:, :, cols]
        for b in range(streams):

            def step(p, carry):
                sr, si = carry
                u = row(row_ref, b, p)
                m = row(keep_ref, b, p)
                sr = sr * m
                si = si * m
                nr = (lr * sr - li * si) + u
                ni = lr * si + li * sr
                acc = (cr * nr - ci * ni).sum(0)
                part_ref[pl.ds(pl.multiple_of(p * 8, 8), 8), :] = acc
                return nr, ni

            start = (tile(init_ref, (b, 0), every, cols), tile(init_ref, (b, 1), every, cols))
            lax.fori_loop(0, length, step, start, unroll=2)
            total = part_ref[pl.ds(0, length, stride=8), :]
            for j in range(1, 8):
                total = total + part_ref[pl.ds(j, length, stride=8), :]
            y = total + skip_ref[:, cols] * u_ref[b, :, cols]
            y_ref[b, :, cols] = y
            act_ref[b, :, cols] = gelu_parts(y)[0].astype(jnp.bfloat16)


def forward_scan(inputs, keep, init, lam, coef, skip):
    streams, length, width = inputs.shape
    return pl.pallas_call(
        forward_kernel,
        out_shape=(
            jax.ShapeDtypeStruct(inputs.shape, jnp.float32),
            jax.ShapeDtypeStruct(inputs.shape, jnp.bfloat16),
        ),
        in_specs=[VM] * 6,
        out_specs=(VM, VM),
        scratch_shapes=[
            pltpu.VMEM((streams, length, LANES), jnp.float32),
            pltpu.VMEM((length * 8, LANES), jnp.float32),
        ],
        compiler_params=pltpu.CompilerParams(vmem_limit_bytes=32 * 1024 * 1024),
    )(inputs, keep, init, lam, coef, skip[None])


def backward_kernel(
    u_ref, g_ref, keep_ref, init_ref, adj_ref, lam_ref, coef_ref, skip_ref,
    du_ref, glam_ref, gco_ref, u_row, g_row, s_ref, part_ref, *, group,
):
    streams, length, width = u_ref.shape
    states = lam_ref.shape[1]
    zero = jnp.zeros((group // 8, 8, LANES), jnp.float32)
    for c in range(width // LANES):
        cols = pl.ds(c * LANES, LANES)
        u_row[...] = u_ref[:, :, cols]
        g_row[...] = g_ref[:, :, cols]
        for h in range(states // group):
            rows = pl.ds(h * group, group)
            lr, li = tile(lam_ref, (0,), rows, cols), tile(lam_ref, (1,), rows, cols)
            cr, ci = tile(coef_ref, (0,), rows, cols), tile(coef_ref, (1,), rows, cols)

            def again(p, carry):
                new = []
                for b in range(streams):
                    sr, si = carry[2 * b], carry[2 * b + 1]
                    u = row(u_row, b, p)
                    m = row(keep_ref, b, p)
                    sr = sr * m
                    si = si * m
                    nr = (lr * sr - li * si) + u
                    ni = lr * si + li * sr
                    s_ref[p + 1, b, 0] = nr
                    s_ref[p + 1, b, 1] = ni
                    new += [nr, ni]
                return tuple(new)

            first = []
            for b in range(streams):
                first += [tile(init_ref, (b, 0), rows, cols), tile(init_ref, (b, 1), rows, cols)]
                s_ref[0, b, 0] = first[-2]
                s_ref[0, b, 1] = first[-1]
            lax.fori_loop(0, length, again, tuple(first), unroll=2)

            def back(i, carry):
                glr, gli, gcr, gci = carry[:4]
                adj = carry[4:]
                p = length - 1 - i
                new = []
                for b in range(streams):
                    ar, ai = adj[2 * b], adj[2 * b + 1]
                    g = row(g_row, b, p)
                    m = row(keep_ref, b, p)
                    nr = (lr * ar + li * ai) + cr * g
                    ni = (lr * ai - li * ar) - ci * g
                    acc = nr.sum(0)
                    at = pl.ds(pl.multiple_of((b * length + p) * 8, 8), 8)
                    if h == 0:
                        part_ref[at, :] = acc
                    else:
                        part_ref[at, :] += acc
                    gcr = gcr + g * s_ref[p + 1, b, 0]
                    gci = gci - g * s_ref[p + 1, b, 1]
                    nr = nr * m
                    ni = ni * m
                    sr, si = s_ref[p, b, 0], s_ref[p, b, 1]
                    glr = glr + (nr * sr + ni * si)
                    gli = gli + (ni * sr - nr * si)
                    new += [nr, ni]
                return (glr, gli, gcr, gci, *new)

            start = []
            for b in range(streams):
                start += [tile(adj_ref, (b, 0), rows, cols), tile(adj_ref, (b, 1), rows, cols)]
            out = lax.fori_loop(0, length, back, (zero, zero, zero, zero, *start))
            glam_ref[0, rows, cols] = out[0].reshape(-1, LANES)
            glam_ref[1, rows, cols] = out[1].reshape(-1, LANES)
            gco_ref[0, rows, cols] = out[2].reshape(-1, LANES)
            gco_ref[1, rows, cols] = out[3].reshape(-1, LANES)
        for b in range(streams):
            total = part_ref[pl.ds(b * length * 8, length, stride=8), :]
            for j in range(1, 8):
                total = total + part_ref[pl.ds(b * length * 8 + j, length, stride=8), :]
            du_ref[b, :, cols] = total + skip_ref[:, cols] * g_ref[b, :, cols]


def backward_scan(inputs, grads, keep, init, adj, lam, coef, skip):
    streams, length, width = inputs.shape
    states = lam.shape[1]
    group = min(32, states)
    return pl.pallas_call(
        functools.partial(backward_kernel, group=group),
        out_shape=(
            jax.ShapeDtypeStruct(inputs.shape, jnp.float32),
            jax.ShapeDtypeStruct((2, states, width), jnp.float32),
            jax.ShapeDtypeStruct((2, states, width), jnp.float32),
        ),
        in_specs=[VM] * 8,
        out_specs=(VM, VM, VM),
        scratch_shapes=[
            pltpu.VMEM((streams, length, LANES), jnp.float32),
            pltpu.VMEM((streams, length, LANES), jnp.float32),
            pltpu.VMEM((length + 1, streams, 2, group // 8, 8, LANES), jnp.float32),
            pltpu.VMEM((streams * length * 8, LANES), jnp.float32),
        ],
        compiler_params=pltpu.CompilerParams(vmem_limit_bytes=40 * 1024 * 1024),
    )(inputs, grads, keep, init, adj, lam, coef, skip[None])


def carry_over(parts, flags, step, reverse):
    count = lax.axis_size("seq")
    place = lax.axis_index("seq")
    gathered = lax.all_gather(parts, "seq")
    ahead = count - 1 - place if reverse else place

    def one(turn, state):
        source = count - 1 - turn if reverse else turn
        part = lax.dynamic_index_in_dim(gathered, source, 0, False)
        flag = lax.dynamic_index_in_dim(flags, source, 0, False)[:, None, None]
        real = flag * (step[0] * state[:, 0] - step[1] * state[:, 1])
        imag = flag * (step[0] * state[:, 1] + step[1] * state[:, 0])
        return part + jnp.stack([real, imag], 1)

    return lax.fori_loop(0, ahead, one, jnp.zeros_like(parts))


def token_sums(*sums):
    return lax.psum(sums, "chan")


def per_device(
    block_in, doc_lengths, out_grad, first_gain, decay_rate, turn_angle, out_real, out_imag,
    skip_gain, glu_value, glu_gate, second_gain, ffn_in, ffn_out,
):
    streams, length, width = block_in.shape
    tokens = streams * length
    full = width * lax.axis_size("chan")
    blocks = lax.axis_size("seq")
    place = lax.axis_index("seq")

    doc_ends = jnp.cumsum(doc_lengths, axis=1)

    def segment_at(positions):
        return jnp.sum((doc_ends[:, None, :] <= positions[None, :, None]).astype(jnp.int32), axis=2)

    positions = place * length + jnp.arange(length, dtype=jnp.int32)
    segment = segment_at(positions)
    before_all = segment_at(positions - 1)
    before = before_all[:, :1]
    keep = (segment == before_all).astype(jnp.float32)
    first_mask = (segment == before).astype(jnp.float32)
    last_mask = (segment == segment[:, -1:]).astype(jnp.float32)
    valid = (positions[None, :] < doc_ends[:, -1:]).astype(jnp.float32)
    starts = jnp.arange(blocks, dtype=jnp.int32) * length
    flags = (segment_at(starts - 1) == segment_at(starts + length - 1)).astype(jnp.float32).T

    def wide(mask):
        return jnp.broadcast_to(mask[:, :, None], (streams, length, LANES))

    decay, angle = decay_rate.T, turn_angle.T
    real, imag = out_real.T, out_imag.T
    magnitude = jnp.exp(-decay)
    lam = jnp.stack([magnitude * jnp.cos(angle), magnitude * jnp.sin(angle)])
    block_mag = jnp.exp(-decay * length)
    block_step = (block_mag * jnp.cos(angle * length), block_mag * jnp.sin(angle * length))
    factor = jnp.sqrt(-jnp.expm1(-2.0 * decay))
    coef = jnp.stack([real * factor, imag * factor])

    rows = block_in.reshape(tokens, width)
    sums = token_sums(jnp.sum(rows, -1), jnp.sum(rows * rows, -1))
    average1 = sums[0] / full
    scaler1 = lax.rsqrt(sums[1] / full - average1 * average1 + epsilon)[:, None]
    normed1 = (rows - average1[:, None]) * scaler1
    valid_rows = valid.reshape(tokens, 1)
    mixer_in = (normed1 * first_gain * valid_rows).reshape(streams, length, width)

    ends = edge_states(mixer_in, wide(last_mask), lam, False)
    init = carry_over(ends, flags, block_step, False)
    mixer_out, act = forward_scan(mixer_in, wide(keep), init, lam, coef, skip_gain)
    act_full = lax.all_gather(act.reshape(tokens, width), "chan", axis=1, tiled=True)

    value_pre = jnp.dot(act_full, glu_value, preferred_element_type=jnp.float32)
    gate_pre = jnp.dot(act_full, glu_gate, preferred_element_type=jnp.float32)
    gate = jax.nn.sigmoid(gate_pre)
    resid = rows + value_pre * gate

    sums = token_sums(jnp.sum(resid, -1), jnp.sum(resid * resid, -1))
    average2 = sums[0] / full
    scaler2 = lax.rsqrt(sums[1] / full - average2 * average2 + epsilon)[:, None]
    normed2 = (resid - average2[:, None]) * scaler2
    mid = (normed2 * second_gain).astype(jnp.bfloat16)
    grad_rows = out_grad.reshape(tokens, width)
    grad_low = grad_rows.astype(jnp.bfloat16)
    mid_full = lax.all_gather(mid, "chan", axis=1, tiled=True)
    grad_full = lax.all_gather(grad_low, "chan", axis=1, tiled=True)

    hidden_pre = jnp.dot(mid_full, ffn_in, preferred_element_type=jnp.float32)
    hidden, slope = gelu_parts(hidden_pre)
    hidden = hidden.astype(jnp.bfloat16)
    part_out = jnp.dot(hidden, ffn_out, preferred_element_type=jnp.float32)
    hidden_grad = jnp.dot(grad_full, ffn_out.T, preferred_element_type=jnp.float32)
    pre_grad = (hidden_grad * slope).astype(jnp.bfloat16)
    part_grad = jnp.dot(pre_grad, ffn_in.T, preferred_element_type=jnp.float32)
    ffn_out_grad = jnp.dot(hidden.T, grad_full, preferred_element_type=jnp.float32)
    ffn_in_grad = jnp.dot(mid_full.T, pre_grad, preferred_element_type=jnp.float32)
    ffn_in_grad, ffn_out_grad = lax.psum(
        (ffn_in_grad.astype(jnp.bfloat16), ffn_out_grad.astype(jnp.bfloat16)), "seq"
    )
    mid_grad = lax.psum_scatter(part_grad, "chan", scatter_dimension=1, tiled=True)
    ffn_result = lax.psum_scatter(part_out, "chan", scatter_dimension=1, tiled=True)
    block_out = (resid + ffn_result).reshape(streams, length, width)

    second_gain_grad = jnp.sum(mid_grad * normed2, axis=0)
    scaled = mid_grad * second_gain
    sums = token_sums(jnp.sum(scaled, -1), jnp.sum(scaled * normed2, -1))
    resid_grad = grad_rows + scaler2 * (
        scaled - sums[0][:, None] / full - normed2 * (sums[1][:, None] / full)
    )

    value_grad = (resid_grad * gate).astype(jnp.bfloat16)
    gate_grad = (resid_grad * value_pre * gate * (1.0 - gate)).astype(jnp.bfloat16)
    glu_value_grad = jnp.dot(act_full.T, value_grad, preferred_element_type=jnp.float32)
    glu_gate_grad = jnp.dot(act_full.T, gate_grad, preferred_element_type=jnp.float32)
    act_part = jnp.dot(value_grad, glu_value.T, preferred_element_type=jnp.float32) + jnp.dot(
        gate_grad, glu_gate.T, preferred_element_type=jnp.float32
    )
    act_grad = lax.psum_scatter(act_part, "chan", scatter_dimension=1, tiled=True)
    mixer_grad = act_grad.reshape(streams, length, width) * gelu_parts(mixer_out)[1]

    starts_sum = edge_states(mixer_grad, wide(first_mask), lam, True)
    starts_part = jnp.stack(
        [
            coef[0] * starts_sum[:, 0] + coef[1] * starts_sum[:, 1],
            coef[0] * starts_sum[:, 1] - coef[1] * starts_sum[:, 0],
        ],
        1,
    )
    adj = carry_over(starts_part, flags, (block_step[0], -block_step[1]), True)
    mixer_in_grad, glam, gco = backward_scan(
        mixer_in, mixer_grad, wide(keep), init, adj, lam, coef, skip_gain
    )
    skip_gain_grad = jnp.sum(mixer_grad * mixer_in, axis=(0, 1))
    ratio = jnp.exp(-2.0 * decay) / factor
    decay_grad = (gco[0] * real + gco[1] * imag) * ratio - (glam[0] * lam[0] + glam[1] * lam[1])
    angle_grad = glam[1] * lam[0] - glam[0] * lam[1]
    table_grads = jnp.stack([decay_grad, angle_grad, factor * gco[0], factor * gco[1]])

    unit_grad = mixer_in_grad.reshape(tokens, width) * valid_rows
    first_gain_grad = jnp.sum(unit_grad * normed1, axis=0)
    scaled = unit_grad * first_gain
    sums = token_sums(jnp.sum(scaled, -1), jnp.sum(scaled * normed1, -1))
    in_grad = resid_grad + scaler1 * (
        scaled - sums[0][:, None] / full - normed1 * (sums[1][:, None] / full)
    )

    gains, table_grads, glu_value_grad, glu_gate_grad = lax.psum(
        (
            jnp.stack([first_gain_grad, skip_gain_grad, second_gain_grad]),
            table_grads,
            glu_value_grad,
            glu_gate_grad,
        ),
        "seq",
    )
    return (
        block_out,
        in_grad.reshape(streams, length, width),
        gains[0],
        table_grads[0].T,
        table_grads[1].T,
        table_grads[2].T,
        table_grads[3].T,
        gains[1],
        glu_value_grad,
        glu_gate_grad,
        gains[2],
        ffn_in_grad.astype(jnp.float32),
        ffn_out_grad.astype(jnp.float32),
    )


def solution(mesh):
    act = P(None, "seq", "chan")
    vec, mat = P("chan"), P("chan", None)
    col = P(None, "chan")
    return jax.shard_map(
        per_device,
        mesh=mesh,
        in_specs=(act, P(), act, vec, mat, mat, mat, mat, vec, col, col, vec, col, mat),
        out_specs=(act, act, vec, mat, mat, mat, mat, vec, col, col, vec, col, mat),
        check_vma=False,
    )
```

```python
import functools

import jax
import jax.numpy as jnp
from jax import lax
from jax.experimental import pallas as pl
from jax.experimental.pallas import tpu as pltpu
from jax.sharding import PartitionSpec as P

epsilon = 1e-05
LANES = 128
MESH = pl.DeviceIdType.MESH
VM = pl.BlockSpec(memory_space=pltpu.VMEM)
ANY = pl.BlockSpec(memory_space=pl.ANY)
GELU_A = 0.7978845608028654
GELU_B = 0.044715
NN = (((1,), (0,)), ((), ()))
NT = (((1,), (1,)), ((), ()))
SLOTS = 15
f32, bf16 = jnp.float32, jnp.bfloat16


def gelu_parts(x):
    inner = GELU_A * (x + GELU_B * (x * x * x))
    t = jnp.tanh(inner)
    half = 0.5 * (1.0 + t)
    slope = half + 0.5 * x * (1.0 - t * t) * (GELU_A * (1.0 + 3.0 * GELU_B * (x * x)))
    return x * half, slope


def dot(a, b, dims=NN):
    return lax.dot_general(a, b, dims, preferred_element_type=f32)


def cmul(ar, ai, br, bi):
    return ar * br - ai * bi, ar * bi + ai * br


def power(re, im, count):
    out = None
    while count:
        if count & 1:
            out = (re, im) if out is None else cmul(*out, re, im)
        re, im = cmul(re, im, re, im)
        count >>= 1
    return out


def row(ref, b, p):
    return jnp.broadcast_to(ref[b, pl.ds(p, 1), :], (8, LANES))


def tile(ref, lead, rows, cols):
    return ref[(*lead, rows, cols)].reshape(-1, 8, LANES)


class Ring:
    def __init__(self, sign, left, right, out, cols, first, buf, send, recv, count, place, to):
        self.left, self.right, self.out, self.cols = left, right, out, cols
        self.first, self.buf, self.send, self.recv = first, buf, send, recv
        self.count, self.to = count, to
        self.place = place if sign > 0 else lax.rem(count - place, count)
        self.rows = left.shape[0] // count

    def chunk(self, t):
        c = lax.rem(self.place - t + 2 * self.count, self.count)
        return pl.ds(pl.multiple_of(c * self.rows, self.rows), self.rows)

    def own(self, t):
        return dot(self.left[self.chunk(t), :], self.right[:, self.cols])

    def copy(self, src, dst, t):
        return pltpu.make_async_remote_copy(
            src_ref=src, dst_ref=dst, send_sem=self.send.at[t], recv_sem=self.recv.at[t],
            device_id=self.to, device_id_type=MESH,
        )

    def arrived(self, t):
        self.copy(self.first, self.first, t).wait_recv()

    def head(self, t):
        self.first[...] = self.own(t).astype(bf16)
        self.copy(self.first, self.buf.at[t], t).start()

    def reduce(self, t):
        total = self.own(t)
        self.arrived(t - 1)
        self.buf[t - 1] = (total + self.buf[t - 1].astype(f32)).astype(bf16)
        self.copy(self.buf.at[t - 1], self.buf.at[t], t).start()

    def turn(self, t):
        total = self.own(t)
        self.arrived(t - 1)
        self.out[self.chunk(t), self.cols] = (total + self.buf[t - 1].astype(f32)).astype(bf16)
        self.spread(t)

    def spread(self, t):
        part = self.out.at[self.chunk(t), self.cols]
        self.copy(part, part, t).start()

    def gather(self, t):
        self.arrived(t - 1)
        self.spread(t)

    def run(self, start, stop):
        n = self.count

        def many(lo, hi, body):
            lo, hi = max(start, lo), min(stop, hi)
            if hi - lo == 1:
                body(lo)
            elif hi > lo:
                lax.fori_loop(lo, hi, lambda t, none: body(t), None)

        many(0, 1, self.head)
        many(1, n - 1, self.reduce)
        many(n - 1, n, self.turn)
        many(n, 2 * n - 2, self.gather)
        many(2 * n - 2, 2 * n - 1, lambda t: self.arrived(t - 1))

    def slot(self, i):
        total = 2 * self.count - 1
        self.run(i * total // SLOTS, (i + 1) * total // SLOTS)

    def finish(self):
        def sent(t, none):
            self.copy(self.first, self.first, t).wait_send()

        lax.fori_loop(0, 2 * self.count - 2, sent, None)


def block_kernel(
    sizes,
    docs, x_ref, og_ref, gain1, dec_ref, ang_ref, real_ref, imag_ref, skip_ref, gluv_hbm, glug_hbm, gain2, win_hbm, wout_hbm,
    block_out, in_grad, tables_out, gains_out, gin_out, gout_out, gv_out, gg_out,
    gluv, glug, win, wout,
    keep, first_mask, last_mask, valid,
    param, lam, coef, step_l, factor,
    normed1, u_ref, y_ref, edge_sum, init, adj,
    act_full, val, gate, resid, normed2, grad_full, mid_full, hidden_grad, hidden, pre,
    act_t, mid_t, hidden_t, part_own, mid_grad, out_own, resid_grad, value_grad, gate_grad, act_own, mixer_grad, du,
    row_a, row_b, part, states,
    stat_send, stat_recv, rs_send, rs_recv,
    pair_send, pair_recv, line_send, line_recv, back_send, back_low, back_recv,
    table, table_recv, table_line, table_back,
    first_in, buf_in, first_out, buf_out, first_v, buf_v, first_g, buf_g,
    load_sem, chan_send, chan_recv, seq_send, seq_recv, ring_send, ring_recv,
):
    n_seq, n_chan = sizes
    pairs = n_seq // 2
    streams, length, width = x_ref.shape
    n_states = lam.shape[1]
    tokens = streams * length
    full = width * n_chan
    units = win.shape[1]
    group = states.shape[3] * 8
    s, c = lax.axis_index("seq"), lax.axis_index("chan")
    odd = lax.rem(s, 2)
    level = lax.div(s, 2)
    partner = (s + 1 - 2 * odd, c)
    every = pl.ds(0, n_states)

    def chan_peer(j):
        return lax.rem(c + j, n_chan)

    def chan_block(k, size):
        return pl.ds(pl.multiple_of(k * size, size), size)

    own_cols = chan_block(c, width)

    barrier = pltpu.get_barrier_semaphore()
    for j in range(1, n_chan):
        pl.semaphore_signal(barrier, inc=1, device_id=(s, chan_peer(j)), device_id_type=MESH)
    pl.semaphore_signal(barrier, inc=1, device_id=partner, device_id_type=MESH)
    for d in range(1, pairs):
        other = 2 * lax.rem(level + d, pairs) + odd
        pl.semaphore_signal(barrier, inc=1, device_id=(other, c), device_id_type=MESH)

    loads = [
        pltpu.make_async_copy(src, dst, load_sem.at[i])
        for i, (src, dst) in enumerate(
            ((wout_hbm, wout), (gluv_hbm, gluv), (glug_hbm, glug), (win_hbm, win))
        )
    ]
    for load in loads:
        load.start()

    sent = []

    def chan_copy(src, dst, phase, j):
        return pltpu.make_async_remote_copy(
            src_ref=src, dst_ref=dst, send_sem=chan_send.at[phase, j - 1], recv_sem=chan_recv.at[phase, j - 1],
            device_id=(s, chan_peer(j)), device_id_type=MESH,
        )

    def chan_all(pick, phase):
        copies = []
        for j in range(1, n_chan):
            copy = chan_copy(*pick(j), phase, j)
            copy.start()
            copies.append(copy)
        sent.extend(copies)
        return copies

    def landed(copies):
        for copy in copies:
            copy.wait_recv()

    lane = lax.broadcasted_iota(jnp.int32, (tokens, LANES), 1)

    def stats_start(first, second, k, phase):
        packed = jnp.where(lane == 0, first, jnp.where(lane == 1, second, 0.0))
        stat_send[k] = packed.T[:8]
        return chan_all(lambda j: (stat_send.at[k], stat_recv.at[k, j - 1]), phase)

    def stats_end(copies, k):
        landed(copies)
        total = stat_send[k]
        for j in range(1, n_chan):
            total = total + stat_recv[k, j - 1]
        total = jnp.concatenate([total, jnp.zeros((LANES - 8, tokens), f32)], axis=0).T
        return total[:, 0:1] / full, total[:, 1:2] / full

    rows_in = x_ref[...].reshape(tokens, width)
    grad_full[:, own_cols] = og_ref[...].reshape(tokens, width).astype(bf16)
    sum1 = jnp.sum(rows_in, axis=1, keepdims=True)
    square1 = jnp.sum(rows_in * rows_in, axis=1, keepdims=True)
    pl.semaphore_wait(barrier, n_chan + pairs - 1)
    stat_copies = stats_start(sum1, square1, 0, 0)
    grad_copies = chan_all(lambda j: (grad_full.at[:, own_cols], grad_full.at[:, own_cols]), 1)

    start = s * length
    ends = []
    for b in range(streams):
        total, stream = 0, []
        for k in range(docs.shape[1]):
            total = total + docs[b, k]
            stream.append(total)
        ends.append(stream)

    def passed(b, at):
        count = jnp.int32(0)
        for end in ends[b]:
            count = count + jnp.where(end <= at, 1, 0)
        return count

    def kept(block, b):
        return jnp.where(
            passed(b, block * length - 1) == passed(b, block * length + length - 1), 1.0, 0.0
        )

    position = lax.broadcasted_iota(jnp.int32, (length, LANES), 0) + start
    for b in range(streams):
        here = jnp.zeros((length, LANES), jnp.int32)
        prior = jnp.zeros((length, LANES), jnp.int32)
        for end in ends[b]:
            here = here + jnp.where(position >= end, 1, 0)
            prior = prior + jnp.where(position > end, 1, 0)
        keep[b] = jnp.where(here == prior, 1.0, 0.0)
        first_mask[b] = jnp.where(here == passed(b, start - 1), 1.0, 0.0)
        last_mask[b] = jnp.where(here == passed(b, start + length - 1), 1.0, 0.0)
        valid[b] = jnp.where(position < ends[b][-1], 1.0, 0.0)

    param[0:2] = jnp.concatenate([dec_ref[...], ang_ref[...]], axis=1).T.reshape(2, n_states, width)
    param[2:4] = jnp.concatenate([real_ref[...], imag_ref[...]], axis=1).T.reshape(2, n_states, width)
    decay, angle = param[0], param[1]
    magnitude = jnp.exp(-decay)
    a2 = angle * angle
    sine, cosine = jnp.ones_like(a2), jnp.ones_like(a2)
    for k in (13, 11, 9, 7, 5, 3):
        sine = 1.0 - sine * a2 * (1.0 / (k * (k - 1)))
    for k in (14, 12, 10, 8, 6, 4, 2):
        cosine = 1.0 - cosine * a2 * (1.0 / (k * (k - 1)))
    lam[0] = magnitude * cosine
    lam[1] = magnitude * (sine * angle)
    twice = 2.0 * decay
    series = jnp.ones_like(twice)
    for k in (9, 8, 7, 6, 5, 4, 3, 2):
        series = 1.0 - series * twice * (1.0 / k)
    factor[...] = jnp.sqrt(twice * series)
    coef[0] = param[2] * factor[...]
    coef[1] = param[3] * factor[...]
    step_l[0], step_l[1] = power(lam[0], lam[1], length)

    average, square = stats_end(stat_copies, 0)
    scaler1 = lax.rsqrt(square - average * average + epsilon)
    normed1[...] = (rows_in - average) * scaler1
    for b in range(streams):
        rows = slice(b * length, (b + 1) * length)
        for k in range(width // LANES):
            cols = slice(k * LANES, (k + 1) * LANES)
            u_ref[b, :, cols] = normed1[rows, cols] * gain1[:, cols] * valid[b]

    def edges(values, mask, reverse):
        for k in range(width // LANES):
            cols = pl.ds(k * LANES, LANES)
            row_a[...] = values[:, :, cols] * mask[...]
            for h in range(n_states // group):
                rows = pl.ds(h * group, group)
                l1r, l1i = tile(lam, (0,), rows, cols), tile(lam, (1,), rows, cols)
                l1i = -l1i if reverse else l1i
                l2r, l2i = cmul(l1r, l1i, l1r, l1i)
                l3r, l3i = cmul(l2r, l2i, l1r, l1i)
                l4r, l4i = cmul(l2r, l2i, l2r, l2i)

                def move(i, carry):
                    new = []
                    for b in range(streams):
                        sr, si = carry[2 * b], carry[2 * b + 1]
                        base = length - 4 - 4 * i if reverse else 4 * i
                        u = [row(row_a, b, base + (3 - j if reverse else j)) for j in range(4)]
                        nr = (l4r * sr - l4i * si) + (l3r * u[0] + l2r * u[1]) + (l1r * u[2] + u[3])
                        ni = (l4r * si + l4i * sr) + (l3i * u[0] + l2i * u[1]) + l1i * u[2]
                        new += [nr, ni]
                    return tuple(new)

                zero = jnp.zeros((group // 8, 8, LANES), f32)
                final = lax.fori_loop(0, length // 4, move, (zero,) * (2 * streams))
                cr, ci = tile(coef, (0,), rows, cols), tile(coef, (1,), rows, cols)
                for b in range(streams):
                    fr, fi = final[2 * b], final[2 * b + 1]
                    if reverse:
                        fr, fi = cmul(cr, -ci, fr, fi)
                    edge_sum[b, 0, rows, cols] = fr.reshape(-1, LANES)
                    edge_sum[b, 1, rows, cols] = fi.reshape(-1, LANES)

    def carry_over(target, which, reverse, fill):
        def seq_copy(src, dst, k, to):
            return pltpu.make_async_remote_copy(
                src_ref=src, dst_ref=dst, send_sem=seq_send.at[which, k], recv_sem=seq_recv.at[which, k],
                device_id=to, device_id_type=MESH,
            )

        sr = step_l[0]
        si = -step_l[1] if reverse else step_l[1]
        dr, di = cmul(sr, si, sr, si)
        leads = odd == (1 if reverse else 0)
        pair_send[which] = edge_sum[...].astype(bf16)
        across = seq_copy(pair_send.at[which], pair_recv.at[which], 0, partner)
        across.start()
        fill(0)
        across.wait_recv()
        lead = 2 * level + (1 if reverse else 0)
        trail = 2 * level + (0 if reverse else 1)

        def advance(flag, vr, vi, ur, ui):
            r, i = cmul(ur, ui, vr, vi)
            return r * flag, i * flag

        mine_r, mine_i = edge_sum[odd, 0], edge_sum[odd, 1]
        other_r, other_i = pair_recv[which, odd, 0].astype(f32), pair_recv[which, odd, 1].astype(f32)
        flag = jnp.where(odd == 1, kept(trail, 1), kept(trail, 0))
        lr, li = jnp.where(leads, mine_r, other_r), jnp.where(leads, mine_i, other_i)
        tr, ti = jnp.where(leads, other_r, mine_r), jnp.where(leads, other_i, mine_i)
        ar, ai = advance(flag, lr, li, sr, si)
        line_send[which, 0] = (ar + tr).astype(bf16)
        line_send[which, 1] = (ai + ti).astype(bf16)
        for d in range(1, pairs):
            to = level - d if reverse else level + d

            @pl.when(to >= 0 if reverse else to < pairs)
            def _(d=d, to=to):
                seq_copy(line_send.at[which], line_recv.at[which, d - 1], 1 + d, (2 * to + odd, c)).start()

        fill(1)
        back_send[which] = jnp.zeros(back_send.shape[1:], f32)
        for d in range(pairs - 1, 0, -1):
            source = level + d if reverse else level - d

            @pl.when(source < pairs if reverse else source >= 0)
            def _(d=d, source=source):
                seq_copy(line_send.at[which], line_recv.at[which, d - 1], 1 + d, partner).wait_recv()
                both = [kept(2 * source, b) * kept(2 * source + 1, b) for b in (0, 1)]
                flag = jnp.where(odd == 1, both[1], both[0])
                vr, vi = advance(flag, back_send[which, 0], back_send[which, 1], dr, di)
                back_send[which, 0] = vr + line_recv[which, d - 1, 0].astype(f32)
                back_send[which, 1] = vi + line_recv[which, d - 1, 1].astype(f32)

        back_low[which] = back_send[which].astype(bf16)
        home = seq_copy(back_low.at[which], back_recv.at[which], 1, partner)
        home.start()
        fill(2)
        home.wait_recv()
        for b in range(streams):
            flag = kept(lead, b)
            for k in range(2):
                target[b, k] = jnp.where(odd == b, back_send[which, k], back_recv[which, k].astype(f32))
            vr, vi = advance(flag, target[b, 0], target[b, 1], sr, si)
            vr = vr + pair_recv[which, b, 0].astype(f32)
            vi = vi + pair_recv[which, b, 1].astype(f32)
            target[b, 0] = jnp.where(leads, target[b, 0], vr)
            target[b, 1] = jnp.where(leads, target[b, 1], vi)

        def done():
            across.wait_send()
            home.wait_send()
            for d in range(1, pairs):
                to = level - d if reverse else level + d

                @pl.when(to >= 0 if reverse else to < pairs)
                def _(d=d):
                    seq_copy(line_send.at[which], line_recv.at[which, d - 1], 1 + d, partner).wait_send()

        return done

    place = jnp.where(odd == 0, level, n_seq - 1 - level)

    def ring_device(q):
        return (jnp.where(q < pairs, 2 * q, 2 * (n_seq - 1 - q) + 1), c)

    after = ring_device(lax.rem(place + 1, n_seq))
    ahead = ring_device(lax.rem(place + n_seq - 1, n_seq))
    half = units // 2
    rings = []
    for sign, left, right, out, first, buf in (
        (1, mid_t, pre, gin_out, first_in, buf_in),
        (-1, hidden_t, grad_full, gout_out, first_out, buf_out),
    ):
        for k in range(2):
            size = right.shape[1] // 2
            i = len(rings)
            rings.append(
                Ring(sign, left, right, out, pl.ds(k * size, size), first.at[k], buf.at[k], ring_send.at[i], ring_recv.at[i],
                     n_seq, place, after if sign > 0 else ahead)
            )
    rings = [rings[0], rings[2], rings[1], rings[3]]
    glu_rings = [
        Ring(1, act_t, value_grad, gv_out, pl.ds(0, width), first_v, buf_v, ring_send.at[4], ring_recv.at[4], n_seq, place, after),
        Ring(-1, act_t, gate_grad, gg_out, pl.ds(0, width), first_g, buf_g, ring_send.at[5], ring_recv.at[5], n_seq, place, ahead),
    ]
    at = [0, 0]

    def move_rings(count=1):
        for _ in range(count):
            if at[0] < SLOTS:
                for ring in rings:
                    ring.slot(at[0])
                at[0] += 1

    def move_glu(count=1):
        for _ in range(count):
            if at[1] < SLOTS:
                for ring in glu_rings:
                    ring.slot(at[1])
                at[1] += 1

    edges(u_ref, last_mask, False)
    unit_block = min(units, 256)

    def hidden_grad_part(i):
        cols = pl.ds(i * unit_block, unit_block)
        hidden_grad[:, cols] = dot(grad_full[...], wout[cols, :], NT)

    def fill_forward(i):
        if i == 0:
            loads[0].wait()
            landed(grad_copies)
        count = units // unit_block
        for k in range(i * count // 3, (i + 1) * count // 3):
            hidden_grad_part(k)

    carry_done = [carry_over(init, 0, False, fill_forward)]
    act_copies = []
    for k in range(width // LANES):
        cols = pl.ds(k * LANES, LANES)
        lr, li = tile(lam, (0,), every, cols), tile(lam, (1,), every, cols)
        cr, ci = tile(coef, (0,), every, cols), tile(coef, (1,), every, cols)
        row_a[...] = u_ref[:, :, cols]
        for b in range(streams):

            def move(p, carry, b=b, lr=lr, li=li, cr=cr, ci=ci):
                sr, si = carry
                u = row(row_a, b, p)
                m = row(keep, b, p)
                sr = sr * m
                si = si * m
                nr = (lr * sr - li * si) + u
                ni = lr * si + li * sr
                part[pl.ds(pl.multiple_of(p * 8, 8), 8), :] = (cr * nr - ci * ni).sum(0)
                return nr, ni

            begin = (tile(init, (b, 0), every, cols), tile(init, (b, 1), every, cols))
            lax.fori_loop(0, length, move, begin, unroll=2)
            total = part[pl.ds(0, length, stride=8), :]
            for j in range(1, 8):
                total = total + part[pl.ds(j, length, stride=8), :]
            y = total + skip_ref[:, cols] * u_ref[b, :, cols]
            y_ref[b, :, cols] = y
            to = pl.ds(pl.multiple_of(c * width + k * LANES, LANES), LANES)
            act_full[b * length : (b + 1) * length, to] = gelu_parts(y)[0].astype(bf16)
        act_copies.append(chan_all(lambda j: (act_full.at[:, to], act_full.at[:, to]), 2 + k))
    base = 2 + width // LANES

    loads[1].wait()
    loads[2].wait()
    for copies in act_copies:
        landed(copies)
    val[...] = dot(act_full[...], gluv[...])
    gate[...] = jax.nn.sigmoid(dot(act_full[...], glug[...]))
    resid[...] = rows_in_of(x_ref, tokens, width) + val[...] * gate[...]

    sum2 = jnp.sum(resid[...], axis=1, keepdims=True)
    square2 = jnp.sum(resid[...] * resid[...], axis=1, keepdims=True)
    stat_copies = stats_start(sum2, square2, 1, base)
    for k in range(n_chan):
        act_t[pl.ds(k * width, width), :] = act_full[:, k * width : (k + 1) * width].T
    average, square = stats_end(stat_copies, 1)
    scaler2 = lax.rsqrt(square - average * average + epsilon)
    normed2[...] = (resid[...] - average) * scaler2
    mid_full[:, own_cols] = (normed2[...] * gain2[...]).astype(bf16)
    mid_copies = chan_all(lambda j: (mid_full.at[:, own_cols], mid_full.at[:, own_cols]), base + 1)
    loads[3].wait()
    landed(mid_copies)

    for k in range(units // unit_block):
        cols = pl.ds(k * unit_block, unit_block)
        value, slope = gelu_parts(dot(mid_full[...], win[:, cols]))
        hidden[:, cols] = value.astype(bf16)
        pre[:, cols] = (hidden_grad[:, cols] * slope).astype(bf16)
        hidden_t[cols, :] = hidden[:, cols].T
    for k in range(n_chan):
        mid_t[pl.ds(k * width, width), :] = mid_full[:, k * width : (k + 1) * width].T
    move_rings()

    def scatter_start(piece, own, k, phase):
        copies = []
        for j in range(1, n_chan):
            rs_send[k, j - 1] = piece(chan_block(chan_peer(j), width)).astype(bf16)
            copy = chan_copy(rs_send.at[k, j - 1], rs_recv.at[k, j - 1], phase, j)
            copy.start()
            copies.append(copy)
        sent.extend(copies)
        own[...] = piece(own_cols)
        return copies

    def scatter_end(copies, own, k):
        landed(copies)
        total = own[...]
        for j in range(1, n_chan):
            total = total + rs_recv[k, j - 1].astype(f32)
        return total

    grad_parts = scatter_start(lambda rows: dot(pre[...], win[rows, :], NT), part_own, 0, base + 2)
    out_parts = scatter_start(lambda cols: dot(hidden[...], wout[:, cols]), out_own, 1, base + 3)
    move_rings()

    mid_grad[...] = scatter_end(grad_parts, part_own, 0)
    scaled = mid_grad[...] * gain2[...]
    stat_copies = stats_start(
        jnp.sum(scaled, axis=1, keepdims=True),
        jnp.sum(scaled * normed2[...], axis=1, keepdims=True), 2, base + 4,
    )
    gains = jnp.sum(mid_grad[...] * normed2[...], axis=0, keepdims=True)
    first, second = stats_end(stat_copies, 2)
    resid_grad[...] = og_ref[...].reshape(tokens, width) + scaler2 * (
        mid_grad[...] * gain2[...] - first - normed2[...] * second
    )

    value_grad[...] = (resid_grad[...] * gate[...]).astype(bf16)
    gate_grad[...] = (resid_grad[...] * val[...] * gate[...] * (1.0 - gate[...])).astype(bf16)
    act_parts = scatter_start(
        lambda rows: dot(value_grad[...], gluv[rows, :], NT) + dot(gate_grad[...], glug[rows, :], NT), act_own, 2, base + 5
    )
    move_rings()
    move_glu()
    act_grad = scatter_end(act_parts, act_own, 2)
    mixer_grad[...] = act_grad.reshape(streams, length, width) * gelu_parts(y_ref[...])[1]

    edges(mixer_grad, first_mask, True)
    move_rings()
    move_glu()

    def fill_backward(i):
        if i == 0:
            total = scatter_end(out_parts, out_own, 1)
            block_out[...] = (resid[...] + total).reshape(streams, length, width)
        move_rings()
        move_glu()

    carry_done.append(carry_over(adj, 1, True, fill_backward))
    zero = jnp.zeros((group // 8, 8, LANES), f32)
    for k in range(width // LANES):
        cols = pl.ds(k * LANES, LANES)
        row_a[...] = u_ref[:, :, cols]
        row_b[...] = mixer_grad[:, :, cols]
        for h in range(n_states // group):
            rows = pl.ds(h * group, group)
            lr, li = tile(lam, (0,), rows, cols), tile(lam, (1,), rows, cols)
            cr, ci = tile(coef, (0,), rows, cols), tile(coef, (1,), rows, cols)

            def again(p, carry, lr=lr, li=li):
                new = []
                for b in range(streams):
                    sr, si = carry[2 * b], carry[2 * b + 1]
                    u = row(row_a, b, p)
                    m = row(keep, b, p)
                    sr = sr * m
                    si = si * m
                    nr = (lr * sr - li * si) + u
                    ni = lr * si + li * sr
                    states[p + 1, b, 0] = nr
                    states[p + 1, b, 1] = ni
                    new += [nr, ni]
                return tuple(new)

            begin = []
            for b in range(streams):
                begin += [tile(init, (b, 0), rows, cols), tile(init, (b, 1), rows, cols)]
                states[0, b, 0] = begin[-2]
                states[0, b, 1] = begin[-1]
            lax.fori_loop(0, length, again, tuple(begin), unroll=2)

            def back(i, carry, h=h, lr=lr, li=li, cr=cr, ci=ci):
                glr, gli, gcr, gci = carry[:4]
                adjoint = carry[4:]
                p = length - 1 - i
                new = []
                for b in range(streams):
                    ar, ai = adjoint[2 * b], adjoint[2 * b + 1]
                    g = row(row_b, b, p)
                    m = row(keep, b, p)
                    nr = (lr * ar + li * ai) + cr * g
                    ni = (lr * ai - li * ar) - ci * g
                    spot = pl.ds(pl.multiple_of((b * length + p) * 8, 8), 8)
                    if h == 0:
                        part[spot, :] = nr.sum(0)
                    else:
                        part[spot, :] += nr.sum(0)
                    gcr = gcr + g * states[p + 1, b, 0]
                    gci = gci - g * states[p + 1, b, 1]
                    nr = nr * m
                    ni = ni * m
                    sr, si = states[p, b, 0], states[p, b, 1]
                    glr = glr + (nr * sr + ni * si)
                    gli = gli + (ni * sr - nr * si)
                    new += [nr, ni]
                return (glr, gli, gcr, gci, *new)

            begin = []
            for b in range(streams):
                begin += [tile(adj, (b, 0), rows, cols), tile(adj, (b, 1), rows, cols)]
            sums = lax.fori_loop(0, length, back, (zero, zero, zero, zero, *begin))
            glr, gli, gcr, gci = [item.reshape(-1, LANES) for item in sums[:4]]
            share = factor[rows, cols]
            ratio = (1.0 - share * share) / share
            spots = [pl.ds(i * n_states + h * group, group) for i in range(4)]
            table[spots[0], cols] = (gcr * param[2, rows, cols] + gci * param[3, rows, cols]) * ratio - (
                glr * lam[0, rows, cols] + gli * lam[1, rows, cols]
            )
            table[spots[1], cols] = gli * lam[0, rows, cols] - glr * lam[1, rows, cols]
            table[spots[2], cols] = share * gcr
            table[spots[3], cols] = share * gci
            move_rings()
            move_glu()
        for b in range(streams):
            total = part[pl.ds(b * length * 8, length, stride=8), :]
            for j in range(1, 8):
                total = total + part[pl.ds(b * length * 8 + j, length, stride=8), :]
            u_grad = total + skip_ref[:, cols] * row_b[b]
            du[b * length : (b + 1) * length, cols] = u_grad * valid[b]

    scaled = du[...] * gain1[...]
    stat_copies = stats_start(
        jnp.sum(scaled, axis=1, keepdims=True),
        jnp.sum(scaled * normed1[...], axis=1, keepdims=True), 3, base + 6,
    )
    gain_rows = [
        jnp.sum(du[...] * normed1[...], axis=0, keepdims=True),
        jnp.sum(jnp.sum(mixer_grad[...] * u_ref[...], axis=0), axis=0, keepdims=True),
        gains,
    ]
    table[4 * n_states :, :] = jnp.concatenate(
        [*gain_rows, jnp.zeros((table.shape[0] - 4 * n_states - 3, width), f32)], axis=0
    )

    def table_copy(src, dst, k, to):
        return pltpu.make_async_remote_copy(
            src_ref=src, dst_ref=dst, send_sem=seq_send.at[2, k], recv_sem=seq_recv.at[2, k],
            device_id=to, device_id_type=MESH,
        )

    swap = table_copy(table, table_recv, 0, partner)
    swap.start()
    first, second = stats_end(stat_copies, 3)
    in_grad[...] = (
        resid_grad[...] + scaler1 * (du[...] * gain1[...] - first - normed1[...] * second)
    ).reshape(streams, length, width)
    move_rings()
    move_glu()
    swap.wait()
    half_rows = table.shape[0] // 2
    mine = pl.ds(pl.multiple_of(odd * half_rows, 8), half_rows)
    table_line[level] = table[mine, :] + table_recv[mine, :]
    lines = []
    for d in range(1, pairs):
        to = 2 * lax.rem(level + d, pairs) + odd
        copy = pltpu.make_async_remote_copy(
            src_ref=table_line.at[level], dst_ref=table_line.at[level],
            send_sem=seq_send.at[2, 1 + d], recv_sem=seq_recv.at[2, 1 + d],
            device_id=(to, c), device_id_type=MESH,
        )
        copy.start()
        lines.append(copy)
    move_rings()
    move_glu()
    for copy in lines:
        copy.wait_recv()
    total = table_line[0]
    for k in range(1, pairs):
        total = total + table_line[k]
    table[mine, :] = total
    merge = table_copy(table.at[mine, :], table_back, 1, partner)
    merge.start()
    move_rings()
    move_glu()
    merge.wait_recv()
    table[pl.ds(pl.multiple_of((1 - odd) * half_rows, 8), half_rows), :] = table_back[...]
    tables_out[0] = table[0 : 2 * n_states, :].T
    tables_out[1] = table[2 * n_states : 4 * n_states, :].T
    gains_out[...] = table[4 * n_states : 4 * n_states + 8, :]
    while min(at) < SLOTS:
        move_rings()
        move_glu()
    for ring in (*rings, *glu_rings):
        ring.finish()
    for copy in (*sent, *lines, merge):
        copy.wait_send()
    for done in carry_done:
        done()


def rows_in_of(ref, tokens, width):
    return ref[...].reshape(tokens, width)


def cast_kernel(
    gin, gout, gv, gg, block, grad, tables, gains,
    gin_out, gout_out, gv_out, gg_out, block_out, grad_out, dec_out, ang_out, real_out, imag_out,
):
    gin_out[...] = gin[...].astype(f32)
    gout_out[...] = gout[...].astype(f32)
    gv_out[...] = gv[...].astype(f32)
    gg_out[...] = gg[...].astype(f32)

    @pl.when(pl.program_id(0) == 0)
    def _():
        block_out[...] = block[...]
        grad_out[...] = grad[...]
        n = dec_out.shape[1]
        dec_out[...] = tables[0, :, :n]
        ang_out[...] = tables[0, :, n:]
        real_out[...] = tables[1, :, :n]
        imag_out[...] = tables[1, :, n:]


def per_device(
    sizes, block_in, doc_lengths, out_grad, first_gain, decay_rate, turn_angle, out_real, out_imag,
    skip_gain, glu_value, glu_gate, second_gain, ffn_in, ffn_out,
):
    n_seq, n_chan = sizes
    pairs = n_seq // 2
    streams, length, width = block_in.shape
    n_states = decay_rate.shape[1]
    tokens = streams * length
    full = width * n_chan
    units = ffn_in.shape[1]
    glu_cols = glu_value.shape[1]
    group = min(32, n_states)
    like = jax.ShapeDtypeStruct
    table_rows = 4 * n_states + 16
    phases = 2 + width // LANES + 7
    ticks = 2 * n_seq - 2
    in_rows, out_rows, glu_rows = full // n_seq, units // n_seq, full // n_seq
    act = (streams, length, width)
    flat = (tokens, width)
    mask = (streams, length, LANES)
    tab = (2, n_states, width)
    V = pltpu.VMEM
    scratch = [
        V((full, glu_cols), bf16), V((full, glu_cols), bf16), V((full, units), bf16), V((units, full), bf16),
        V(mask, f32), V(mask, f32), V(mask, f32), V(mask, f32),
        V((4, n_states, width), f32), V(tab, f32), V(tab, f32), V(tab, f32), V((n_states, width), f32),
        V(flat, f32), V(act, f32), V(act, f32), V((streams, *tab), f32), V((streams, *tab), f32), V((streams, *tab), f32),
        V((tokens, full), bf16), V((tokens, glu_cols), f32), V((tokens, glu_cols), f32), V(flat, f32), V(flat, f32),
        V((tokens, full), bf16), V((tokens, full), bf16), V((tokens, units), f32), V((tokens, units), bf16), V((tokens, units), bf16),
        V((full, tokens), bf16), V((full, tokens), bf16), V((units, tokens), bf16),
        V(flat, f32), V(flat, f32), V(flat, f32), V(flat, f32), V((tokens, glu_cols), bf16), V((tokens, glu_cols), bf16), V(flat, f32),
        V(act, f32), V(flat, f32),
        V(mask, f32), V(mask, f32), V((tokens * 8, LANES), f32), V((length + 1, streams, 2, group // 8, 8, LANES), f32),
        V((4, 8, tokens), f32), V((4, n_chan - 1, 8, tokens), f32), V((3, n_chan - 1, *flat), bf16), V((3, n_chan - 1, *flat), bf16),
        V((2, streams, *tab), bf16), V((2, streams, *tab), bf16), V((2, *tab), bf16), V((2, pairs - 1, *tab), bf16),
        V((2, *tab), f32), V((2, *tab), bf16), V((2, *tab), bf16),
        V((table_rows, width), f32), V((table_rows, width), f32), V((pairs, table_rows // 2, width), f32), V((table_rows // 2, width), f32),
        V((2, in_rows, units // 2), bf16), V((2, n_seq - 1, in_rows, units // 2), bf16),
        V((2, out_rows, full // 2), bf16), V((2, n_seq - 1, out_rows, full // 2), bf16),
        V((glu_rows, glu_cols), bf16), V((n_seq - 1, glu_rows, glu_cols), bf16),
        V((glu_rows, glu_cols), bf16), V((n_seq - 1, glu_rows, glu_cols), bf16),
        pltpu.SemaphoreType.DMA((4,)),
        pltpu.SemaphoreType.DMA((phases, n_chan - 1)), pltpu.SemaphoreType.DMA((phases, n_chan - 1)),
        pltpu.SemaphoreType.DMA((3, pairs + 1)), pltpu.SemaphoreType.DMA((3, pairs + 1)),
        pltpu.SemaphoreType.DMA((6, ticks)), pltpu.SemaphoreType.DMA((6, ticks)),
    ]
    specs = [pl.BlockSpec(memory_space=pltpu.SMEM)] + [VM] * 8 + [ANY, ANY, VM, ANY, ANY]
    made = pl.pallas_call(
        functools.partial(block_kernel, sizes),
        out_shape=(
            like(act, f32), like(act, f32), like((2, width, 2 * n_states), f32), like((8, width), f32),
            like((full, units), bf16), like((units, full), bf16), like((full, glu_cols), bf16), like((full, glu_cols), bf16),
        ),
        in_specs=specs,
        out_specs=(VM,) * 8,
        scratch_shapes=scratch,
        compiler_params=pltpu.CompilerParams(
            collective_id=0, has_side_effects=True, vmem_limit_bytes=58 * 1024 * 1024
        ),
        name="block",
    )(
        doc_lengths, block_in, out_grad, first_gain[None], decay_rate, turn_angle, out_real, out_imag, skip_gain[None],
        glu_value, glu_gate, second_gain[None], ffn_in, ffn_out,
    )
    block_out, in_grad, tables, gains, gin, gout, gv, gg = made
    steps = 4

    def rows(n, m):
        return pl.BlockSpec((n // steps, m), lambda i: (i, 0))

    def whole(*shape):
        return pl.BlockSpec(shape, lambda i: (0,) * len(shape))

    small = (width, n_states)
    cast = pl.pallas_call(
        cast_kernel,
        grid=(steps,),
        out_shape=(
            like((full, units), f32), like((units, full), f32), like((full, glu_cols), f32), like((full, glu_cols), f32),
            like(act, f32), like(act, f32), like(small, f32), like(small, f32), like(small, f32), like(small, f32),
        ),
        in_specs=[
            rows(full, units), rows(units, full), rows(full, glu_cols), rows(full, glu_cols), whole(*act), whole(*act),
            whole(2, width, 2 * n_states), whole(8, width),
        ],
        out_specs=(
            rows(full, units), rows(units, full), rows(full, glu_cols), rows(full, glu_cols), whole(*act), whole(*act),
            whole(*small), whole(*small), whole(*small), whole(*small),
        ),
        compiler_params=pltpu.CompilerParams(vmem_limit_bytes=32 * 1024 * 1024),
        name="cast",
    )(gin, gout, gv, gg, block_out, in_grad, tables, gains)
    gin, gout, gv, gg, block_out, in_grad, dec, ang, real, imag = cast
    return (
        block_out, in_grad, gains[0], dec, ang, real, imag, gains[1], gv, gg, gains[2], gin, gout,
    )


def solution(mesh):
    act = P(None, "seq", "chan")
    vec, mat = P("chan"), P("chan", None)
    col = P(None, "chan")
    sizes = (mesh.shape["seq"], mesh.shape["chan"])
    return jax.shard_map(
        functools.partial(per_device, sizes),
        mesh=mesh,
        in_specs=(act, P(), act, vec, mat, mat, mat, mat, vec, col, col, vec, col, mat),
        out_specs=(act, act, vec, mat, mat, mat, mat, vec, col, col, vec, col, mat),
        check_vma=False,
    )
```

```python
import functools

import jax
import jax.numpy as jnp
from jax import lax
from jax.experimental import pallas as pl
from jax.experimental.pallas import tpu as pltpu
from jax.sharding import PartitionSpec as P

epsilon = 1e-05
LANES = 128
MESH = pl.DeviceIdType.MESH
VM = pl.BlockSpec(memory_space=pltpu.VMEM)
ANY = pl.BlockSpec(memory_space=pl.ANY)
GELU_A = 0.7978845608028654
GELU_B = 0.044715
NN = (((1,), (0,)), ((), ()))
NT = (((1,), (1,)), ((), ()))
f32, bf16 = jnp.float32, jnp.bfloat16


def gelu_parts(x):
    inner = GELU_A * (x + GELU_B * (x * x * x))
    t = jnp.tanh(inner)
    half = 0.5 * (1.0 + t)
    slope = half + 0.5 * x * (1.0 - t * t) * (GELU_A * (1.0 + 3.0 * GELU_B * (x * x)))
    return x * half, slope


def dot(a, b, dims=NN):
    return lax.dot_general(a, b, dims, preferred_element_type=f32)


def cmul(ar, ai, br, bi):
    return ar * br - ai * bi, ar * bi + ai * br


def power(re, im, count):
    out = None
    while count:
        if count & 1:
            out = (re, im) if out is None else cmul(*out, re, im)
        re, im = cmul(re, im, re, im)
        count >>= 1
    return out


def row(ref, b, p):
    return jnp.broadcast_to(ref[b, pl.ds(p, 1), :], (8, LANES))


def tile(ref, lead, rows, cols):
    return ref[(*lead, rows, cols)].reshape(-1, 8, LANES)


class Line:
    def __init__(self, own, count, at, send, inward, across, sems, where, hand_over, stores=None):
        self.own, self.count, self.at = own, count, at
        self.send, self.inward, self.across = send, inward, across
        self.sent, self.got = sems
        self.pairs, self.is_end, self.is_mid, self.toward, self.away, self.partner = where
        self.hand_over, self.stores = hand_over, stores

    def copy(self, src, dst, i, sent, got, to):
        return pltpu.make_async_remote_copy(
            src_ref=src, dst_ref=dst, send_sem=self.sent.at[sent, i], recv_sem=self.got.at[got, i],
            device_id=to, device_id_type=MESH,
        )

    def pass_in(self, i):
        self.copy(self.send.at[i], self.inward.at[i], i, 0, 0, self.toward).start()

    def pass_across(self, i):
        self.copy(self.send.at[i], self.across.at[i], i, 0, 1, self.toward).start()

    def pass_out(self, i):
        self.copy(self.at(i), self.at(i), i, 1, 2, self.away).start()

    def pass_pair(self, i):
        self.copy(self.at(i), self.at(i), i, 2, 3, self.partner).start()

    def arrived(self, i, kind):
        self.copy(self.send.at[i], self.send.at[i], i, 0, kind, self.toward).wait_recv()

    def begin(self, i):
        if self.pairs > 2:

            @pl.when(self.is_end)
            def _():
                self.send[i] = self.own(i).astype(self.send.dtype)
                self.pass_in(i)

    def join(self, i):
        if self.pairs == 2:
            self.send[i] = self.own(i).astype(self.send.dtype)
            self.pass_across(i)
            return

        @pl.when(jnp.logical_not(self.is_end))
        def _():
            total = self.own(i)
            self.arrived(i, 0)
            self.send[i] = (total + self.inward[i].astype(f32)).astype(self.send.dtype)
            if self.pairs == 4:
                self.pass_across(i)
                return

            @pl.when(self.is_mid)
            def _():
                self.pass_across(i)

            @pl.when(jnp.logical_not(self.is_mid))
            def _():
                self.pass_in(i)

    def settle(self, i):
        @pl.when(self.is_mid)
        def _():
            self.arrived(i, 1)
            total = self.send[i].astype(f32) + self.across[i].astype(f32)
            self.at(i)[...] = total.astype(self.send.dtype)
            if self.pairs > 2:
                self.pass_out(i)
            if self.hand_over:
                self.pass_pair(i)

    def relay(self, i):
        if self.pairs > 2:

            @pl.when(jnp.logical_not(self.is_mid))
            def _():
                self.arrived(i, 2)
                if self.pairs > 4:

                    @pl.when(jnp.logical_not(self.is_end))
                    def _():
                        self.pass_out(i)

                if self.hand_over:
                    self.pass_pair(i)

    def saves(self, i):
        return [pltpu.make_async_copy(src, dst, sem) for src, dst, sem in self.stores(i)]

    def store(self, i):
        self.arrived(i, 3)
        for save in self.saves(i):
            save.start()

    def finish(self):
        for i in range(self.count):
            if self.stores:
                for save in self.saves(i):
                    save.wait()
            self.copy(self.send.at[i], self.send.at[i], i, 0, 0, self.toward).wait_send()
            if self.pairs > 2:

                @pl.when(jnp.logical_not(self.is_end))
                def _(i=i):
                    self.copy(self.send.at[i], self.send.at[i], i, 1, 2, self.toward).wait_send()

            if self.hand_over:
                done = self.copy(self.send.at[i], self.send.at[i], i, 2, 3, self.toward)
                done.wait_send()


def block_kernel(
    sizes,
    docs, x_ref, og_ref, gain1, dec_ref, ang_ref, real_ref, imag_ref, skip_ref, gluv_hbm, glug_hbm, gain2, win_hbm, wout_hbm,
    block_out, in_grad, tables_out, gains_out, gin_hbm, gout_hbm, gv_hbm, gg_hbm,
    gin_out, gout_out, gv_out, gg_out, gluv, glug, win, wout,
    keep, first_mask, last_mask, valid,
    lam, coef, step_l, factor,
    gain_full, normed1, u_ref, y_ref, edge_sum, init, adj,
    act_full, val, gate, resid, normed2, grad_full, mid_full, hidden_grad, hidden, pre,
    act_t, mid_t, hidden_t, part_own, mid_grad, result_own, resid_grad, value_grad, gate_grad, act_own, mixer_grad, du,
    row_a, row_b, part, states,
    stat_send, stat_recv, rs_send, rs_recv,
    pair_send, pair_recv, line_send, line_recv, back_send, back_low, back_recv,
    table, table2, table_sum, table_send, table_in, table_across,
    gain_sums, gain_sums2, gains_sum, gains_send, gains_in, gains_across,
    grad2, act2, mid2, act_t2, mid_t2, hidden_t2, pre2, value2, gate2,
    in_send, in_in, in_across, out_send, out_in, out_across, gv_send, gv_in, gv_across, gg_send, gg_in, gg_across,
    load_sem, save_sem, chan_send, chan_recv, seq_send, seq_recv, fac_send, fac_recv, line_sent, line_got,
):
    n_seq, n_chan = sizes
    pairs = n_seq // 2
    streams, length, width = x_ref.shape
    n_states = lam.shape[1]
    tokens = streams * length
    full = width * n_chan
    units = win.shape[1]
    group = states.shape[3] * 8
    s, c = lax.axis_index("seq"), lax.axis_index("chan")
    odd = lax.rem(s, 2)
    level = lax.div(s, 2)
    partner = (s + 1 - 2 * odd, c)
    every = pl.ds(0, n_states)

    def chan_peer(j):
        return lax.rem(c + j, n_chan)

    def chan_block(k, size):
        return pl.ds(pl.multiple_of(k * size, size), size)

    own_cols = chan_block(c, width)

    barrier = pltpu.get_barrier_semaphore()
    for j in range(1, n_chan):
        pl.semaphore_signal(barrier, inc=1, device_id=(s, chan_peer(j)), device_id_type=MESH)
    pl.semaphore_signal(barrier, inc=1, device_id=partner, device_id_type=MESH)
    for d in range(1, pairs):
        other = 2 * lax.rem(level + d, pairs) + odd
        pl.semaphore_signal(barrier, inc=1, device_id=(other, c), device_id_type=MESH)

    loads = [
        pltpu.make_async_copy(src, dst, load_sem.at[i])
        for i, (src, dst) in enumerate(
            ((wout_hbm, wout), (gluv_hbm, gluv), (glug_hbm, glug), (win_hbm, win))
        )
    ]
    for load in loads:
        load.start()

    sent = []

    def chan_copy(src, dst, phase, j):
        return pltpu.make_async_remote_copy(
            src_ref=src, dst_ref=dst, send_sem=chan_send.at[phase, j - 1], recv_sem=chan_recv.at[phase, j - 1],
            device_id=(s, chan_peer(j)), device_id_type=MESH,
        )

    def chan_all(pick, phase):
        copies = []
        for j in range(1, n_chan):
            copy = chan_copy(*pick(j), phase, j)
            copy.start()
            copies.append(copy)
        sent.extend(copies)
        return copies

    def landed(copies):
        for copy in copies:
            copy.wait_recv()

    lane = lax.broadcasted_iota(jnp.int32, (tokens, LANES), 1)

    def stats_start(first, second, k, phase):
        packed = jnp.where(lane == 0, first, jnp.where(lane == 1, second, 0.0))
        stat_send[k] = packed.T[:8]
        return chan_all(lambda j: (stat_send.at[k], stat_recv.at[k, j - 1]), phase)

    def stats_end(copies, k):
        landed(copies)
        total = stat_send[k]
        for j in range(1, n_chan):
            total = total + stat_recv[k, j - 1]
        total = jnp.concatenate([total, jnp.zeros((LANES - 8, tokens), f32)], axis=0).T
        return total[:, 0:1] / full, total[:, 1:2] / full

    rows_in = x_ref[...].reshape(tokens, width)
    grad_full[:, own_cols] = og_ref[...].reshape(tokens, width).astype(bf16)
    sum1 = jnp.sum(rows_in, axis=1, keepdims=True)
    square1 = jnp.sum(rows_in * rows_in, axis=1, keepdims=True)
    pl.semaphore_wait(barrier, n_chan + pairs - 1)
    stat_copies = stats_start(sum1, square1, 0, 0)
    grad_copies = chan_all(lambda j: (grad_full.at[:, own_cols], grad_full.at[:, own_cols]), 1)
    gain_full[:, own_cols] = jnp.broadcast_to(gain2[...], (8, width))
    gain_copies = chan_all(lambda j: (gain_full.at[:, own_cols], gain_full.at[:, own_cols]), 11)

    start = s * length
    ends = []
    for b in range(streams):
        total, stream = 0, []
        for k in range(docs.shape[1]):
            total = total + docs[b, k]
            stream.append(total)
        ends.append(stream)

    def passed(b, at):
        count = jnp.int32(0)
        for end in ends[b]:
            count = count + jnp.where(end <= at, 1, 0)
        return count

    def kept(block, b):
        return jnp.where(
            passed(b, block * length - 1) == passed(b, block * length + length - 1), 1.0, 0.0
        )

    pair_flags = [[kept(2 * level + x, b) for b in range(2)] for x in range(2)]

    def line_flag(source):
        both = [kept(2 * source, b) * kept(2 * source + 1, b) for b in range(2)]
        return jnp.where(odd == 1, both[1], both[0])

    line_flags = [[line_flag(level + (d if back else -d)) for d in range(1, pairs)] for back in (False, True)]
    position = lax.broadcasted_iota(jnp.int32, (length, LANES), 0) + start
    for b in range(streams):
        here = jnp.zeros((length, LANES), jnp.int32)
        prior = jnp.zeros((length, LANES), jnp.int32)
        for end in ends[b]:
            here = here + jnp.where(position >= end, 1, 0)
            prior = prior + jnp.where(position > end, 1, 0)
        keep[b] = jnp.where(here == prior, 1.0, 0.0)
        first_mask[b] = jnp.where(here == passed(b, start - 1), 1.0, 0.0)
        last_mask[b] = jnp.where(here == passed(b, start + length - 1), 1.0, 0.0)
        valid[b] = jnp.where(position < ends[b][-1], 1.0, 0.0)

    decay, angle = dec_ref[...], ang_ref[...]
    magnitude = jnp.exp(-decay)
    a2 = angle * angle
    sine, cosine = jnp.ones_like(a2), jnp.ones_like(a2)
    for k in (13, 11, 9, 7, 5, 3):
        sine = 1.0 - sine * a2 * (1.0 / (k * (k - 1)))
    for k in (14, 12, 10, 8, 6, 4, 2):
        cosine = 1.0 - cosine * a2 * (1.0 / (k * (k - 1)))
    lam[0] = magnitude * cosine
    lam[1] = magnitude * (sine * angle)
    twice = 2.0 * decay
    series = jnp.ones_like(twice)
    for k in (9, 8, 7, 6, 5, 4, 3, 2):
        series = 1.0 - series * twice * (1.0 / k)
    factor[...] = jnp.sqrt(twice * series)
    coef[0] = real_ref[...] * factor[...]
    coef[1] = imag_ref[...] * factor[...]
    step_l[0], step_l[1] = power(lam[0], lam[1], length)

    average, square = stats_end(stat_copies, 0)
    scaler1 = lax.rsqrt(square - average * average + epsilon)
    normed1[...] = (rows_in - average) * scaler1
    for b in range(streams):
        rows = slice(b * length, (b + 1) * length)
        for k in range(width // LANES):
            cols = slice(k * LANES, (k + 1) * LANES)
            u_ref[b, :, cols] = normed1[rows, cols] * gain1[:, cols] * valid[b]

    def edges(values, mask, reverse, k):
            cols = pl.ds(k * LANES, LANES)
            row_a[...] = values[:, :, cols] * mask[...]
            for h in range(n_states // group):
                rows = pl.ds(h * group, group)
                l1r, l1i = tile(lam, (0,), rows, cols), tile(lam, (1,), rows, cols)
                l1i = -l1i if reverse else l1i
                l2r, l2i = cmul(l1r, l1i, l1r, l1i)
                l3r, l3i = cmul(l2r, l2i, l1r, l1i)
                l4r, l4i = cmul(l2r, l2i, l2r, l2i)

                def move(i, carry):
                    new = []
                    for b in range(streams):
                        sr, si = carry[2 * b], carry[2 * b + 1]
                        base = length - 4 - 4 * i if reverse else 4 * i
                        u = [row(row_a, b, base + (3 - j if reverse else j)) for j in range(4)]
                        nr = (l4r * sr - l4i * si) + (l3r * u[0] + l2r * u[1]) + (l1r * u[2] + u[3])
                        ni = (l4r * si + l4i * sr) + (l3i * u[0] + l2i * u[1]) + l1i * u[2]
                        new += [nr, ni]
                    return tuple(new)

                zero = jnp.zeros((group // 8, 8, LANES), f32)
                final = lax.fori_loop(0, length // 4, move, (zero,) * (2 * streams))
                cr, ci = tile(coef, (0,), rows, cols), tile(coef, (1,), rows, cols)
                for b in range(streams):
                    fr, fi = final[2 * b], final[2 * b + 1]
                    if reverse:
                        fr, fi = cmul(cr, -ci, fr, fi)
                    edge_sum[k, b, 0, rows] = fr.reshape(-1, LANES)
                    edge_sum[k, b, 1, rows] = fi.reshape(-1, LANES)

    class Carry:
        def __init__(self, target, which, reverse, k):
            self.target, self.which, self.reverse, self.k = target, which, reverse, k
            cols = pl.ds(k * LANES, LANES)
            self.sr = step_l[0, :, cols]
            self.si = -step_l[1, :, cols] if reverse else step_l[1, :, cols]
            self.leads = odd == (1 if reverse else 0)

        def copy(self, src, dst, i, to):
            return pltpu.make_async_remote_copy(
                src_ref=src.at[self.which, self.k], dst_ref=dst, send_sem=seq_send.at[self.which, self.k, i],
                recv_sem=seq_recv.at[self.which, self.k, i], device_id=to, device_id_type=MESH,
            )

        def advance(self, flag, vr, vi, ur, ui):
            r, i = cmul(ur, ui, vr, vi)
            return r * flag, i * flag

        def start(self):
            at = (self.which, self.k)
            pair_send[at] = edge_sum[self.k].astype(bf16)
            self.across = self.copy(pair_send, pair_recv.at[at], 0, partner)
            self.across.start()

        def line(self):
            at = (self.which, self.k)
            self.across.wait_recv()
            mine_r, mine_i = edge_sum[self.k, odd, 0], edge_sum[self.k, odd, 1]
            other_r, other_i = pair_recv[(*at, odd, 0)].astype(f32), pair_recv[(*at, odd, 1)].astype(f32)
            flag = jnp.where(odd == 1, *[pair_flags[0 if self.reverse else 1][b] for b in (1, 0)])
            lr, li = jnp.where(self.leads, mine_r, other_r), jnp.where(self.leads, mine_i, other_i)
            tr, ti = jnp.where(self.leads, other_r, mine_r), jnp.where(self.leads, other_i, mine_i)
            ar, ai = self.advance(flag, lr, li, self.sr, self.si)
            line_send[(*at, 0)] = (ar + tr).astype(bf16)
            line_send[(*at, 1)] = (ai + ti).astype(bf16)
            for d in range(1, pairs):
                to = level - d if self.reverse else level + d

                @pl.when(to >= 0 if self.reverse else to < pairs)
                def _(d=d, to=to):
                    self.onward(d, (2 * to + odd, c)).start()

        def onward(self, d, to=partner):
            return self.copy(line_send, line_recv.at[self.which, self.k, d - 1], 1 + d, to)

        def home(self):
            at = (self.which, self.k)
            dr, di = cmul(self.sr, self.si, self.sr, self.si)
            back_send[...] = jnp.zeros(back_send.shape, f32)
            for d in range(pairs - 1, 0, -1):
                source = level + d if self.reverse else level - d

                @pl.when(source < pairs if self.reverse else source >= 0)
                def _(d=d):
                    self.onward(d).wait_recv()
                    flag = line_flags[self.reverse][d - 1]
                    vr, vi = self.advance(flag, back_send[0], back_send[1], dr, di)
                    back_send[0] = vr + line_recv[(*at, d - 1, 0)].astype(f32)
                    back_send[1] = vi + line_recv[(*at, d - 1, 1)].astype(f32)

            back_low[at] = back_send[...].astype(bf16)
            self.back = self.copy(back_low, back_recv.at[at], 1, partner)
            self.back.start()

        def end(self):
            at = (self.which, self.k)
            cols = pl.ds(self.k * LANES, LANES)
            self.back.wait_recv()
            for b in range(streams):
                flag = pair_flags[1 if self.reverse else 0][b]
                near = [
                    jnp.where(odd == b, back_low[(*at, i)], back_recv[(*at, i)]).astype(f32) for i in range(2)
                ]
                far = self.advance(flag, *near, self.sr, self.si)
                for i in range(2):
                    other = far[i] + pair_recv[(*at, b, i)].astype(f32)
                    self.target[b, i, :, cols] = jnp.where(self.leads, near[i], other)

        def finish(self):
            self.across.wait_send()
            self.back.wait_send()

            for d in range(1, pairs):
                to = level - d if self.reverse else level + d

                @pl.when(to >= 0 if self.reverse else to < pairs)
                def _(d=d):
                    self.onward(d).wait_send()

    low_side = level < pairs // 2
    toward = (s + jnp.where(low_side, 2, -2), c)
    away = (s + jnp.where(low_side, -2, 2), c)
    where = (
        pairs,
        jnp.logical_or(level == 0, level == pairs - 1),
        jnp.logical_or(level == pairs // 2 - 1, level == pairs // 2),
        toward, away, partner,
    )
    factors = []

    def swap_factor(src, dst, k, to=partner):
        copy = pltpu.make_async_remote_copy(
            src_ref=src, dst_ref=dst, send_sem=fac_send.at[k], recv_sem=fac_recv.at[k], device_id=to, device_id_type=MESH
        )
        copy.start()
        factors.append(copy)
        return copy

    half_units = units // 2
    my_half = chan_block(odd, half_units)
    their_half = chan_block(1 - odd, half_units)
    wanted = {}

    def need(*names):
        for name in names:
            wanted[name].wait_recv()

    in_rows, in_cols = full // 2, half_units // 4
    out_cols = full // 8
    glu_rows, glu_half = full // 4, width // 2
    my_glu, their_glu = chan_block(odd, glu_half), chan_block(1 - odd, glu_half)

    def in_own(i):
        if i == 0:
            need("pre")
        rows, cols = pl.ds((i % 2) * in_rows, in_rows), (i // 2) * in_cols
        mine = pl.ds(pl.multiple_of(odd * half_units + cols, in_cols), in_cols)
        return dot(mid_t[rows, :], pre[:, mine]) + dot(mid_t2[rows, :], pre2[:, pl.ds(cols, in_cols)])

    def in_at(i):
        return gin_out.at[odd, i // 2, i % 2]

    def out_own(i):
        if i == 0:
            need("grad", "hidden")
        cols = pl.ds(i * out_cols, out_cols)
        return dot(hidden_t[my_half, :], grad_full[:, cols]) + dot(hidden_t2[...], grad2[:, cols])

    def out_at(i):
        return gout_out.at[odd, i]

    def glu_own(near, far, names):
        def own(i):
            if i == 0:
                need(*names)
            rows = pl.ds(i * glu_rows, glu_rows)
            return dot(act_t[rows, :], near[:, my_glu]) + dot(act_t2[rows, :], far[...])

        return own

    def glu_at(out):
        def at(i):
            return out.at[odd, i]

        return at

    def table_own(q):
        need(("table", q))
        return table[q] + table2[q]

    def gains_own(i):
        need("gains")
        return gain_sums[...] + gain_sums2[...]

    sem_at = [0]

    def line(own, count, at, bufs, hand_over, kept_at=None):
        spot, base = pl.ds(sem_at[0], count), sem_at[0]
        stores = None
        if kept_at:
            held, final, place = kept_at

            def stores(i):
                return [(held.at[(x, *place(i))], final.at[(x, *place(i))], save_sem.at[x, base + i]) for x in range(2)]

        sem_at[0] += count
        return Line(own, count, at, *bufs, (line_sent.at[:, spot], line_got.at[:, spot]), where, hand_over, stores)

    quarters = (width // LANES) * (n_states // group)
    in_line = line(in_own, 8, in_at, (in_send, in_in, in_across), True, (gin_out, gin_hbm, lambda i: (i // 2, i % 2)))
    out_line = line(out_own, 8, out_at, (out_send, out_in, out_across), True, (gout_out, gout_hbm, lambda i: (i,)))
    gv_line = line(glu_own(value_grad, value2, ("value",)), 4, glu_at(gv_out), (gv_send, gv_in, gv_across), True, (gv_out, gv_hbm, lambda i: (i,)))
    gg_line = line(glu_own(gate_grad, gate2, ("gate",)), 4, glu_at(gg_out), (gg_send, gg_in, gg_across), True, (gg_out, gg_hbm, lambda i: (i,)))
    table_line = line(table_own, quarters, lambda q: table_sum.at[q], (table_send, table_in, table_across), False)
    gains_line = line(gains_own, 1, lambda i: gains_sum.at[i], (gains_send, gains_in, gains_across), False)
    lines = [out_line, gv_line, in_line, gg_line, table_line, gains_line]
    pieces = [(entry, i) for entry in lines[:4] for i in range(entry.count)]
    tick, begun = [0], [0]
    MID, LAST, STORE = 2, 4, 8

    def launch(count):
        for _ in range(count):
            if begun[0] < len(pieces):
                entry, i = pieces[begun[0]]
                entry.begin(i)
            begun[0] += 1

    def pump(count, lead=3):
        for _ in range(count):
            t = tick[0]
            tick[0] += 1
            launch(t + 1 + lead - begun[0])
            for ahead, act in ((0, "join"), (-MID, "settle"), (-LAST, "relay"), (-STORE, "store")):
                if 0 <= t + ahead < len(pieces):
                    entry, i = pieces[t + ahead]
                    getattr(entry, act)(i)

    tiles = width // LANES
    forward = [Carry(init, 0, False, k) for k in range(tiles)]
    for k in range(tiles):
        edges(u_ref, last_mask, False, k)
        forward[k].start()
    unit_block = min(units, 256)

    def hidden_grad_part(i):
        cols = pl.ds(i * unit_block, unit_block)
        hidden_grad[:, cols] = dot(grad_full[...], wout[cols, :], NT)

    loads[0].wait()
    landed(grad_copies)
    blocks = units // unit_block
    for k in range(blocks // 2):
        hidden_grad_part(k)
    for k in range(tiles):
        forward[k].line()
    for k in range(blocks // 2, blocks):
        hidden_grad_part(k)
    for k in range(tiles):
        forward[k].home()
    wanted["grad"] = swap_factor(grad_full, grad2, 0)
    act_copies = []
    for k in range(tiles):
        forward[k].end()
        cols = pl.ds(k * LANES, LANES)
        lr, li = tile(lam, (0,), every, cols), tile(lam, (1,), every, cols)
        cr, ci = tile(coef, (0,), every, cols), tile(coef, (1,), every, cols)
        row_a[...] = u_ref[:, :, cols]
        for b in range(streams):

            def move(p, carry, b=b, lr=lr, li=li, cr=cr, ci=ci):
                sr, si = carry
                u = row(row_a, b, p)
                m = row(keep, b, p)
                sr = sr * m
                si = si * m
                nr = (lr * sr - li * si) + u
                ni = lr * si + li * sr
                part[pl.ds(pl.multiple_of(p * 8, 8), 8), :] = (cr * nr - ci * ni).sum(0)
                return nr, ni

            begin = (tile(init, (b, 0), every, cols), tile(init, (b, 1), every, cols))
            lax.fori_loop(0, length, move, begin, unroll=2)
            total = part[pl.ds(0, length, stride=8), :]
            for j in range(1, 8):
                total = total + part[pl.ds(j, length, stride=8), :]
            y = total + skip_ref[:, cols] * u_ref[b, :, cols]
            y_ref[b, :, cols] = y
            to = pl.ds(pl.multiple_of(c * width + k * LANES, LANES), LANES)
            act_full[b * length : (b + 1) * length, to] = gelu_parts(y)[0].astype(bf16)
        act_copies.append(chan_all(lambda j: (act_full.at[:, to], act_full.at[:, to]), 2 + k))
    base = 2 + width // LANES

    loads[1].wait()
    loads[2].wait()
    for copies in act_copies:
        landed(copies)
    beside = (s, c + 1 - 2 * lax.rem(c, 2))
    core_half = chan_block(lax.rem(c, 2), tokens // 2)
    wanted["act_near"] = swap_factor(act_full.at[core_half, :], act2.at[core_half, :], 1)
    val[...] = dot(act_full[...], gluv[...])
    gate[...] = jax.nn.sigmoid(dot(act_full[...], glug[...]))
    resid[...] = rows_in_of(x_ref, tokens, width) + val[...] * gate[...]

    sum2 = jnp.sum(resid[...], axis=1, keepdims=True)
    square2 = jnp.sum(resid[...] * resid[...], axis=1, keepdims=True)
    stat_copies = stats_start(sum2, square2, 1, base)
    average, square = stats_end(stat_copies, 1)
    scaler2 = lax.rsqrt(square - average * average + epsilon)
    normed2[...] = (resid[...] - average) * scaler2
    mid_full[:, own_cols] = (normed2[...] * gain2[...]).astype(bf16)
    mid_copies = chan_all(lambda j: (mid_full.at[:, own_cols], mid_full.at[:, own_cols]), base + 1)
    loads[3].wait()
    landed(mid_copies)

    for k in range(units // unit_block):
        cols = pl.ds(k * unit_block, unit_block)
        value, slope = gelu_parts(dot(mid_full[...], win[:, cols]))
        hidden[:, cols] = value.astype(bf16)
        pre[:, cols] = (hidden_grad[:, cols] * slope).astype(bf16)
        hidden_t[cols, :] = hidden[:, cols].T
    def scatter_fill(piece, own, k):
        for j in range(1, n_chan):
            rs_send[k, j - 1] = piece(chan_block(chan_peer(j), width)).astype(bf16)
        own[...] = piece(own_cols)

    def scatter_start(k, phase):
        return chan_all(lambda j: (rs_send.at[k, j - 1], rs_recv.at[k, j - 1]), phase)

    def transposed(source, target, count):
        for k in range(count):
            target[pl.ds(k * width, width), :] = source[:, k * width : (k + 1) * width].T

    def scatter_end(copies, own, k):
        landed(copies)
        total = own[...]
        for j in range(1, n_chan):
            total = total + rs_recv[k, j - 1].astype(f32)
        return total

    scatter_fill(lambda rows: dot(pre[...], win[rows, :], NT), part_own, 0)
    grad_parts = scatter_start(0, base + 2)
    wanted["hidden"] = swap_factor(hidden_t.at[their_half, :], hidden_t2, 4)
    landed(gain_copies)
    first, second = 0.0, 0.0
    for j in range(n_chan):
        cols = chan_block(chan_peer(j), width) if j else own_cols
        values = rs_send[0, j - 1].astype(f32) if j else part_own[...]
        first = first + jnp.sum(values * gain_full[0:1, cols], axis=1, keepdims=True)
        second = second + jnp.sum(values * mid_full[:, cols].astype(f32), axis=1, keepdims=True)
    stat_copies = stats_start(first, second, 2, base + 4)
    scatter_fill(lambda cols: dot(hidden[...], wout[:, cols]), result_own, 1)
    transposed(act_full, act_t, n_chan)
    transposed(mid_full, mid_t, n_chan)
    wanted["act_near"].wait_recv()
    wanted["act_far"] = swap_factor(act2.at[core_half, :], act2.at[core_half, :], 9, beside)
    launch(2)
    mid_grad[...] = scatter_end(grad_parts, part_own, 0)
    wanted["pre"] = swap_factor(pre.at[:, their_half], pre2, 5)
    gains = jnp.sum(mid_grad[...] * normed2[...], axis=0, keepdims=True)
    first, second = stats_end(stat_copies, 2)
    resid_grad[...] = og_ref[...].reshape(tokens, width) + scaler2 * (
        mid_grad[...] * gain2[...] - first - normed2[...] * second
    )

    value_grad[...] = (resid_grad[...] * gate[...]).astype(bf16)
    gate_grad[...] = (resid_grad[...] * val[...] * gate[...] * (1.0 - gate[...])).astype(bf16)
    scatter_fill(
        lambda rows: dot(value_grad[...], gluv[rows, :], NT) + dot(gate_grad[...], glug[rows, :], NT), act_own, 2
    )
    act_parts = scatter_start(2, base + 5)
    wanted["value"] = swap_factor(value_grad.at[:, their_glu], value2, 6)
    wanted["gate"] = swap_factor(gate_grad.at[:, their_glu], gate2, 7)
    pump(1, 2)
    act_grad = scatter_end(act_parts, act_own, 2)
    mixer_grad[...] = act_grad.reshape(streams, length, width) * gelu_parts(y_ref[...])[1]

    out_parts = scatter_start(1, base + 3)

    backward = [Carry(adj, 1, True, k) for k in range(tiles)]
    for k in range(tiles):
        edges(mixer_grad, first_mask, True, k)
        backward[k].start()
        if k == 0:
            pump(1, 2)
    pump(1, 2)
    for k in range(tiles):
        backward[k].line()
    wanted["mid_near"] = swap_factor(mid_full.at[core_half, :], mid2.at[core_half, :], 2)
    pump(2, 2)
    total = scatter_end(out_parts, result_own, 1)
    block_out[...] = (resid[...] + total).reshape(streams, length, width)
    for k in range(tiles):
        backward[k].home()
    need("act_far")
    transposed(act2, act_t2, n_chan)
    pump(2, 2)
    zero = jnp.zeros((group // 8, 8, LANES), f32)
    q = 0
    for k in range(width // LANES):
        backward[k].end()
        cols = pl.ds(k * LANES, LANES)
        row_a[...] = u_ref[:, :, cols]
        row_b[...] = mixer_grad[:, :, cols]
        for h in range(n_states // group):
            rows = pl.ds(h * group, group)
            lr, li = tile(lam, (0,), rows, cols), tile(lam, (1,), rows, cols)
            cr, ci = tile(coef, (0,), rows, cols), tile(coef, (1,), rows, cols)

            def again(p, carry, lr=lr, li=li):
                new = []
                for b in range(streams):
                    sr, si = carry[2 * b], carry[2 * b + 1]
                    u = row(row_a, b, p)
                    m = row(keep, b, p)
                    sr = sr * m
                    si = si * m
                    nr = (lr * sr - li * si) + u
                    ni = lr * si + li * sr
                    states[p + 1, b, 0] = nr
                    states[p + 1, b, 1] = ni
                    new += [nr, ni]
                return tuple(new)

            begin = []
            for b in range(streams):
                begin += [tile(init, (b, 0), rows, cols), tile(init, (b, 1), rows, cols)]
                states[0, b, 0] = begin[-2]
                states[0, b, 1] = begin[-1]
            lax.fori_loop(0, length, again, tuple(begin), unroll=2)
            pump(2)
            if q == 0:
                wanted["mid_near"].wait_recv()
                wanted["mid_far"] = swap_factor(mid2.at[core_half, :], mid2.at[core_half, :], 3, beside)
            if q > 0:
                table_line.begin(q - 1)
            if q > 1:
                table_line.settle(q - 2)

            def back(i, carry, h=h, lr=lr, li=li, cr=cr, ci=ci):
                glr, gli, gcr, gci = carry[:4]
                adjoint = carry[4:]
                p = length - 1 - i
                new = []
                for b in range(streams):
                    ar, ai = adjoint[2 * b], adjoint[2 * b + 1]
                    g = row(row_b, b, p)
                    m = row(keep, b, p)
                    nr = (lr * ar + li * ai) + cr * g
                    ni = (lr * ai - li * ar) - ci * g
                    spot = pl.ds(pl.multiple_of((b * length + p) * 8, 8), 8)
                    if h == 0:
                        part[spot, :] = nr.sum(0)
                    else:
                        part[spot, :] += nr.sum(0)
                    gcr = gcr + g * states[p + 1, b, 0]
                    gci = gci - g * states[p + 1, b, 1]
                    nr = nr * m
                    ni = ni * m
                    sr, si = states[p, b, 0], states[p, b, 1]
                    glr = glr + (nr * sr + ni * si)
                    gli = gli + (ni * sr - nr * si)
                    new += [nr, ni]
                return (glr, gli, gcr, gci, *new)

            begin = []
            for b in range(streams):
                begin += [tile(adj, (b, 0), rows, cols), tile(adj, (b, 1), rows, cols)]
            sums = lax.fori_loop(0, length, back, (zero, zero, zero, zero, *begin))
            glr, gli, gcr, gci = [item.reshape(-1, LANES) for item in sums[:4]]
            share = factor[rows, cols]
            ratio = (1.0 - share * share) / share
            spots = [pl.ds(i * group, group) for i in range(4)]
            table[q, spots[0], :] = (gcr * real_ref[rows, cols] + gci * imag_ref[rows, cols]) * ratio - (
                glr * lam[0, rows, cols] + gli * lam[1, rows, cols]
            )
            table[q, spots[1], :] = gli * lam[0, rows, cols] - glr * lam[1, rows, cols]
            table[q, spots[2], :] = share * gcr
            table[q, spots[3], :] = share * gci
            wanted["table", q] = swap_factor(table.at[q], table2.at[q], 10 + q)
            if q == 0:
                need("mid_far")
                transposed(mid2, mid_t2, n_chan)
            pump(2)
            if q > 0:
                table_line.join(q - 1)
            if q > 1:
                table_line.relay(q - 2)
            q += 1
        for b in range(streams):
            total = part[pl.ds(b * length * 8, length, stride=8), :]
            for j in range(1, 8):
                total = total + part[pl.ds(b * length * 8 + j, length, stride=8), :]
            u_grad = total + skip_ref[:, cols] * row_b[b]
            du[b * length : (b + 1) * length, cols] = u_grad * valid[b]

    scaled = du[...] * gain1[...]
    stat_copies = stats_start(
        jnp.sum(scaled, axis=1, keepdims=True),
        jnp.sum(scaled * normed1[...], axis=1, keepdims=True), 3, base + 6,
    )
    gain_rows = [
        jnp.sum(du[...] * normed1[...], axis=0, keepdims=True),
        jnp.sum(jnp.sum(mixer_grad[...] * u_ref[...], axis=0), axis=0, keepdims=True),
        gains,
    ]
    gain_sums[...] = jnp.concatenate([*gain_rows, jnp.zeros((5, width), f32)], axis=0)
    wanted["gains"] = swap_factor(gain_sums, gain_sums2, 8)
    last = quarters - 1
    table_line.begin(last)
    if last > 0:
        table_line.settle(last - 1)
    first, second = stats_end(stat_copies, 3)
    in_grad[...] = (
        resid_grad[...] + scaler1 * (du[...] * gain1[...] - first - normed1[...] * second)
    ).reshape(streams, length, width)
    gains_line.begin(0)
    pump(1)
    table_line.join(last)
    if last > 0:
        table_line.relay(last - 1)
    gains_line.join(0)
    pump(2)
    table_line.settle(last)
    gains_line.settle(0)
    pump(2)
    table_line.relay(last)
    gains_line.relay(0)
    while tick[0] < len(pieces) + STORE:
        pump(1)
    for k in range(width // LANES):
        for h in range(n_states // group):
            for i in range(4):
                tables_out[i, h * group : (h + 1) * group, k * LANES : (k + 1) * LANES] = table_sum[
                    k * (n_states // group) + h, i * group : (i + 1) * group, :
                ]
    gains_out[...] = gains_sum[0]
    for entry in lines:
        entry.finish()
    for copy in factors:
        copy.wait_send()
    for copy in sent:
        copy.wait_send()
    for carry in (*forward, *backward):
        carry.finish()


def rows_in_of(ref, tokens, width):
    return ref[...].reshape(tokens, width)


def cast_kernel(
    steps, gin, gout, gv, gg, block, grad, tables, gains,
    gin_hbm, gout_hbm, gv_hbm, gg_hbm, block_out, grad_out, dec_out, ang_out, real_out, imag_out, gain_a, gain_b, gain_c,
    gin_low, gout_low, gv_low, gg_low, gin_out, gout_out, gv_out, gg_out, table_low, gain_low, block_low, grad_low, load_sem, save_sem, small_sem,
):
    whole = [
        pltpu.make_async_copy(src, dst, small_sem.at[i])
        for i, (src, dst) in enumerate(
            [(tables, table_low), (gains, gain_low), (block, block_low), (grad, grad_low)]
        )
    ]
    full, units = gin_out.shape
    loads, saves = [], []
    for p in range(steps):
        high = 2 * p // steps
        low = p % (steps // 2)
        rows, tall = full // steps, units // steps
        part = pl.ds(low * rows, rows)
        tall_part = pl.ds(low * tall, tall)
        here, tall_here = pl.ds(p * rows, rows), pl.ds(p * tall, tall)
        loads.append(
            [
                pltpu.make_async_copy(gin.at[:, :, high, part], gin_low.at[:, :, high, part], load_sem.at[0, p]),
                pltpu.make_async_copy(gout.at[high, :, tall_part], gout_low.at[high, :, tall_part], load_sem.at[1, p]),
                pltpu.make_async_copy(gv.at[:, here], gv_low.at[:, here], load_sem.at[2, p]),
                pltpu.make_async_copy(gg.at[:, here], gg_low.at[:, here], load_sem.at[3, p]),
            ]
        )
        saves.append(
            [
                pltpu.make_async_copy(gin_out.at[here], gin_hbm.at[here], save_sem.at[0, p]),
                pltpu.make_async_copy(gout_out.at[tall_here], gout_hbm.at[tall_here], save_sem.at[1, p]),
                pltpu.make_async_copy(gv_out.at[here], gv_hbm.at[here], save_sem.at[2, p]),
                pltpu.make_async_copy(gg_out.at[here], gg_hbm.at[here], save_sem.at[3, p]),
            ]
        )
    for copies in loads:
        for copy in copies:
            copy.start()
    for copy in whole:
        copy.start()
    for p in range(steps):
        high, low = 2 * p // steps, p % (steps // 2)
        rows, tall = full // steps, units // steps
        part, tall_part = slice(low * rows, (low + 1) * rows), slice(low * tall, (low + 1) * tall)
        here, tall_here = slice(p * rows, (p + 1) * rows), slice(p * tall, (p + 1) * tall)
        for copy in loads[p]:
            copy.wait()
        cols = gin.shape[-1]
        for x in range(2):
            for i in range(4):
                at = (4 * x + i) * cols
                gin_out[here, at : at + cols] = gin_low[x, i, high, part].astype(f32)
        cols = gout.shape[-1]
        for i in range(8):
            gout_out[tall_here, i * cols : (i + 1) * cols] = gout_low[high, i, tall_part].astype(f32)
        cols = gv.shape[-1]
        for x in range(2):
            gv_out[here, x * cols : (x + 1) * cols] = gv_low[x, here].astype(f32)
            gg_out[here, x * cols : (x + 1) * cols] = gg_low[x, here].astype(f32)
        for copy in saves[p]:
            copy.start()
    for copy in whole:
        copy.wait()
    passed_on = [
        pltpu.make_async_copy(block_low, block_out, small_sem.at[4]),
        pltpu.make_async_copy(grad_low, grad_out, small_sem.at[5]),
    ]
    for copy in passed_on:
        copy.start()
    for k, out in enumerate((dec_out, ang_out, real_out, imag_out)):
        out[...] = table_low[k]
    for k, out in enumerate((gain_a, gain_b, gain_c)):
        out[...] = gain_low[k : k + 1, :]
    for copies in (*saves, passed_on):
        for copy in copies:
            copy.wait()


def per_device(
    sizes, block_in, doc_lengths, out_grad, first_gain, decay_rate, turn_angle, out_real, out_imag,
    skip_gain, glu_value, glu_gate, second_gain, ffn_in, ffn_out,
):
    n_seq, n_chan = sizes
    pairs = n_seq // 2
    streams, length, width = block_in.shape
    n_states = decay_rate.shape[1]
    tokens = streams * length
    full = width * n_chan
    units = ffn_in.shape[1]
    glu_cols = glu_value.shape[1]
    group = min(32, n_states)
    like = jax.ShapeDtypeStruct
    quarters = (width // LANES) * (n_states // group)
    phases = 12
    act = (streams, length, width)
    flat = (tokens, width)
    mask = (streams, length, LANES)
    tab, lane_tab = (2, n_states, width), (2, n_states, LANES)
    tiles = width // LANES
    V = pltpu.VMEM
    scratch = [
        V((2, 4, 2, full // 2, units // 8), bf16), V((2, 8, units // 2, full // 8), bf16), *[V((2, 4, full // 4, glu_cols // 2), bf16)] * 2,
        V((full, glu_cols), bf16), V((full, glu_cols), bf16), V((full, units), bf16), V((units, full), bf16),
        V(mask, f32), V(mask, f32), V(mask, f32), V(mask, f32),
        V(tab, f32), V(tab, f32), V(tab, f32), V((n_states, width), f32),
        V((8, full), f32), V(flat, f32), V(act, f32), V(act, f32), V((tiles, streams, 2, n_states, LANES), f32), V((streams, *tab), f32), V((streams, *tab), f32),
        V((tokens, full), bf16), V((tokens, glu_cols), f32), V((tokens, glu_cols), f32), V(flat, f32), V(flat, f32),
        V((tokens, full), bf16), V((tokens, full), bf16), V((tokens, units), f32), V((tokens, units), bf16), V((tokens, units), bf16),
        V((full, tokens), bf16), V((full, tokens), bf16), V((units, tokens), bf16),
        V(flat, f32), V(flat, f32), V(flat, f32), V(flat, f32), V((tokens, glu_cols), bf16), V((tokens, glu_cols), bf16), V(flat, f32),
        V(act, f32), V(flat, f32),
        V(mask, f32), V(mask, f32), V((tokens * 8, LANES), f32), V((length + 1, streams, 2, group // 8, 8, LANES), f32),
        V((4, 8, tokens), f32), V((4, n_chan - 1, 8, tokens), f32), V((3, n_chan - 1, *flat), bf16), V((3, n_chan - 1, *flat), bf16),
        *[V((2, tiles, streams, *lane_tab), bf16)] * 2, V((2, tiles, *lane_tab), bf16), V((2, tiles, pairs - 1, *lane_tab), bf16),
        V(lane_tab, f32), *[V((2, tiles, *lane_tab), bf16)] * 2,
        *[V((quarters, 4 * group, LANES), f32)] * 6,
        V((8, width), f32), V((8, width), f32), *[V((1, 8, width), f32)] * 4,
        *[V((tokens, full), bf16)] * 3, V((full, tokens), bf16), V((full, tokens), bf16), V((units // 2, tokens), bf16),
        V((tokens, units // 2), bf16), V((tokens, glu_cols // 2), bf16), V((tokens, glu_cols // 2), bf16),
        *[V((8, full // 2, units // 8), bf16)] * 3, *[V((8, units // 2, full // 8), bf16)] * 3,
        *[V((4, full // 4, glu_cols // 2), bf16)] * 6,
        pltpu.SemaphoreType.DMA((4,)), pltpu.SemaphoreType.DMA((2, 24)),
        pltpu.SemaphoreType.DMA((phases, n_chan - 1)), pltpu.SemaphoreType.DMA((phases, n_chan - 1)),
        pltpu.SemaphoreType.DMA((2, tiles, pairs + 1)), pltpu.SemaphoreType.DMA((2, tiles, pairs + 1)),
        pltpu.SemaphoreType.DMA((10 + quarters,)), pltpu.SemaphoreType.DMA((10 + quarters,)),
        pltpu.SemaphoreType.DMA((3, 25 + quarters)), pltpu.SemaphoreType.DMA((4, 25 + quarters)),
    ]
    specs = [pl.BlockSpec(memory_space=pltpu.SMEM)] + [VM] * 8 + [ANY, ANY, VM, ANY, ANY]
    made = pl.pallas_call(
        functools.partial(block_kernel, sizes),
        out_shape=(
            like(act, f32), like(act, f32), like((4, n_states, width), f32), like((8, width), f32),
            like((2, 4, 2, full // 2, units // 8), bf16), like((2, 8, units // 2, full // 8), bf16),
            like((2, 4, full // 4, glu_cols // 2), bf16), like((2, 4, full // 4, glu_cols // 2), bf16),
        ),
        in_specs=specs,
        out_specs=(VM,) * 4 + (ANY,) * 4,
        scratch_shapes=scratch,
        compiler_params=pltpu.CompilerParams(
            collective_id=0, has_side_effects=True, vmem_limit_bytes=58 * 1024 * 1024
        ),
        name="block",
    )(
        doc_lengths, block_in, out_grad, first_gain[None], decay_rate.T, turn_angle.T, out_real.T, out_imag.T, skip_gain[None],
        glu_value, glu_gate, second_gain[None], ffn_in, ffn_out,
    )
    block_out, in_grad, tables, gains, gin, gout, gv, gg = made
    steps = 4
    small = (n_states, width)
    low_glu = (2, full, glu_cols // 2)
    cast = pl.pallas_call(
        functools.partial(cast_kernel, steps),
        out_shape=(
            like((full, units), f32), like((units, full), f32), like((full, glu_cols), f32), like((full, glu_cols), f32),
            like(act, f32), like(act, f32), like(small, f32), like(small, f32), like(small, f32), like(small, f32),
            *[like((1, width), f32)] * 3,
        ),
        in_specs=[ANY] * 8,
        out_specs=(ANY,) * 6 + (VM,) * 7,
        scratch_shapes=[
            V(gin.shape, bf16), V(gout.shape, bf16), V(low_glu, bf16), V(low_glu, bf16),
            V((full, units), f32), V((units, full), f32), V((full, glu_cols), f32), V((full, glu_cols), f32),
            V(tables.shape, f32), V(gains.shape, f32), V(act, f32), V(act, f32),
            pltpu.SemaphoreType.DMA((4, steps)), pltpu.SemaphoreType.DMA((4, steps)), pltpu.SemaphoreType.DMA((6,)),
        ],
        compiler_params=pltpu.CompilerParams(vmem_limit_bytes=58 * 1024 * 1024),
        name="cast",
    )(gin, gout, gv.reshape(low_glu), gg.reshape(low_glu), block_out, in_grad, tables, gains)
    gin, gout, gv, gg, block_out, in_grad, dec, ang, real, imag, *gains = cast
    return (
        block_out, in_grad, gains[0][0], dec.T, ang.T, real.T, imag.T, gains[1][0], gv, gg, gains[2][0], gin, gout,
    )


def solution(mesh):
    act = P(None, "seq", "chan")
    vec, mat = P("chan"), P("chan", None)
    col = P(None, "chan")
    sizes = (mesh.shape["seq"], mesh.shape["chan"])
    return jax.shard_map(
        functools.partial(per_device, sizes),
        mesh=mesh,
        in_specs=(act, P(), act, vec, mat, mat, mat, mat, vec, col, col, vec, col, mat),
        out_specs=(act, act, vec, mat, mat, mat, mat, vec, col, col, vec, col, mat),
        check_vma=False,
    )
```

```python
import functools

import jax
import jax.numpy as jnp
from jax import lax
from jax.experimental import pallas as pl
from jax.experimental.pallas import tpu as pltpu
from jax.sharding import PartitionSpec as P

epsilon = 1e-05
LANES = 128
MESH = pl.DeviceIdType.MESH
VM = pl.BlockSpec(memory_space=pltpu.VMEM)
ANY = pl.BlockSpec(memory_space=pl.ANY)
GELU_A = 0.7978845608028654
GELU_B = 0.044715
NN = (((1,), (0,)), ((), ()))
NT = (((1,), (1,)), ((), ()))
f32, bf16 = jnp.float32, jnp.bfloat16


def gelu_parts(x):
    inner = GELU_A * (x + GELU_B * (x * x * x))
    t = jnp.tanh(inner)
    half = 0.5 * (1.0 + t)
    slope = half + 0.5 * x * (1.0 - t * t) * (GELU_A * (1.0 + 3.0 * GELU_B * (x * x)))
    return x * half, slope


def dot(a, b, dims=NN):
    return lax.dot_general(a, b, dims, preferred_element_type=f32)


def cmul(ar, ai, br, bi):
    return ar * br - ai * bi, ar * bi + ai * br


def power(re, im, count):
    out = None
    while count:
        if count & 1:
            out = (re, im) if out is None else cmul(*out, re, im)
        re, im = cmul(re, im, re, im)
        count >>= 1
    return out


def row(ref, b, p):
    return jnp.broadcast_to(ref[b, pl.ds(p, 1), :], (8, LANES))


def tile(ref, lead, rows, cols):
    return ref[(*lead, rows, cols)].reshape(-1, 8, LANES)


class Line:
    def __init__(self, own, count, at, send, inward, across, sems, where, hand_over, stores=None):
        self.own, self.count, self.at = own, count, at
        self.send, self.inward, self.across = send, inward, across
        self.sent, self.got = sems
        self.pairs, self.is_end, self.is_mid, self.toward, self.away, self.partner = where
        self.hand_over, self.stores = hand_over, stores

    def copy(self, src, dst, i, sent, got, to):
        return pltpu.make_async_remote_copy(
            src_ref=src, dst_ref=dst, send_sem=self.sent.at[sent, i], recv_sem=self.got.at[got, i],
            device_id=to, device_id_type=MESH,
        )

    def pass_in(self, i):
        self.copy(self.send.at[i], self.inward.at[i], i, 0, 0, self.toward).start()

    def pass_across(self, i):
        self.copy(self.send.at[i], self.across.at[i], i, 0, 1, self.toward).start()

    def pass_out(self, i):
        self.copy(self.at(i), self.at(i), i, 1, 2, self.away).start()

    def pass_pair(self, i):
        self.copy(self.at(i), self.at(i), i, 2, 3, self.partner).start()

    def arrived(self, i, kind):
        self.copy(self.send.at[i], self.send.at[i], i, 0, kind, self.toward).wait_recv()

    def begin(self, i):
        if self.pairs > 2:

            @pl.when(self.is_end)
            def _():
                self.send[i] = self.own(i).astype(self.send.dtype)
                self.pass_in(i)

    def join(self, i):
        if self.pairs == 2:
            self.send[i] = self.own(i).astype(self.send.dtype)
            self.pass_across(i)
            return

        @pl.when(jnp.logical_not(self.is_end))
        def _():
            total = self.own(i)
            self.arrived(i, 0)
            self.send[i] = (total + self.inward[i].astype(f32)).astype(self.send.dtype)
            if self.pairs == 4:
                self.pass_across(i)
                return

            @pl.when(self.is_mid)
            def _():
                self.pass_across(i)

            @pl.when(jnp.logical_not(self.is_mid))
            def _():
                self.pass_in(i)

    def settle(self, i):
        @pl.when(self.is_mid)
        def _():
            self.arrived(i, 1)
            total = self.send[i].astype(f32) + self.across[i].astype(f32)
            self.at(i)[...] = total.astype(self.send.dtype)
            if self.pairs > 2:
                self.pass_out(i)
            if self.hand_over:
                self.pass_pair(i)

    def relay(self, i):
        if self.pairs > 2:

            @pl.when(jnp.logical_not(self.is_mid))
            def _():
                self.arrived(i, 2)
                if self.pairs > 4:

                    @pl.when(jnp.logical_not(self.is_end))
                    def _():
                        self.pass_out(i)

                if self.hand_over:
                    self.pass_pair(i)

    def saves(self, i):
        return [pltpu.make_async_copy(src, dst, sem) for src, dst, sem in self.stores(i)]

    def store(self, i):
        self.arrived(i, 3)
        for save in self.saves(i):
            save.start()

    def finish(self):
        for i in range(self.count):
            if self.stores:
                for save in self.saves(i):
                    save.wait()
            self.copy(self.send.at[i], self.send.at[i], i, 0, 0, self.toward).wait_send()
            if self.pairs > 2:

                @pl.when(jnp.logical_not(self.is_end))
                def _(i=i):
                    self.copy(self.send.at[i], self.send.at[i], i, 1, 2, self.toward).wait_send()

            if self.hand_over:
                done = self.copy(self.send.at[i], self.send.at[i], i, 2, 3, self.toward)
                done.wait_send()


def block_kernel(
    sizes,
    docs, x_ref, og_ref, gain1, dec_ref, ang_ref, real_ref, imag_ref, skip_ref, gluv_hbm, glug_hbm, gain2, win_hbm, wout_hbm,
    block_out, in_grad, tables_out, gains_out, gin_hbm, gout_hbm, gv_hbm, gg_hbm,
    gin_out, gout_out, gv_out, gg_out, gluv, glug, win, wout,
    keep, first_mask, last_mask, valid,
    lam, coef, step_l, factor,
    gain_full, normed1, u_ref, y_ref, edge_sum, init, adj,
    act_full, centred, val, gate, resid, normed2, grad_full, mid_full, hidden_grad, hidden, pre,
    act_t, mid_t, hidden_t, part_own, mid_grad, result_own, resid_grad, value_grad, gate_grad, mixer_grad,
    row_a, row_b, u_rows, keep4, tails, part, states,
    stat_send, stat_recv, rs_send, rs_recv,
    pair_send, pair_recv, line_send, line_recv, back_send, back_low, back_recv,
    table, table2, table_sum, table_send, table_in, table_across,
    gain_all,
    grad2, act2, mid2, act_t2, mid_t2, hidden_t2, pre2, value2, gate2,
    in_send, in_in, in_across, out_send, out_in, out_across, gv_send, gv_in, gv_across, gg_send, gg_in, gg_across,
    load_sem, save_sem, chan_send, chan_recv, seq_send, seq_recv, fac_send, fac_recv, gain_send, gain_recv, line_sent, line_got,
):
    n_seq, n_chan = sizes
    pairs = n_seq // 2
    streams, length, width = x_ref.shape
    n_states = lam.shape[1]
    tokens = streams * length
    full = width * n_chan
    units = win.shape[1]
    group = states.shape[4] * 8
    s, c = lax.axis_index("seq"), lax.axis_index("chan")
    odd = lax.rem(s, 2)
    level = lax.div(s, 2)
    partner = (s + 1 - 2 * odd, c)
    every = pl.ds(0, n_states)
    tiles = width // LANES

    def chan_peer(j):
        return lax.rem(c + j, n_chan)

    def chan_block(k, size):
        return pl.ds(pl.multiple_of(k * size, size), size)

    own_cols = chan_block(c, width)

    barrier = pltpu.get_barrier_semaphore()
    for j in range(1, n_chan):
        pl.semaphore_signal(barrier, inc=1, device_id=(s, chan_peer(j)), device_id_type=MESH)
    for d in range(1, n_seq):
        pl.semaphore_signal(barrier, inc=1, device_id=(lax.rem(s + d, n_seq), c), device_id_type=MESH)

    loads = [
        pltpu.make_async_copy(src, dst, load_sem.at[i])
        for i, (src, dst) in enumerate(
            ((wout_hbm, wout), (gluv_hbm, gluv), (glug_hbm, glug), (win_hbm, win))
        )
    ]
    for load in loads:
        load.start()

    sent = []

    def chan_copy(src, dst, phase, j):
        return pltpu.make_async_remote_copy(
            src_ref=src, dst_ref=dst, send_sem=chan_send.at[phase, j - 1], recv_sem=chan_recv.at[phase, j - 1],
            device_id=(s, chan_peer(j)), device_id_type=MESH,
        )

    def chan_all(pick, phase):
        copies = []
        for j in range(1, n_chan):
            copy = chan_copy(*pick(j), phase, j)
            copy.start()
            copies.append(copy)
        sent.extend(copies)
        return copies

    def landed(copies):
        for copy in copies:
            copy.wait_recv()

    lane = lax.broadcasted_iota(jnp.int32, (tokens, LANES), 1)

    def stats_start(first, second, k, phase):
        packed = jnp.where(lane == 0, first, jnp.where(lane == 1, second, 0.0))
        stat_send[k] = packed.T[:8]
        return chan_all(lambda j: (stat_send.at[k], stat_recv.at[k, j - 1]), phase)

    def stats_end(copies, k):
        landed(copies)
        total = stat_send[k]
        for j in range(1, n_chan):
            total = total + stat_recv[k, j - 1]
        total = jnp.concatenate([total, jnp.zeros((LANES - 8, tokens), f32)], axis=0).T
        return total[:, 0:1] / full, total[:, 1:2] / full

    rows_in = x_ref[...].reshape(tokens, width)
    grad_full[:, own_cols] = og_ref[...].reshape(tokens, width).astype(bf16)
    sum1 = jnp.sum(rows_in, axis=1, keepdims=True)
    square1 = jnp.sum(rows_in * rows_in, axis=1, keepdims=True)
    pl.semaphore_wait(barrier, n_chan + n_seq - 2)
    stat_copies = stats_start(sum1, square1, 0, 0)
    grad_copies = chan_all(lambda j: (grad_full.at[:, own_cols], grad_full.at[:, own_cols]), 1)
    gain_full[:, own_cols] = jnp.broadcast_to(gain2[...], (8, width))
    gain_copies = chan_all(lambda j: (gain_full.at[:, own_cols], gain_full.at[:, own_cols]), 9 + streams * tiles)

    start = s * length
    ends = []
    for b in range(streams):
        total, stream = 0, []
        for k in range(docs.shape[1]):
            total = total + docs[b, k]
            stream.append(total)
        ends.append(stream)

    def passed(b, at):
        count = jnp.int32(0)
        for end in ends[b]:
            count = count + jnp.where(end <= at, 1, 0)
        return count

    def kept(block, b):
        return jnp.where(
            passed(b, block * length - 1) == passed(b, block * length + length - 1), 1.0, 0.0
        )

    pair_flags = [[kept(2 * level + x, b) for b in range(2)] for x in range(2)]

    def line_flag(source):
        both = [kept(2 * source, b) * kept(2 * source + 1, b) for b in range(2)]
        return jnp.where(odd == 1, both[1], both[0])

    line_flags = [[line_flag(level + (d if back else -d)) for d in range(1, pairs)] for back in (False, True)]
    position = lax.broadcasted_iota(jnp.int32, (length, LANES), 0) + start
    for b in range(streams):
        here = jnp.zeros((length, LANES), jnp.int32)
        prior = jnp.zeros((length, LANES), jnp.int32)
        for end in ends[b]:
            here = here + jnp.where(position >= end, 1, 0)
            prior = prior + jnp.where(position > end, 1, 0)
        keep[b] = jnp.where(here == prior, 1.0, 0.0)
        first_mask[b] = jnp.where(here == passed(b, start - 1), 1.0, 0.0)
        last_mask[b] = jnp.where(here == passed(b, start + length - 1), 1.0, 0.0)
        valid[b] = jnp.where(position < ends[b][-1], 1.0, 0.0)

    decay, angle = dec_ref[...], ang_ref[...]
    magnitude = jnp.exp(-decay)
    a2 = angle * angle
    sine, cosine = jnp.ones_like(a2), jnp.ones_like(a2)
    for k in (13, 11, 9, 7, 5, 3):
        sine = 1.0 - sine * a2 * (1.0 / (k * (k - 1)))
    for k in (14, 12, 10, 8, 6, 4, 2):
        cosine = 1.0 - cosine * a2 * (1.0 / (k * (k - 1)))
    lam[0] = magnitude * cosine
    lam[1] = magnitude * (sine * angle)
    twice = 2.0 * decay
    series = jnp.ones_like(twice)
    for k in (9, 8, 7, 6, 5, 4, 3, 2):
        series = 1.0 - series * twice * (1.0 / k)
    factor[...] = jnp.sqrt(twice * series)
    coef[0] = real_ref[...] * factor[...]
    coef[1] = imag_ref[...] * factor[...]
    step_l[0], step_l[1] = power(lam[0], lam[1], length)

    average, square = stats_end(stat_copies, 0)
    scaler1 = lax.rsqrt(square - average * average + epsilon)
    normed1[...] = (rows_in - average) * scaler1
    for b in range(streams):
        rows = slice(b * length, (b + 1) * length)
        for k in range(width // LANES):
            cols = slice(k * LANES, (k + 1) * LANES)
            u_ref[b, :, cols] = normed1[rows, cols] * gain1[:, cols] * valid[b]

    def edges(values, mask, reverse, k):
            cols = pl.ds(k * LANES, LANES)
            row_a[...] = values[:, :, cols] * mask[...]
            for h in range(n_states // group):
                rows = pl.ds(h * group, group)
                l1r, l1i = tile(lam, (0,), rows, cols), tile(lam, (1,), rows, cols)
                l1i = -l1i if reverse else l1i
                l2r, l2i = cmul(l1r, l1i, l1r, l1i)
                l3r, l3i = cmul(l2r, l2i, l1r, l1i)
                l4r, l4i = cmul(l2r, l2i, l2r, l2i)

                def move(i, carry):
                    new = []
                    for b in range(streams):
                        sr, si = carry[2 * b], carry[2 * b + 1]
                        base = length - 4 - 4 * i if reverse else 4 * i
                        u = [row(row_a, b, base + (3 - j if reverse else j)) for j in range(4)]
                        nr = (l4r * sr - l4i * si) + (l3r * u[0] + l2r * u[1]) + (l1r * u[2] + u[3])
                        ni = (l4r * si + l4i * sr) + (l3i * u[0] + l2i * u[1]) + l1i * u[2]
                        new += [nr, ni]
                    return tuple(new)

                zero = jnp.zeros((group // 8, 8, LANES), f32)
                final = lax.fori_loop(0, length // 4, move, (zero,) * (2 * streams))
                cr, ci = tile(coef, (0,), rows, cols), tile(coef, (1,), rows, cols)
                for b in range(streams):
                    fr, fi = final[2 * b], final[2 * b + 1]
                    if reverse:
                        fr, fi = cmul(cr, -ci, fr, fi)
                    edge_sum[k, b, 0, rows] = fr.reshape(-1, LANES)
                    edge_sum[k, b, 1, rows] = fi.reshape(-1, LANES)

    class Carry:
        def __init__(self, target, which, reverse, k):
            self.target, self.which, self.reverse, self.k = target, which, reverse, k
            cols = pl.ds(k * LANES, LANES)
            self.sr = step_l[0, :, cols]
            self.si = -step_l[1, :, cols] if reverse else step_l[1, :, cols]
            self.leads = odd == (1 if reverse else 0)

        def copy(self, src, dst, i, to):
            return pltpu.make_async_remote_copy(
                src_ref=src.at[self.which, self.k], dst_ref=dst, send_sem=seq_send.at[self.which, self.k, i],
                recv_sem=seq_recv.at[self.which, self.k, i], device_id=to, device_id_type=MESH,
            )

        def advance(self, flag, vr, vi, ur, ui):
            r, i = cmul(ur, ui, vr, vi)
            return r * flag, i * flag

        def start(self):
            at = (self.which, self.k)
            pair_send[at] = edge_sum[self.k].astype(bf16)
            self.across = self.copy(pair_send, pair_recv.at[at], 0, partner)
            self.across.start()

        def line(self):
            at = (self.which, self.k)
            self.across.wait_recv()
            mine_r, mine_i = edge_sum[self.k, odd, 0], edge_sum[self.k, odd, 1]
            other_r, other_i = pair_recv[(*at, odd, 0)].astype(f32), pair_recv[(*at, odd, 1)].astype(f32)
            flag = jnp.where(odd == 1, *[pair_flags[0 if self.reverse else 1][b] for b in (1, 0)])
            lr, li = jnp.where(self.leads, mine_r, other_r), jnp.where(self.leads, mine_i, other_i)
            tr, ti = jnp.where(self.leads, other_r, mine_r), jnp.where(self.leads, other_i, mine_i)
            ar, ai = self.advance(flag, lr, li, self.sr, self.si)
            line_send[(*at, 0)] = (ar + tr).astype(bf16)
            line_send[(*at, 1)] = (ai + ti).astype(bf16)
            for d in range(1, pairs):
                to = level - d if self.reverse else level + d

                @pl.when(to >= 0 if self.reverse else to < pairs)
                def _(d=d, to=to):
                    self.onward(d, (2 * to + odd, c)).start()

        def onward(self, d, to=partner):
            return self.copy(line_send, line_recv.at[self.which, self.k, d - 1], 1 + d, to)

        def home(self):
            at = (self.which, self.k)
            dr, di = cmul(self.sr, self.si, self.sr, self.si)
            back_send[...] = jnp.zeros(back_send.shape, f32)
            for d in range(pairs - 1, 0, -1):
                source = level + d if self.reverse else level - d

                @pl.when(source < pairs if self.reverse else source >= 0)
                def _(d=d):
                    self.onward(d).wait_recv()
                    flag = line_flags[self.reverse][d - 1]
                    vr, vi = self.advance(flag, back_send[0], back_send[1], dr, di)
                    back_send[0] = vr + line_recv[(*at, d - 1, 0)].astype(f32)
                    back_send[1] = vi + line_recv[(*at, d - 1, 1)].astype(f32)

            back_low[at] = back_send[...].astype(bf16)
            self.back = self.copy(back_low, back_recv.at[at], 1, partner)
            self.back.start()

        def end(self):
            at = (self.which, self.k)
            cols = pl.ds(self.k * LANES, LANES)
            self.back.wait_recv()
            for b in range(streams):
                flag = pair_flags[1 if self.reverse else 0][b]
                near = [
                    jnp.where(odd == b, back_low[(*at, i)], back_recv[(*at, i)]).astype(f32) for i in range(2)
                ]
                far = self.advance(flag, *near, self.sr, self.si)
                for i in range(2):
                    other = far[i] + pair_recv[(*at, b, i)].astype(f32)
                    self.target[b, i, :, cols] = jnp.where(self.leads, near[i], other)

        def finish(self):
            self.across.wait_send()
            self.back.wait_send()

            for d in range(1, pairs):
                to = level - d if self.reverse else level + d

                @pl.when(to >= 0 if self.reverse else to < pairs)
                def _(d=d):
                    self.onward(d).wait_send()

    low_side = level < pairs // 2
    toward = (s + jnp.where(low_side, 2, -2), c)
    away = (s + jnp.where(low_side, -2, 2), c)
    where = (
        pairs,
        jnp.logical_or(level == 0, level == pairs - 1),
        jnp.logical_or(level == pairs // 2 - 1, level == pairs // 2),
        toward, away, partner,
    )
    factors = []

    def swap_factor(src, dst, k, to=partner):
        copy = pltpu.make_async_remote_copy(
            src_ref=src, dst_ref=dst, send_sem=fac_send.at[k], recv_sem=fac_recv.at[k], device_id=to, device_id_type=MESH
        )
        copy.start()
        factors.append(copy)
        return copy

    half_units = units // 2
    my_half = chan_block(odd, half_units)
    their_half = chan_block(1 - odd, half_units)
    wanted = {}

    def need(*names):
        for name in names:
            wanted[name].wait_recv()

    in_rows, in_cols = full // 4, units // 4
    out_rows, out_cols = units // 4, full // 4
    glu_rows, glu_half = full // 4, width // 2
    my_glu, their_glu = chan_block(odd, glu_half), chan_block(1 - odd, glu_half)

    ready = []

    def in_own(i):
        assert "mid" in ready
        if i == 0:
            need("pre")
        rows, cols = pl.ds((i // 2) * in_rows, in_rows), (i % 2) * in_cols
        mine = pl.ds(pl.multiple_of(odd * half_units + cols, in_cols), in_cols)
        return dot(mid_t[rows, :], pre[:, mine]) + dot(mid_t2[rows, :], pre2[:, pl.ds(cols, in_cols)])

    def in_at(i):
        return gin_out.at[odd, i // 2, i % 2]

    def out_own(i):
        if i == 0:
            need("grad", ("hidden", 0))
        if i == 4:
            need(("hidden", 1))
        rows, cols = (i // 4) * out_rows, pl.ds((i % 4) * out_cols, out_cols)
        mine = pl.ds(pl.multiple_of(odd * half_units + rows, out_rows), out_rows)
        return dot(hidden_t[mine, :], grad_full[:, cols]) + dot(hidden_t2[pl.ds(rows, out_rows), :], grad2[:, cols])

    def out_at(i):
        return gout_out.at[odd, i // 4, i % 4]

    def glu_own(near, far, names):
        def own(i):
            if i == 0:
                need(*names)
            assert "act" in ready
            rows = pl.ds(i * glu_rows, glu_rows)
            return dot(act_t[rows, :], near[:, my_glu]) + dot(act_t2[rows, :], far[...])

        return own

    def glu_at(out):
        def at(i):
            return out.at[odd, i]

        return at

    def table_own(q):
        need(("table", q))
        return table[q] + table2[q]

    sem_at = [0]

    def line(own, count, at, bufs, hand_over, kept_at=None):
        spot, base = pl.ds(sem_at[0], count), sem_at[0]
        stores = None
        if kept_at:
            held, final, place = kept_at

            def stores(i):
                return [(held.at[(x, *place(i))], final.at[(x, *place(i))], save_sem.at[x, base + i]) for x in range(2)]

        sem_at[0] += count
        return Line(own, count, at, *bufs, (line_sent.at[:, spot], line_got.at[:, spot]), where, hand_over, stores)

    quarters = (width // LANES) * (n_states // group)
    in_line = line(in_own, 8, in_at, (in_send, in_in, in_across), True, (gin_out, gin_hbm, lambda i: (i // 2, i % 2)))
    out_line = line(out_own, 8, out_at, (out_send, out_in, out_across), True, (gout_out, gout_hbm, lambda i: (i // 4, i % 4)))
    gv_line = line(glu_own(value_grad, value2, ("value",)), 4, glu_at(gv_out), (gv_send, gv_in, gv_across), True, (gv_out, gv_hbm, lambda i: (i,)))
    gg_line = line(glu_own(gate_grad, gate2, ("gate",)), 4, glu_at(gg_out), (gg_send, gg_in, gg_across), True, (gg_out, gg_hbm, lambda i: (i,)))
    table_line = line(table_own, quarters, lambda q: table_sum.at[q], (table_send, table_in, table_across), False)
    lines = [out_line, gv_line, in_line, gg_line, table_line]
    pieces = [(entry, i) for entry in lines[:4] for i in range(entry.count)]
    tick, begun = [0], [0]
    MID, LAST, STORE = 2, 4, 8

    def launch(count):
        for _ in range(count):
            if begun[0] < len(pieces):
                entry, i = pieces[begun[0]]
                entry.begin(i)
            begun[0] += 1

    def pump(count, lead=4):
        for _ in range(count):
            t = tick[0]
            tick[0] += 1
            launch(t + 1 + lead - begun[0])
            for ahead, act in ((0, "join"), (-MID, "settle"), (-LAST, "relay"), (-STORE, "store")):
                if 0 <= t + ahead < len(pieces):
                    entry, i = pieces[t + ahead]
                    getattr(entry, act)(i)

    forward = [Carry(init, 0, False, k) for k in range(tiles)]
    for k in range(tiles):
        edges(u_ref, last_mask, False, k)
        forward[k].start()
    unit_block = min(units, 256)

    def hidden_grad_part(i):
        cols = pl.ds(i * unit_block, unit_block)
        hidden_grad[:, cols] = dot(grad_full[...], wout[cols, :], NT)

    loads[0].wait()
    landed(grad_copies)
    blocks = units // unit_block
    for k in range(blocks // 2):
        hidden_grad_part(k)
    for k in range(tiles):
        forward[k].line()
    for k in range(blocks // 2, blocks):
        hidden_grad_part(k)
    for k in range(tiles):
        forward[k].home()
    wanted["grad"] = swap_factor(grad_full, grad2, 0)
    act_copies = []
    for k in range(tiles):
        forward[k].end()
        cols = pl.ds(k * LANES, LANES)
        u_rows[k] = u_ref[:, :, cols]
        near = [jnp.sum(coef[0, :, cols], axis=0, keepdims=True)]
        qr, qi = coef[0, :, cols], coef[1, :, cols]
        for _ in range(3):
            qr, qi = cmul(qr, qi, lam[0, :, cols], lam[1, :, cols])
            near.append(jnp.sum(qr, axis=0, keepdims=True))
        fours = length // 4
        local, through = [], []
        for b in range(streams):
            us = [u_rows[k, b, pl.ds(j, fours, stride=4), :] for j in range(4)]
            ks = [keep[b, pl.ds(j, fours, stride=4), :] for j in range(4)]
            reach = ks[0]
            passed_by = [reach]
            for j in range(1, 4):
                reach = reach * ks[j]
                passed_by.append(reach)
            through.append(passed_by)
            keep4[b] = reach
            terms, outs = [], []
            for j in range(4):
                terms = [term * ks[j] for term in terms] + [us[j]]
                out = skip_ref[:, cols] * us[j]
                for i, term in enumerate(terms):
                    out = out + near[j - i] * term
                outs.append(out)
            local.append(outs)
            for j in range(4):
                tails[b, j] = terms[j]
        for h in range(n_states // group):
            rows = pl.ds(h * group, group)
            l1r, l1i = tile(lam, (0,), rows, cols), tile(lam, (1,), rows, cols)
            l2r, l2i = cmul(l1r, l1i, l1r, l1i)
            l3r, l3i = cmul(l2r, l2i, l1r, l1i)
            l4r, l4i = cmul(l2r, l2i, l2r, l2i)
            cr, ci = tile(coef, (0,), rows, cols), tile(coef, (1,), rows, cols)
            taps = [cmul(cr, ci, *power_of) for power_of in ((l1r, l1i), (l2r, l2i), (l3r, l3i), (l4r, l4i))]

            def move(i, carry, h=h, l1=(l1r, l1i), l2=(l2r, l2i), l3=(l3r, l3i), l4=(l4r, l4i), taps=taps):
                new = []
                for b in range(streams):
                    sr, si = carry[2 * b], carry[2 * b + 1]
                    for j in range(4):
                        spot = pl.ds(pl.multiple_of(((b * 4 + j) * fours + i) * 8, 8), 8)
                        out = (taps[j][0] * sr - taps[j][1] * si).sum(0)
                        if h == 0:
                            part[spot, :] = out
                        else:
                            part[spot, :] += out
                    m = row(keep4, b, i)
                    t = [row(tails.at[b], j, i) for j in range(4)]
                    sr = sr * m
                    si = si * m
                    nr = (l4[0] * sr - l4[1] * si) + (l3[0] * t[0] + l2[0] * t[1]) + (l1[0] * t[2] + t[3])
                    ni = (l4[0] * si + l4[1] * sr) + (l3[1] * t[0] + l2[1] * t[1]) + l1[1] * t[2]
                    new += [nr, ni]
                return tuple(new)

            begin = []
            for b in range(streams):
                begin += [tile(init, (b, 0), rows, cols), tile(init, (b, 1), rows, cols)]
            lax.fori_loop(0, fours, move, tuple(begin))
        for b in range(streams):
            for j in range(4):
                first = (b * 4 + j) * fours * 8
                total = part[pl.ds(first, fours, stride=8), :]
                for i in range(1, 8):
                    total = total + part[pl.ds(first + i, fours, stride=8), :]
                row_a[b, pl.ds(j, fours, stride=4), :] = through[b][j] * total + local[b][j]
            y = row_a[b]
            y_ref[b, :, cols] = y
            to = pl.ds(pl.multiple_of(c * width + k * LANES, LANES), LANES)
            here = pl.ds(b * length, length)
            act_full[here, to] = gelu_parts(y)[0].astype(bf16)
            act_copies.append(
                chan_all(lambda j: (act_full.at[here, to], act_full.at[here, to]), 2 + streams * k + b)
            )
    base = 2 + streams * tiles

    def again_pass(q):
        k, h = q // (n_states // group), q % (n_states // group)
        rows, cols = pl.ds(h * group, group), pl.ds(k * LANES, LANES)
        lr, li = tile(lam, (0,), rows, cols), tile(lam, (1,), rows, cols)
        held = states.at[q % 2]

        def again(p, carry):
            new = []
            for b in range(streams):
                sr, si = carry[2 * b], carry[2 * b + 1]
                u = row(u_rows.at[k], b, p)
                m = row(keep, b, p)
                sr = sr * m
                si = si * m
                nr = (lr * sr - li * si) + u
                ni = lr * si + li * sr
                held[p + 1, b, 0] = nr
                held[p + 1, b, 1] = ni
                new += [nr, ni]
            return tuple(new)

        begin = []
        for b in range(streams):
            begin += [tile(init, (b, 0), rows, cols), tile(init, (b, 1), rows, cols)]
            held[0, b, 0] = begin[-2]
            held[0, b, 1] = begin[-1]
        lax.fori_loop(0, length, again, tuple(begin), unroll=2)

    loads[1].wait()
    loads[2].wait()
    for copies in act_copies:
        landed(copies)
    beside = (s, c + 1 - 2 * lax.rem(c, 2))
    core_half = chan_block(lax.rem(c, 2), tokens // 2)
    wanted["act_near"] = swap_factor(act_full.at[core_half, :], act2.at[core_half, :], 1)
    val[...] = dot(act_full[...], gluv[...])
    gate[...] = jax.nn.sigmoid(dot(act_full[...], glug[...]))
    resid[...] = rows_in_of(x_ref, tokens, width) + val[...] * gate[...]

    sum2 = jnp.sum(resid[...], axis=1, keepdims=True)
    square2 = jnp.sum(resid[...] * resid[...], axis=1, keepdims=True)
    centred[:, own_cols] = (resid[...] - sum2 / width).astype(bf16)
    stat_copies = stats_start(sum2, square2, 1, base)
    mid_copies = chan_all(lambda j: (centred.at[:, own_cols], centred.at[:, own_cols]), base + 1)
    landed(gain_copies)
    landed(stat_copies)
    shares = [stat_send[1], *[stat_recv[1, j - 1] for j in range(1, n_chan)]]
    shares = jnp.concatenate([*shares, jnp.zeros((LANES - 8 * n_chan, tokens), f32)], axis=0).T
    average, square = 0.0, 0.0
    for j in range(n_chan):
        average = average + shares[:, 8 * j : 8 * j + 1] / full
        square = square + shares[:, 8 * j + 1 : 8 * j + 2] / full
    scaler2 = lax.rsqrt(square - average * average + epsilon)
    normed2[...] = (resid[...] - average) * scaler2
    mid_full[:, own_cols] = (normed2[...] * gain2[...]).astype(bf16)
    landed(mid_copies)
    for j in range(1, n_chan):
        cols = chan_block(lax.rem(c - j + n_chan, n_chan), width)
        shift = shares[:, 8 * j : 8 * j + 1] / width - average
        mid_full[:, cols] = ((centred[:, cols].astype(f32) + shift) * scaler2 * gain_full[0:1, cols]).astype(bf16)
    loads[3].wait()

    for k in range(4):
        cols = pl.ds(k * out_rows, out_rows)
        value, slope = gelu_parts(dot(mid_full[...], win[:, cols]))
        hidden[:, cols] = value.astype(bf16)
        pre[:, cols] = (hidden_grad[:, cols] * slope).astype(bf16)
        hidden_t[cols, :] = hidden[:, cols].T
    for k in range(2):
        theirs = pl.ds(pl.multiple_of((1 - odd) * half_units + k * out_rows, out_rows), out_rows)
        wanted["hidden", k] = swap_factor(
            hidden_t.at[theirs, :], hidden_t2.at[pl.ds(k * out_rows, out_rows), :], 4 if k == 0 else 10 + quarters
        )

    def scatter_fill(piece, own, k):
        for j in range(1, n_chan):
            rs_send[k, j - 1] = piece(chan_block(chan_peer(j), width)).astype(bf16)
        own[...] = piece(own_cols)

    def scatter_start(k, phase):
        return chan_all(lambda j: (rs_send.at[k, j - 1], rs_recv.at[k, j - 1]), phase)

    def transposed(source, target, count):
        for k in range(count):
            target[pl.ds(k * width, width), :] = source[:, k * width : (k + 1) * width].T

    def scatter_end(copies, own, k):
        landed(copies)
        total = own[...]
        for j in range(1, n_chan):
            total = total + rs_recv[k, j - 1].astype(f32)
        return total

    scatter_fill(lambda rows: dot(pre[...], win[rows, :], NT), part_own, 0)
    grad_parts = scatter_start(0, base + 2)
    first, second = 0.0, 0.0
    for j in range(n_chan):
        cols = chan_block(chan_peer(j), width) if j else own_cols
        values = rs_send[0, j - 1].astype(f32) if j else part_own[...]
        first = first + jnp.sum(values * gain_full[0:1, cols], axis=1, keepdims=True)
        second = second + jnp.sum(values * mid_full[:, cols].astype(f32), axis=1, keepdims=True)
    stat_copies = stats_start(first, second, 2, base + 4)
    scatter_fill(lambda cols: dot(hidden[...], wout[:, cols]), result_own, 1)
    transposed(act_full, act_t, n_chan)
    transposed(mid_full, mid_t, n_chan)
    wanted["act_near"].wait_recv()
    wanted["act_far"] = swap_factor(act2.at[core_half, :], act2.at[core_half, :], 9, beside)
    for q in range(min(2, quarters)):
        again_pass(q)
    launch(4)
    mid_grad[...] = scatter_end(grad_parts, part_own, 0)
    wanted["pre"] = swap_factor(pre.at[:, their_half], pre2, 5)
    gains = jnp.sum(mid_grad[...] * normed2[...], axis=0, keepdims=True)
    first, second = stats_end(stat_copies, 2)
    resid_grad[...] = og_ref[...].reshape(tokens, width) + scaler2 * (
        mid_grad[...] * gain2[...] - first - normed2[...] * second
    )

    value_grad[...] = (resid_grad[...] * gate[...]).astype(bf16)
    gate_grad[...] = (resid_grad[...] * val[...] * gate[...] * (1.0 - gate[...])).astype(bf16)
    scatter_fill(
        lambda rows: dot(value_grad[...], gluv[rows, :], NT) + dot(gate_grad[...], glug[rows, :], NT), val, 2
    )
    act_parts = scatter_start(2, base + 5)
    wanted["value"] = swap_factor(value_grad.at[:, their_glu], value2, 6)
    wanted["gate"] = swap_factor(gate_grad.at[:, their_glu], gate2, 7)
    pump(2, 2)
    act_grad = scatter_end(act_parts, val, 2)
    mixer_grad[...] = act_grad.reshape(streams, length, width) * gelu_parts(y_ref[...])[1]

    out_parts = scatter_start(1, base + 3)

    backward = [Carry(adj, 1, True, k) for k in range(tiles)]
    for k in range(tiles):
        edges(mixer_grad, first_mask, True, k)
        backward[k].start()
        if k == 0:
            pump(1, 2)
    pump(1, 2)
    for k in range(tiles):
        backward[k].line()
    wanted["mid_near"] = swap_factor(mid_full.at[core_half, :], mid2.at[core_half, :], 2)
    pump(1, 2)
    total = scatter_end(out_parts, result_own, 1)
    block_out[...] = (resid[...] + total).reshape(streams, length, width)
    for k in range(tiles):
        backward[k].home()
    need("act_far")
    transposed(act2, act_t2, n_chan)
    ready.append("act")
    pump(2)
    zero = jnp.zeros((group // 8, 8, LANES), f32)
    q = 0
    for k in range(width // LANES):
        backward[k].end()
        cols = pl.ds(k * LANES, LANES)
        row_b[...] = mixer_grad[:, :, cols]
        for h in range(n_states // group):
            rows = pl.ds(h * group, group)
            lr, li = tile(lam, (0,), rows, cols), tile(lam, (1,), rows, cols)
            cr, ci = tile(coef, (0,), rows, cols), tile(coef, (1,), rows, cols)

            if q > 1:
                again_pass(q)
            pump(2, 3 if q == 0 else 4)
            if q == 0:
                wanted["mid_near"].wait_recv()
                wanted["mid_far"] = swap_factor(mid2.at[core_half, :], mid2.at[core_half, :], 3, beside)
            if q > 0:
                table_line.begin(q - 1)
            if q > 1:
                table_line.settle(q - 2)
            held = states.at[q % 2]

            def back(i, carry, h=h, held=held, lr=lr, li=li, cr=cr, ci=ci):
                glr, gli, gcr, gci = carry[:4]
                adjoint = carry[4:]
                p = length - 1 - i
                new = []
                for b in range(streams):
                    ar, ai = adjoint[2 * b], adjoint[2 * b + 1]
                    g = row(row_b, b, p)
                    m = row(keep, b, p)
                    nr = (lr * ar + li * ai) + cr * g
                    ni = (lr * ai - li * ar) - ci * g
                    spot = pl.ds(pl.multiple_of((b * length + p) * 8, 8), 8)
                    if h == 0:
                        part[spot, :] = nr.sum(0)
                    else:
                        part[spot, :] += nr.sum(0)
                    gcr = gcr + g * held[p + 1, b, 0]
                    gci = gci - g * held[p + 1, b, 1]
                    nr = nr * m
                    ni = ni * m
                    sr, si = held[p, b, 0], held[p, b, 1]
                    glr = glr + (nr * sr + ni * si)
                    gli = gli + (ni * sr - nr * si)
                    new += [nr, ni]
                return (glr, gli, gcr, gci, *new)

            begin = []
            for b in range(streams):
                begin += [tile(adj, (b, 0), rows, cols), tile(adj, (b, 1), rows, cols)]
            sums = lax.fori_loop(0, length, back, (zero, zero, zero, zero, *begin))
            glr, gli, gcr, gci = [item.reshape(-1, LANES) for item in sums[:4]]
            share = factor[rows, cols]
            ratio = (1.0 - share * share) / share
            spots = [pl.ds(i * group, group) for i in range(4)]
            table[q, spots[0], :] = (gcr * real_ref[rows, cols] + gci * imag_ref[rows, cols]) * ratio - (
                glr * lam[0, rows, cols] + gli * lam[1, rows, cols]
            )
            table[q, spots[1], :] = gli * lam[0, rows, cols] - glr * lam[1, rows, cols]
            table[q, spots[2], :] = share * gcr
            table[q, spots[3], :] = share * gci
            wanted["table", q] = swap_factor(table.at[q], table2.at[q], 10 + q)
            if q == 0:
                need("mid_far")
                transposed(mid2, mid_t2, n_chan)
                ready.append("mid")
            pump(2)
            if q > 0:
                table_line.join(q - 1)
            if q > 1:
                table_line.relay(q - 2)
            q += 1
        for b in range(streams):
            total = part[pl.ds(b * length * 8, length, stride=8), :]
            for j in range(1, 8):
                total = total + part[pl.ds(b * length * 8 + j, length, stride=8), :]
            u_grad = total + skip_ref[:, cols] * row_b[b]
            part_own[b * length : (b + 1) * length, cols] = u_grad * valid[b]

    last = quarters - 1
    pump(1)
    table_line.begin(last)
    if last > 0:
        table_line.settle(last - 1)
    scaled = part_own[...] * gain1[...]
    stat_copies = stats_start(
        jnp.sum(scaled, axis=1, keepdims=True),
        jnp.sum(scaled * normed1[...], axis=1, keepdims=True), 3, base + 6,
    )
    gain_rows = [
        jnp.sum(part_own[...] * normed1[...], axis=0, keepdims=True),
        jnp.sum(jnp.sum(mixer_grad[...] * u_ref[...], axis=0), axis=0, keepdims=True),
        gains,
    ]
    gain_all[s] = jnp.concatenate([*gain_rows, jnp.zeros((5, width), f32)], axis=0)
    for d in range(1, n_seq):
        copy = pltpu.make_async_remote_copy(
            src_ref=gain_all.at[s], dst_ref=gain_all.at[s], send_sem=gain_send.at[d], recv_sem=gain_recv.at[s],
            device_id=(lax.rem(s + d, n_seq), c), device_id_type=MESH,
        )
        copy.start()
        sent.append(copy)
    pump(1)
    first, second = stats_end(stat_copies, 3)
    in_grad[...] = (
        resid_grad[...] + scaler1 * (part_own[...] * gain1[...] - first - normed1[...] * second)
    ).reshape(streams, length, width)
    table_line.join(last)
    if last > 0:
        table_line.relay(last - 1)
    pump(1)
    table_line.settle(last)
    pump(2)
    table_line.relay(last)
    while tick[0] < len(pieces) + STORE:
        pump(1)
    for k in range(width // LANES):
        for h in range(n_states // group):
            for i in range(4):
                tables_out[i, h * group : (h + 1) * group, k * LANES : (k + 1) * LANES] = table_sum[
                    k * (n_states // group) + h, i * group : (i + 1) * group, :
                ]
    for d in range(1, n_seq):
        source = lax.rem(s + d, n_seq)
        pltpu.make_async_remote_copy(
            src_ref=gain_all.at[s], dst_ref=gain_all.at[source], send_sem=gain_send.at[d], recv_sem=gain_recv.at[source],
            device_id=(source, c), device_id_type=MESH,
        ).wait_recv()
    total = gain_all[0]
    for k in range(1, n_seq):
        total = total + gain_all[k]
    gains_out[...] = total
    for entry in lines:
        entry.finish()
    for copy in factors:
        copy.wait_send()
    for copy in sent:
        copy.wait_send()
    for carry in (*forward, *backward):
        carry.finish()


def rows_in_of(ref, tokens, width):
    return ref[...].reshape(tokens, width)


def cast_kernel(
    steps, gin, gout, gv, gg, block, grad, tables, gains,
    gin_hbm, gout_hbm, gv_hbm, gg_hbm, block_out, grad_out, dec_out, ang_out, real_out, imag_out, gain_a, gain_b, gain_c,
    gin_low, gout_low, gv_low, gg_low, gin_out, gout_out, gv_out, gg_out, table_low, gain_low, block_low, grad_low, load_sem, save_sem, small_sem,
):
    whole = [
        pltpu.make_async_copy(src, dst, small_sem.at[i])
        for i, (src, dst) in enumerate(
            [(tables, table_low), (gains, gain_low), (block, block_low), (grad, grad_low)]
        )
    ]
    full, units = gin_out.shape
    rows, tall = full // steps, units // steps
    loads, saves = [], []
    for p in range(steps):
        here, tall_here = pl.ds(p * rows, rows), pl.ds(p * tall, tall)
        loads.append(
            [
                pltpu.make_async_copy(gin.at[:, p], gin_low.at[:, p], load_sem.at[0, p]),
                pltpu.make_async_copy(gout.at[p // 2, p % 2], gout_low.at[p // 2, p % 2], load_sem.at[1, p]),
                pltpu.make_async_copy(gv.at[:, p], gv_low.at[:, p], load_sem.at[2, p]),
                pltpu.make_async_copy(gg.at[:, p], gg_low.at[:, p], load_sem.at[3, p]),
            ]
        )
        saves.append(
            [
                pltpu.make_async_copy(gin_out.at[here], gin_hbm.at[here], save_sem.at[0, p]),
                pltpu.make_async_copy(gout_out.at[tall_here], gout_hbm.at[tall_here], save_sem.at[1, p]),
                pltpu.make_async_copy(gv_out.at[here], gv_hbm.at[here], save_sem.at[2, p]),
                pltpu.make_async_copy(gg_out.at[here], gg_hbm.at[here], save_sem.at[3, p]),
            ]
        )
    for copies in loads:
        for copy in copies:
            copy.start()
    for copy in whole:
        copy.start()
    for p in range(steps):
        here, tall_here = slice(p * rows, (p + 1) * rows), slice(p * tall, (p + 1) * tall)
        for copy in loads[p]:
            copy.wait()
        for i in range(4):
            cols = slice(i * tall, (i + 1) * tall)
            gin_out[here, cols] = gin_low[i // 2, p, i % 2].astype(f32)
        for i in range(4):
            cols = slice(i * rows, (i + 1) * rows)
            gout_out[tall_here, cols] = gout_low[p // 2, p % 2, i].astype(f32)
        for x in range(2):
            cols = slice(x * gv.shape[-1], (x + 1) * gv.shape[-1])
            gv_out[here, cols] = gv_low[x, p].astype(f32)
            gg_out[here, cols] = gg_low[x, p].astype(f32)
        for copy in saves[p]:
            copy.start()
    for copy in whole:
        copy.wait()
    passed_on = [
        pltpu.make_async_copy(block_low, block_out, small_sem.at[4]),
        pltpu.make_async_copy(grad_low, grad_out, small_sem.at[5]),
    ]
    for copy in passed_on:
        copy.start()
    for k, out in enumerate((dec_out, ang_out, real_out, imag_out)):
        out[...] = table_low[k]
    for k, out in enumerate((gain_a, gain_b, gain_c)):
        out[...] = gain_low[k : k + 1, :]
    for copies in (*saves, passed_on):
        for copy in copies:
            copy.wait()


def per_device(
    sizes, block_in, doc_lengths, out_grad, first_gain, decay_rate, turn_angle, out_real, out_imag,
    skip_gain, glu_value, glu_gate, second_gain, ffn_in, ffn_out,
):
    n_seq, n_chan = sizes
    pairs = n_seq // 2
    streams, length, width = block_in.shape
    n_states = decay_rate.shape[1]
    tokens = streams * length
    full = width * n_chan
    units = ffn_in.shape[1]
    glu_cols = glu_value.shape[1]
    group = min(32, n_states)
    like = jax.ShapeDtypeStruct
    quarters = (width // LANES) * (n_states // group)
    phases = 10 + streams * (width // LANES)
    act = (streams, length, width)
    flat = (tokens, width)
    mask = (streams, length, LANES)
    tab, lane_tab = (2, n_states, width), (2, n_states, LANES)
    tiles = width // LANES
    V = pltpu.VMEM
    scratch = [
        V((2, 4, 2, full // 4, units // 4), bf16), V((2, 2, 4, units // 4, full // 4), bf16), *[V((2, 4, full // 4, glu_cols // 2), bf16)] * 2,
        V((full, glu_cols), bf16), V((full, glu_cols), bf16), V((full, units), bf16), V((units, full), bf16),
        V(mask, f32), V(mask, f32), V(mask, f32), V(mask, f32),
        V(tab, f32), V(tab, f32), V(tab, f32), V((n_states, width), f32),
        V((8, full), f32), V(flat, f32), V(act, f32), V(act, f32), V((tiles, streams, 2, n_states, LANES), f32), V((streams, *tab), f32), V((streams, *tab), f32),
        V((tokens, full), bf16), V((tokens, full), bf16), V((tokens, glu_cols), f32), V((tokens, glu_cols), f32), V(flat, f32), V(flat, f32),
        V((tokens, full), bf16), V((tokens, full), bf16), V((tokens, units), f32), V((tokens, units), bf16), V((tokens, units), bf16),
        V((full, tokens), bf16), V((full, tokens), bf16), V((units, tokens), bf16),
        V(flat, f32), V(flat, f32), V(flat, f32), V(flat, f32), V((tokens, glu_cols), bf16), V((tokens, glu_cols), bf16),
        V(act, f32),
        V(mask, f32), V(mask, f32), V((tiles, *mask), f32), V((streams, length // 4, LANES), f32), V((streams, 4, length // 4, LANES), f32), V((tokens * 8, LANES), f32), V((2, length + 1, streams, 2, group // 8, 8, LANES), f32),
        V((4, 8, tokens), f32), V((4, n_chan - 1, 8, tokens), f32), V((3, n_chan - 1, *flat), bf16), V((3, n_chan - 1, *flat), bf16),
        *[V((2, tiles, streams, *lane_tab), bf16)] * 2, V((2, tiles, *lane_tab), bf16), V((2, tiles, pairs - 1, *lane_tab), bf16),
        V(lane_tab, f32), *[V((2, tiles, *lane_tab), bf16)] * 2,
        *[V((quarters, 4 * group, LANES), f32)] * 6,
        V((n_seq, 8, width), f32),
        *[V((tokens, full), bf16)] * 3, V((full, tokens), bf16), V((full, tokens), bf16), V((units // 2, tokens), bf16),
        V((tokens, units // 2), bf16), V((tokens, glu_cols // 2), bf16), V((tokens, glu_cols // 2), bf16),
        *[V((8, full // 4, units // 4), bf16)] * 3, *[V((8, units // 4, full // 4), bf16)] * 3,
        *[V((4, full // 4, glu_cols // 2), bf16)] * 6,
        pltpu.SemaphoreType.DMA((4,)), pltpu.SemaphoreType.DMA((2, 24)),
        pltpu.SemaphoreType.DMA((phases, n_chan - 1)), pltpu.SemaphoreType.DMA((phases, n_chan - 1)),
        pltpu.SemaphoreType.DMA((2, tiles, pairs + 1)), pltpu.SemaphoreType.DMA((2, tiles, pairs + 1)),
        pltpu.SemaphoreType.DMA((11 + quarters,)), pltpu.SemaphoreType.DMA((11 + quarters,)),
        pltpu.SemaphoreType.DMA((n_seq,)), pltpu.SemaphoreType.DMA((n_seq,)),
        pltpu.SemaphoreType.DMA((3, 25 + quarters)), pltpu.SemaphoreType.DMA((4, 25 + quarters)),
    ]
    specs = [pl.BlockSpec(memory_space=pltpu.SMEM)] + [VM] * 8 + [ANY, ANY, VM, ANY, ANY]
    made = pl.pallas_call(
        functools.partial(block_kernel, sizes),
        out_shape=(
            like(act, f32), like(act, f32), like((4, n_states, width), f32), like((8, width), f32),
            like((2, 4, 2, full // 4, units // 4), bf16), like((2, 2, 4, units // 4, full // 4), bf16),
            like((2, 4, full // 4, glu_cols // 2), bf16), like((2, 4, full // 4, glu_cols // 2), bf16),
        ),
        in_specs=specs,
        out_specs=(VM,) * 4 + (ANY,) * 4,
        scratch_shapes=scratch,
        compiler_params=pltpu.CompilerParams(
            collective_id=0, has_side_effects=True, vmem_limit_bytes=60 * 1024 * 1024
        ),
        name="block",
    )(
        doc_lengths, block_in, out_grad, first_gain[None], decay_rate.T, turn_angle.T, out_real.T, out_imag.T, skip_gain[None],
        glu_value, glu_gate, second_gain[None], ffn_in, ffn_out,
    )
    block_out, in_grad, tables, gains, gin, gout, gv, gg = made
    steps = 4
    small = (n_states, width)
    cast = pl.pallas_call(
        functools.partial(cast_kernel, steps),
        out_shape=(
            like((full, units), f32), like((units, full), f32), like((full, glu_cols), f32), like((full, glu_cols), f32),
            like(act, f32), like(act, f32), like(small, f32), like(small, f32), like(small, f32), like(small, f32),
            *[like((1, width), f32)] * 3,
        ),
        in_specs=[ANY] * 8,
        out_specs=(ANY,) * 6 + (VM,) * 7,
        scratch_shapes=[
            V(gin.shape, bf16), V(gout.shape, bf16), V(gv.shape, bf16), V(gg.shape, bf16),
            V((full, units), f32), V((units, full), f32), V((full, glu_cols), f32), V((full, glu_cols), f32),
            V(tables.shape, f32), V(gains.shape, f32), V(act, f32), V(act, f32),
            pltpu.SemaphoreType.DMA((4, steps)), pltpu.SemaphoreType.DMA((4, steps)), pltpu.SemaphoreType.DMA((6,)),
        ],
        compiler_params=pltpu.CompilerParams(vmem_limit_bytes=58 * 1024 * 1024),
        name="cast",
    )(gin, gout, gv, gg, block_out, in_grad, tables, gains)
    gin, gout, gv, gg, block_out, in_grad, dec, ang, real, imag, *gains = cast
    return (
        block_out, in_grad, gains[0][0], dec.T, ang.T, real.T, imag.T, gains[1][0], gv, gg, gains[2][0], gin, gout,
    )


def solution(mesh):
    act = P(None, "seq", "chan")
    vec, mat = P("chan"), P("chan", None)
    col = P(None, "chan")
    sizes = (mesh.shape["seq"], mesh.shape["chan"])
    return jax.shard_map(
        functools.partial(per_device, sizes),
        mesh=mesh,
        in_specs=(act, P(), act, vec, mat, mat, mat, mat, vec, col, col, vec, col, mat),
        out_specs=(act, act, vec, mat, mat, mat, mat, vec, col, col, vec, col, mat),
        check_vma=False,
    )
```

```python
import functools

import jax
import jax.numpy as jnp
from jax import lax
from jax.experimental import pallas as pl
from jax.experimental.pallas import tpu as pltpu
from jax.sharding import PartitionSpec as P

epsilon = 1e-05
LANES = 128
MESH = pl.DeviceIdType.MESH
VM = pl.BlockSpec(memory_space=pltpu.VMEM)
ANY = pl.BlockSpec(memory_space=pl.ANY)
GELU_A = 0.7978845608028654
GELU_B = 0.044715
NN = (((1,), (0,)), ((), ()))
NT = (((1,), (1,)), ((), ()))
f32, bf16 = jnp.float32, jnp.bfloat16


def gelu_parts(x):
    inner = GELU_A * (x + GELU_B * (x * x * x))
    t = jnp.tanh(inner)
    half = 0.5 * (1.0 + t)
    slope = half + 0.5 * x * (1.0 - t * t) * (GELU_A * (1.0 + 3.0 * GELU_B * (x * x)))
    return x * half, slope


def dot(a, b, dims=NN):
    return lax.dot_general(a, b, dims, preferred_element_type=f32)


def cmul(ar, ai, br, bi):
    return ar * br - ai * bi, ar * bi + ai * br


def power(re, im, count):
    out = None
    while count:
        if count & 1:
            out = (re, im) if out is None else cmul(*out, re, im)
        re, im = cmul(re, im, re, im)
        count >>= 1
    return out


def row(ref, b, p):
    return jnp.broadcast_to(ref[b, pl.ds(p, 1), :], (8, LANES))


def tile(ref, lead, rows, cols):
    return ref[(*lead, rows, cols)].reshape(-1, 8, LANES)


class Line:
    def __init__(self, own, count, at, send, inward, across, sems, where, hand_over, stores=None):
        self.own, self.count, self.at = own, count, at
        self.send, self.inward, self.across = send, inward, across
        self.sent, self.got = sems
        self.pairs, self.is_end, self.is_mid, self.toward, self.away, self.partner = where
        self.hand_over, self.stores = hand_over, stores

    def copy(self, src, dst, i, sent, got, to):
        return pltpu.make_async_remote_copy(
            src_ref=src, dst_ref=dst, send_sem=self.sent.at[sent, i], recv_sem=self.got.at[got, i],
            device_id=to, device_id_type=MESH,
        )

    def pass_in(self, i):
        self.copy(self.send.at[i], self.inward.at[i], i, 0, 0, self.toward).start()

    def pass_across(self, i):
        self.copy(self.send.at[i], self.across.at[i], i, 0, 1, self.toward).start()

    def pass_out(self, i):
        self.copy(self.at(i), self.at(i), i, 1, 2, self.away).start()

    def pass_pair(self, i):
        self.copy(self.at(i), self.at(i), i, 2, 3, self.partner).start()

    def arrived(self, i, kind):
        self.copy(self.send.at[i], self.send.at[i], i, 0, kind, self.toward).wait_recv()

    def begin(self, i):
        if self.pairs > 2:

            @pl.when(self.is_end)
            def _():
                self.send[i] = self.own(i).astype(self.send.dtype)
                self.pass_in(i)

    def join(self, i):
        if self.pairs == 2:
            self.send[i] = self.own(i).astype(self.send.dtype)
            self.pass_across(i)
            return

        @pl.when(jnp.logical_not(self.is_end))
        def _():
            total = self.own(i)
            self.arrived(i, 0)
            self.send[i] = (total + self.inward[i].astype(f32)).astype(self.send.dtype)
            if self.pairs == 4:
                self.pass_across(i)
                return

            @pl.when(self.is_mid)
            def _():
                self.pass_across(i)

            @pl.when(jnp.logical_not(self.is_mid))
            def _():
                self.pass_in(i)

    def settle(self, i):
        @pl.when(self.is_mid)
        def _():
            self.arrived(i, 1)
            total = self.send[i].astype(f32) + self.across[i].astype(f32)
            self.at(i)[...] = total.astype(self.send.dtype)
            if self.pairs > 2:
                self.pass_out(i)
            if self.hand_over:
                self.pass_pair(i)

    def relay(self, i):
        if self.pairs > 2:

            @pl.when(jnp.logical_not(self.is_mid))
            def _():
                self.arrived(i, 2)
                if self.pairs > 4:

                    @pl.when(jnp.logical_not(self.is_end))
                    def _():
                        self.pass_out(i)

                if self.hand_over:
                    self.pass_pair(i)

    def saves(self, i):
        return [pltpu.make_async_copy(src, dst, sem) for src, dst, sem in self.stores(i)]

    def store(self, i):
        self.arrived(i, 3)
        for save in self.saves(i):
            save.start()

    def finish(self):
        for i in range(self.count):
            if self.stores:
                for save in self.saves(i):
                    save.wait()
            self.copy(self.send.at[i], self.send.at[i], i, 0, 0, self.toward).wait_send()
            if self.pairs > 2:

                @pl.when(jnp.logical_not(self.is_end))
                def _(i=i):
                    self.copy(self.send.at[i], self.send.at[i], i, 1, 2, self.toward).wait_send()

            if self.hand_over:
                done = self.copy(self.send.at[i], self.send.at[i], i, 2, 3, self.toward)
                done.wait_send()


def block_kernel(
    sizes,
    docs, x_hbm, og_hbm, gain1, dec_hbm, ang_hbm, real_hbm, imag_hbm, skip_ref, gluv_hbm, glug_hbm, gain2, win_hbm, wout_hbm,
    block_out, in_grad, tables_out, gains_out, gin_hbm, gout_hbm, gv_hbm, gg_hbm,
    gin_out, gout_out, gv_out, gg_out, gluv, glug, win, wout, x_ref, og_ref, dec_ref, ang_ref, real_ref, imag_ref,
    keep, first_mask, last_mask, valid,
    lam, coef, step_l, factor,
    gain_full, normed1, u_ref, y_ref, edge_sum, init, adj,
    act_full, centred, val, gate, resid, normed2, grad_full, mid_full, hidden_grad, hidden, pre,
    act_t, mid_t, hidden_t, part_own, mid_grad, result_own, resid_grad, value_grad, gate_grad, mixer_grad,
    row_a, row_b, u_rows, keep4, tails, part, states,
    stat_send, stat_recv, rs_send, rs_recv,
    pair_send, pair_recv, line_send, line_recv, back_send, back_low, back_recv,
    table, table2, table_sum, table_send, table_in, table_across,
    gain_all,
    grad2, act2, mid2, act_t2, mid_t2, hidden_t2, pre2, value2, gate2,
    in_send, in_in, in_across, out_send, out_in, out_across, gv_send, gv_in, gv_across, gg_send, gg_in, gg_across,
    load_sem, save_sem, chan_send, chan_recv, seq_send, seq_recv, fac_send, fac_recv, gain_send, gain_recv, line_sent, line_got,
):
    n_seq, n_chan = sizes
    pairs = n_seq // 2
    streams, length, width = x_hbm.shape
    n_states = lam.shape[1]
    tokens = streams * length
    full = width * n_chan
    units = win.shape[1]
    group = states.shape[4] * 8
    s, c = lax.axis_index("seq"), lax.axis_index("chan")
    odd = lax.rem(s, 2)
    level = lax.div(s, 2)
    partner = (s + 1 - 2 * odd, c)
    every = pl.ds(0, n_states)
    tiles = width // LANES

    def chan_peer(j):
        return lax.rem(c + j, n_chan)

    def chan_block(k, size):
        return pl.ds(pl.multiple_of(k * size, size), size)

    own_cols = chan_block(c, width)

    barrier = pltpu.get_barrier_semaphore()
    for j in range(1, n_chan):
        pl.semaphore_signal(barrier, inc=1, device_id=(s, chan_peer(j)), device_id_type=MESH)
    for d in range(1, n_seq):
        pl.semaphore_signal(barrier, inc=1, device_id=(lax.rem(s + d, n_seq), c), device_id_type=MESH)

    loads = [
        pltpu.make_async_copy(src, dst, load_sem.at[i])
        for i, (src, dst) in enumerate(
            (
                (wout_hbm, wout), (gluv_hbm, gluv), (glug_hbm, glug), (win_hbm, win), (x_hbm, x_ref), (og_hbm, og_ref),
                (dec_hbm, dec_ref), (ang_hbm, ang_ref), (real_hbm, real_ref), (imag_hbm, imag_ref),
            )
        )
    ]
    for i in (4, 5, 6, 7, 8, 9, 0, 1, 2, 3):
        loads[i].start()

    sent = []

    def chan_copy(src, dst, phase, j):
        return pltpu.make_async_remote_copy(
            src_ref=src, dst_ref=dst, send_sem=chan_send.at[phase, j - 1], recv_sem=chan_recv.at[phase, j - 1],
            device_id=(s, chan_peer(j)), device_id_type=MESH,
        )

    def chan_all(pick, phase):
        copies = []
        for j in range(1, n_chan):
            copy = chan_copy(*pick(j), phase, j)
            copy.start()
            copies.append(copy)
        sent.extend(copies)
        return copies

    def landed(copies):
        for copy in copies:
            copy.wait_recv()

    lane = lax.broadcasted_iota(jnp.int32, (tokens, LANES), 1)

    def stats_start(first, second, k, phase):
        packed = jnp.where(lane == 0, first, jnp.where(lane == 1, second, 0.0))
        stat_send[k] = packed.T[:8]
        return chan_all(lambda j: (stat_send.at[k], stat_recv.at[k, j - 1]), phase)

    def stats_end(copies, k):
        landed(copies)
        total = stat_send[k]
        for j in range(1, n_chan):
            total = total + stat_recv[k, j - 1]
        total = jnp.concatenate([total, jnp.zeros((LANES - 8, tokens), f32)], axis=0).T
        return total[:, 0:1] / full, total[:, 1:2] / full

    loads[4].wait()
    loads[5].wait()
    rows_in = x_ref[...].reshape(tokens, width)
    grad_full[:, own_cols] = og_ref[...].reshape(tokens, width).astype(bf16)
    sum1 = jnp.sum(rows_in, axis=1, keepdims=True)
    square1 = jnp.sum(rows_in * rows_in, axis=1, keepdims=True)
    pl.semaphore_wait(barrier, n_chan + n_seq - 2)
    stat_copies = stats_start(sum1, square1, 0, 0)
    grad_copies = chan_all(lambda j: (grad_full.at[:, own_cols], grad_full.at[:, own_cols]), 1)
    gain_full[:, own_cols] = jnp.broadcast_to(gain2[...], (8, width))
    gain_copies = chan_all(lambda j: (gain_full.at[:, own_cols], gain_full.at[:, own_cols]), 9 + streams * tiles)

    start = s * length
    ends = []
    for b in range(streams):
        total, stream = 0, []
        for k in range(docs.shape[1]):
            total = total + docs[b, k]
            stream.append(total)
        ends.append(stream)

    def passed(b, at):
        count = jnp.int32(0)
        for end in ends[b]:
            count = count + jnp.where(end <= at, 1, 0)
        return count

    def kept(block, b):
        return jnp.where(
            passed(b, block * length - 1) == passed(b, block * length + length - 1), 1.0, 0.0
        )

    pair_flags = [[kept(2 * level + x, b) for b in range(2)] for x in range(2)]

    def line_flag(source):
        both = [kept(2 * source, b) * kept(2 * source + 1, b) for b in range(2)]
        return jnp.where(odd == 1, both[1], both[0])

    line_flags = [[line_flag(level + (d if back else -d)) for d in range(1, pairs)] for back in (False, True)]
    position = lax.broadcasted_iota(jnp.int32, (length, LANES), 0) + start
    for b in range(streams):
        here = jnp.zeros((length, LANES), jnp.int32)
        prior = jnp.zeros((length, LANES), jnp.int32)
        for end in ends[b]:
            here = here + jnp.where(position >= end, 1, 0)
            prior = prior + jnp.where(position > end, 1, 0)
        keep[b] = jnp.where(here == prior, 1.0, 0.0)
        first_mask[b] = jnp.where(here == passed(b, start - 1), 1.0, 0.0)
        last_mask[b] = jnp.where(here == passed(b, start + length - 1), 1.0, 0.0)
        valid[b] = jnp.where(position < ends[b][-1], 1.0, 0.0)

    for load in loads[6:]:
        load.wait()
    decay, angle = dec_ref[...], ang_ref[...]
    magnitude = jnp.exp(-decay)
    a2 = angle * angle
    sine, cosine = jnp.ones_like(a2), jnp.ones_like(a2)
    for k in (13, 11, 9, 7, 5, 3):
        sine = 1.0 - sine * a2 * (1.0 / (k * (k - 1)))
    for k in (14, 12, 10, 8, 6, 4, 2):
        cosine = 1.0 - cosine * a2 * (1.0 / (k * (k - 1)))
    lam[0] = magnitude * cosine
    lam[1] = magnitude * (sine * angle)
    twice = 2.0 * decay
    series = jnp.ones_like(twice)
    for k in (9, 8, 7, 6, 5, 4, 3, 2):
        series = 1.0 - series * twice * (1.0 / k)
    factor[...] = jnp.sqrt(twice * series)
    coef[0] = real_ref[...] * factor[...]
    coef[1] = imag_ref[...] * factor[...]
    step_l[0], step_l[1] = power(lam[0], lam[1], length)

    average, square = stats_end(stat_copies, 0)
    scaler1 = lax.rsqrt(square - average * average + epsilon)
    normed1[...] = (rows_in - average) * scaler1
    for b in range(streams):
        rows = slice(b * length, (b + 1) * length)
        for k in range(width // LANES):
            cols = slice(k * LANES, (k + 1) * LANES)
            u_ref[b, :, cols] = normed1[rows, cols] * gain1[:, cols] * valid[b]

    def edges(values, mask, reverse, k):
            cols = pl.ds(k * LANES, LANES)
            row_a[...] = values[:, :, cols] * mask[...]
            for h in range(n_states // group):
                rows = pl.ds(h * group, group)
                l1r, l1i = tile(lam, (0,), rows, cols), tile(lam, (1,), rows, cols)
                l1i = -l1i if reverse else l1i
                l2r, l2i = cmul(l1r, l1i, l1r, l1i)
                l3r, l3i = cmul(l2r, l2i, l1r, l1i)
                l4r, l4i = cmul(l2r, l2i, l2r, l2i)

                def move(i, carry):
                    new = []
                    for b in range(streams):
                        sr, si = carry[2 * b], carry[2 * b + 1]
                        base = length - 4 - 4 * i if reverse else 4 * i
                        u = [row(row_a, b, base + (3 - j if reverse else j)) for j in range(4)]
                        nr = (l4r * sr - l4i * si) + (l3r * u[0] + l2r * u[1]) + (l1r * u[2] + u[3])
                        ni = (l4r * si + l4i * sr) + (l3i * u[0] + l2i * u[1]) + l1i * u[2]
                        new += [nr, ni]
                    return tuple(new)

                zero = jnp.zeros((group // 8, 8, LANES), f32)
                final = lax.fori_loop(0, length // 4, move, (zero,) * (2 * streams), unroll=2)
                cr, ci = tile(coef, (0,), rows, cols), tile(coef, (1,), rows, cols)
                for b in range(streams):
                    fr, fi = final[2 * b], final[2 * b + 1]
                    if reverse:
                        fr, fi = cmul(cr, -ci, fr, fi)
                    edge_sum[k, b, 0, rows] = fr.reshape(-1, LANES)
                    edge_sum[k, b, 1, rows] = fi.reshape(-1, LANES)

    class Carry:
        def __init__(self, target, which, reverse, k):
            self.target, self.which, self.reverse, self.k = target, which, reverse, k
            cols = pl.ds(k * LANES, LANES)
            self.sr = step_l[0, :, cols]
            self.si = -step_l[1, :, cols] if reverse else step_l[1, :, cols]
            self.leads = odd == (1 if reverse else 0)

        def copy(self, src, dst, i, to):
            return pltpu.make_async_remote_copy(
                src_ref=src.at[self.which, self.k], dst_ref=dst, send_sem=seq_send.at[self.which, self.k, i],
                recv_sem=seq_recv.at[self.which, self.k, i], device_id=to, device_id_type=MESH,
            )

        def advance(self, flag, vr, vi, ur, ui):
            r, i = cmul(ur, ui, vr, vi)
            return r * flag, i * flag

        def start(self):
            at = (self.which, self.k)
            pair_send[at] = edge_sum[self.k].astype(bf16)
            self.across = self.copy(pair_send, pair_recv.at[at], 0, partner)
            self.across.start()

        def line(self):
            at = (self.which, self.k)
            self.across.wait_recv()
            mine_r, mine_i = edge_sum[self.k, odd, 0], edge_sum[self.k, odd, 1]
            other_r, other_i = pair_recv[(*at, odd, 0)].astype(f32), pair_recv[(*at, odd, 1)].astype(f32)
            flag = jnp.where(odd == 1, *[pair_flags[0 if self.reverse else 1][b] for b in (1, 0)])
            lr, li = jnp.where(self.leads, mine_r, other_r), jnp.where(self.leads, mine_i, other_i)
            tr, ti = jnp.where(self.leads, other_r, mine_r), jnp.where(self.leads, other_i, mine_i)
            ar, ai = self.advance(flag, lr, li, self.sr, self.si)
            line_send[(*at, 0)] = (ar + tr).astype(bf16)
            line_send[(*at, 1)] = (ai + ti).astype(bf16)
            for d in range(1, pairs):
                to = level - d if self.reverse else level + d

                @pl.when(to >= 0 if self.reverse else to < pairs)
                def _(d=d, to=to):
                    self.onward(d, (2 * to + odd, c)).start()

        def onward(self, d, to=partner):
            return self.copy(line_send, line_recv.at[self.which, self.k, d - 1], 1 + d, to)

        def home(self):
            at = (self.which, self.k)
            dr, di = cmul(self.sr, self.si, self.sr, self.si)
            back_send[...] = jnp.zeros(back_send.shape, f32)
            for d in range(pairs - 1, 0, -1):
                source = level + d if self.reverse else level - d

                @pl.when(source < pairs if self.reverse else source >= 0)
                def _(d=d):
                    self.onward(d).wait_recv()
                    flag = line_flags[self.reverse][d - 1]
                    vr, vi = self.advance(flag, back_send[0], back_send[1], dr, di)
                    back_send[0] = vr + line_recv[(*at, d - 1, 0)].astype(f32)
                    back_send[1] = vi + line_recv[(*at, d - 1, 1)].astype(f32)

            back_low[at] = back_send[...].astype(bf16)
            self.back = self.copy(back_low, back_recv.at[at], 1, partner)
            self.back.start()

        def end(self):
            at = (self.which, self.k)
            cols = pl.ds(self.k * LANES, LANES)
            self.back.wait_recv()
            for b in range(streams):
                flag = pair_flags[1 if self.reverse else 0][b]
                near = [
                    jnp.where(odd == b, back_low[(*at, i)], back_recv[(*at, i)]).astype(f32) for i in range(2)
                ]
                far = self.advance(flag, *near, self.sr, self.si)
                for i in range(2):
                    other = far[i] + pair_recv[(*at, b, i)].astype(f32)
                    self.target[b, i, :, cols] = jnp.where(self.leads, near[i], other)

        def finish(self):
            self.across.wait_send()
            self.back.wait_send()

            for d in range(1, pairs):
                to = level - d if self.reverse else level + d

                @pl.when(to >= 0 if self.reverse else to < pairs)
                def _(d=d):
                    self.onward(d).wait_send()

    low_side = level < pairs // 2
    toward = (s + jnp.where(low_side, 2, -2), c)
    away = (s + jnp.where(low_side, -2, 2), c)
    where = (
        pairs,
        jnp.logical_or(level == 0, level == pairs - 1),
        jnp.logical_or(level == pairs // 2 - 1, level == pairs // 2),
        toward, away, partner,
    )
    factors = []

    def swap_factor(src, dst, k, to=partner):
        copy = pltpu.make_async_remote_copy(
            src_ref=src, dst_ref=dst, send_sem=fac_send.at[k], recv_sem=fac_recv.at[k], device_id=to, device_id_type=MESH
        )
        copy.start()
        factors.append(copy)
        return copy

    half_units = units // 2
    my_half = chan_block(odd, half_units)
    their_half = chan_block(1 - odd, half_units)
    wanted = {}

    def need(*names):
        for name in names:
            wanted[name].wait_recv()

    in_rows, in_cols = full // 4, units // 4
    out_rows, out_cols = units // 4, full // 4
    glu_rows, glu_half = full // 4, width // 2
    my_glu, their_glu = chan_block(odd, glu_half), chan_block(1 - odd, glu_half)

    ready = []

    def in_own(i):
        assert "mid" in ready
        if i == 0:
            need("pre")
        rows, cols = pl.ds((i // 2) * in_rows, in_rows), (i % 2) * in_cols
        mine = pl.ds(pl.multiple_of(odd * half_units + cols, in_cols), in_cols)
        return dot(mid_t[rows, :], pre[:, mine]) + dot(mid_t2[rows, :], pre2[:, pl.ds(cols, in_cols)])

    def in_at(i):
        return gin_out.at[odd, i // 2, i % 2]

    def out_own(i):
        if i == 0:
            need("grad", ("hidden", 0))
        if i == 4:
            need(("hidden", 1))
        rows, cols = (i // 4) * out_rows, pl.ds((i % 4) * out_cols, out_cols)
        mine = pl.ds(pl.multiple_of(odd * half_units + rows, out_rows), out_rows)
        return dot(hidden_t[mine, :], grad_full[:, cols]) + dot(hidden_t2[pl.ds(rows, out_rows), :], grad2[:, cols])

    def out_at(i):
        return gout_out.at[odd, i // 4, i % 4]

    def glu_own(near, far, names):
        def own(i):
            if i == 0:
                need(*names)
            assert "act" in ready
            rows = pl.ds(i * glu_rows, glu_rows)
            return dot(act_t[rows, :], near[:, my_glu]) + dot(act_t2[rows, :], far[...])

        return own

    def glu_at(out):
        def at(i):
            return out.at[odd, i]

        return at

    def table_own(q):
        need(("table", q))
        return table[q] + table2[q]

    sem_at = [0]

    def line(own, count, at, bufs, hand_over, kept_at=None):
        spot, base = pl.ds(sem_at[0], count), sem_at[0]
        stores = None
        if kept_at:
            held, final, place = kept_at

            def stores(i):
                return [(held.at[(x, *place(i))], final.at[(x, *place(i))], save_sem.at[x, base + i]) for x in range(2)]

        sem_at[0] += count
        return Line(own, count, at, *bufs, (line_sent.at[:, spot], line_got.at[:, spot]), where, hand_over, stores)

    quarters = (width // LANES) * (n_states // group)
    in_line = line(in_own, 8, in_at, (in_send, in_in, in_across), True, (gin_out, gin_hbm, lambda i: (i // 2, i % 2)))
    out_line = line(out_own, 8, out_at, (out_send, out_in, out_across), True, (gout_out, gout_hbm, lambda i: (i // 4, i % 4)))
    gv_line = line(glu_own(value_grad, value2, ("value",)), 4, glu_at(gv_out), (gv_send, gv_in, gv_across), True, (gv_out, gv_hbm, lambda i: (i,)))
    gg_line = line(glu_own(gate_grad, gate2, ("gate",)), 4, glu_at(gg_out), (gg_send, gg_in, gg_across), True, (gg_out, gg_hbm, lambda i: (i,)))
    table_line = line(table_own, quarters, lambda q: table_sum.at[q], (table_send, table_in, table_across), False)
    lines = [out_line, gv_line, in_line, gg_line, table_line]
    pieces = [(entry, i) for entry in lines[:4] for i in range(entry.count)]
    tick, begun = [0], [0]
    MID, LAST, STORE = 2, 4, 8

    def launch(count):
        for _ in range(count):
            if begun[0] < len(pieces):
                entry, i = pieces[begun[0]]
                entry.begin(i)
            begun[0] += 1

    def pump(count, lead=4):
        for _ in range(count):
            t = tick[0]
            tick[0] += 1
            launch(t + 1 + lead - begun[0])
            for ahead, act in ((0, "join"), (-MID, "settle"), (-LAST, "relay"), (-STORE, "store")):
                if 0 <= t + ahead < len(pieces):
                    entry, i = pieces[t + ahead]
                    getattr(entry, act)(i)

    forward = [Carry(init, 0, False, k) for k in range(tiles)]
    for k in range(tiles):
        edges(u_ref, last_mask, False, k)
        forward[k].start()
    unit_block = min(units, 256)

    def hidden_grad_part(i):
        cols = pl.ds(i * unit_block, unit_block)
        hidden_grad[:, cols] = dot(grad_full[...], wout[cols, :], NT)

    loads[0].wait()
    landed(grad_copies)
    blocks = units // unit_block
    for k in range(blocks // 2):
        hidden_grad_part(k)
    for k in range(tiles):
        forward[k].line()
    for k in range(blocks // 2, blocks):
        hidden_grad_part(k)
    for k in range(tiles):
        forward[k].home()
    wanted["grad"] = swap_factor(grad_full, grad2, 0)
    act_copies = []
    for k in range(tiles):
        forward[k].end()
        cols = pl.ds(k * LANES, LANES)
        u_rows[k] = u_ref[:, :, cols]
        near = [jnp.sum(coef[0, :, cols], axis=0, keepdims=True)]
        qr, qi = coef[0, :, cols], coef[1, :, cols]
        for _ in range(3):
            qr, qi = cmul(qr, qi, lam[0, :, cols], lam[1, :, cols])
            near.append(jnp.sum(qr, axis=0, keepdims=True))
        fours = length // 4
        local, through = [], []
        for b in range(streams):
            us = [u_rows[k, b, pl.ds(j, fours, stride=4), :] for j in range(4)]
            ks = [keep[b, pl.ds(j, fours, stride=4), :] for j in range(4)]
            reach = ks[0]
            passed_by = [reach]
            for j in range(1, 4):
                reach = reach * ks[j]
                passed_by.append(reach)
            through.append(passed_by)
            keep4[b] = reach
            terms, outs = [], []
            for j in range(4):
                terms = [term * ks[j] for term in terms] + [us[j]]
                out = skip_ref[:, cols] * us[j]
                for i, term in enumerate(terms):
                    out = out + near[j - i] * term
                outs.append(out)
            local.append(outs)
            for j in range(4):
                tails[b, j] = terms[j]
        for h in range(n_states // group):
            rows = pl.ds(h * group, group)
            l1r, l1i = tile(lam, (0,), rows, cols), tile(lam, (1,), rows, cols)
            l2r, l2i = cmul(l1r, l1i, l1r, l1i)
            l3r, l3i = cmul(l2r, l2i, l1r, l1i)
            l4r, l4i = cmul(l2r, l2i, l2r, l2i)
            cr, ci = tile(coef, (0,), rows, cols), tile(coef, (1,), rows, cols)
            taps = [cmul(cr, ci, *power_of) for power_of in ((l1r, l1i), (l2r, l2i), (l3r, l3i), (l4r, l4i))]

            def move(i, carry, h=h, l1=(l1r, l1i), l2=(l2r, l2i), l3=(l3r, l3i), l4=(l4r, l4i), taps=taps):
                new = []
                for b in range(streams):
                    sr, si = carry[2 * b], carry[2 * b + 1]
                    for j in range(4):
                        spot = pl.ds(pl.multiple_of(((b * 4 + j) * fours + i) * 8, 8), 8)
                        out = (taps[j][0] * sr - taps[j][1] * si).sum(0)
                        if h == 0:
                            part[spot, :] = out
                        else:
                            part[spot, :] += out
                    m = row(keep4, b, i)
                    t = [row(tails.at[b], j, i) for j in range(4)]
                    sr = sr * m
                    si = si * m
                    nr = (l4[0] * sr - l4[1] * si) + (l3[0] * t[0] + l2[0] * t[1]) + (l1[0] * t[2] + t[3])
                    ni = (l4[0] * si + l4[1] * sr) + (l3[1] * t[0] + l2[1] * t[1]) + l1[1] * t[2]
                    new += [nr, ni]
                return tuple(new)

            begin = []
            for b in range(streams):
                begin += [tile(init, (b, 0), rows, cols), tile(init, (b, 1), rows, cols)]
            lax.fori_loop(0, fours, move, tuple(begin), unroll=2)
        for b in range(streams):
            for j in range(4):
                first = (b * 4 + j) * fours * 8
                total = part[pl.ds(first, fours, stride=8), :]
                for i in range(1, 8):
                    total = total + part[pl.ds(first + i, fours, stride=8), :]
                row_a[b, pl.ds(j, fours, stride=4), :] = through[b][j] * total + local[b][j]
            y = row_a[b]
            y_ref[b, :, cols] = y
            to = pl.ds(pl.multiple_of(c * width + k * LANES, LANES), LANES)
            here = pl.ds(b * length, length)
            act_full[here, to] = gelu_parts(y)[0].astype(bf16)
            act_copies.append(
                chan_all(lambda j: (act_full.at[here, to], act_full.at[here, to]), 2 + streams * k + b)
            )
    base = 2 + streams * tiles

    def again_pass(q):
        k, h = q // (n_states // group), q % (n_states // group)
        rows, cols = pl.ds(h * group, group), pl.ds(k * LANES, LANES)
        lr, li = tile(lam, (0,), rows, cols), tile(lam, (1,), rows, cols)
        held = states.at[q % 2]

        def again(p, carry):
            new = []
            for b in range(streams):
                sr, si = carry[2 * b], carry[2 * b + 1]
                u = row(u_rows.at[k], b, p)
                m = row(keep, b, p)
                sr = sr * m
                si = si * m
                nr = (lr * sr - li * si) + u
                ni = lr * si + li * sr
                held[p + 1, b, 0] = nr
                held[p + 1, b, 1] = ni
                new += [nr, ni]
            return tuple(new)

        begin = []
        for b in range(streams):
            begin += [tile(init, (b, 0), rows, cols), tile(init, (b, 1), rows, cols)]
            held[0, b, 0] = begin[-2]
            held[0, b, 1] = begin[-1]
        lax.fori_loop(0, length, again, tuple(begin), unroll=2)

    loads[1].wait()
    loads[2].wait()
    for copies in act_copies:
        landed(copies)
    beside = (s, c + 1 - 2 * lax.rem(c, 2))
    core_half = chan_block(lax.rem(c, 2), tokens // 2)
    wanted["act_near"] = swap_factor(act_full.at[core_half, :], act2.at[core_half, :], 1)
    val[...] = dot(act_full[...], gluv[...])
    gate[...] = jax.nn.sigmoid(dot(act_full[...], glug[...]))
    resid[...] = rows_in_of(x_ref, tokens, width) + val[...] * gate[...]

    sum2 = jnp.sum(resid[...], axis=1, keepdims=True)
    square2 = jnp.sum(resid[...] * resid[...], axis=1, keepdims=True)
    centred[:, own_cols] = (resid[...] - sum2 / width).astype(bf16)
    stat_copies = stats_start(sum2, square2, 1, base)
    mid_copies = chan_all(lambda j: (centred.at[:, own_cols], centred.at[:, own_cols]), base + 1)
    landed(gain_copies)
    landed(stat_copies)
    shares = [stat_send[1], *[stat_recv[1, j - 1] for j in range(1, n_chan)]]
    shares = jnp.concatenate([*shares, jnp.zeros((LANES - 8 * n_chan, tokens), f32)], axis=0).T
    average, square = 0.0, 0.0
    for j in range(n_chan):
        average = average + shares[:, 8 * j : 8 * j + 1] / full
        square = square + shares[:, 8 * j + 1 : 8 * j + 2] / full
    scaler2 = lax.rsqrt(square - average * average + epsilon)
    normed2[...] = (resid[...] - average) * scaler2
    mid_full[:, own_cols] = (normed2[...] * gain2[...]).astype(bf16)
    landed(mid_copies)
    for j in range(1, n_chan):
        cols = chan_block(lax.rem(c - j + n_chan, n_chan), width)
        shift = shares[:, 8 * j : 8 * j + 1] / width - average
        mid_full[:, cols] = ((centred[:, cols].astype(f32) + shift) * scaler2 * gain_full[0:1, cols]).astype(bf16)
    loads[3].wait()

    for k in range(4):
        cols = pl.ds(k * out_rows, out_rows)
        value, slope = gelu_parts(dot(mid_full[...], win[:, cols]))
        hidden[:, cols] = value.astype(bf16)
        pre[:, cols] = (hidden_grad[:, cols] * slope).astype(bf16)
        hidden_t[cols, :] = hidden[:, cols].T
    for k in range(2):
        theirs = pl.ds(pl.multiple_of((1 - odd) * half_units + k * out_rows, out_rows), out_rows)
        wanted["hidden", k] = swap_factor(
            hidden_t.at[theirs, :], hidden_t2.at[pl.ds(k * out_rows, out_rows), :], 4 if k == 0 else 10 + quarters
        )

    def scatter_fill(piece, own, k):
        for j in range(1, n_chan):
            rs_send[k, j - 1] = piece(chan_block(chan_peer(j), width)).astype(bf16)
        own[...] = piece(own_cols)

    def scatter_start(k, phase):
        return chan_all(lambda j: (rs_send.at[k, j - 1], rs_recv.at[k, j - 1]), phase)

    def transposed(source, target, count):
        for k in range(count):
            target[pl.ds(k * width, width), :] = source[:, k * width : (k + 1) * width].T

    def scatter_end(copies, own, k):
        landed(copies)
        total = own[...]
        for j in range(1, n_chan):
            total = total + rs_recv[k, j - 1].astype(f32)
        return total

    scatter_fill(lambda rows: dot(pre[...], win[rows, :], NT), part_own, 0)
    grad_parts = scatter_start(0, base + 2)
    first, second = 0.0, 0.0
    for j in range(n_chan):
        cols = chan_block(chan_peer(j), width) if j else own_cols
        values = rs_send[0, j - 1].astype(f32) if j else part_own[...]
        first = first + jnp.sum(values * gain_full[0:1, cols], axis=1, keepdims=True)
        second = second + jnp.sum(values * mid_full[:, cols].astype(f32), axis=1, keepdims=True)
    stat_copies = stats_start(first, second, 2, base + 4)
    scatter_fill(lambda cols: dot(hidden[...], wout[:, cols]), result_own, 1)
    transposed(act_full, act_t, n_chan)
    transposed(mid_full, mid_t, n_chan)
    wanted["act_near"].wait_recv()
    wanted["act_far"] = swap_factor(act2.at[core_half, :], act2.at[core_half, :], 9, beside)
    for q in range(min(2, quarters)):
        again_pass(q)
    launch(4)
    mid_grad[...] = scatter_end(grad_parts, part_own, 0)
    wanted["pre"] = swap_factor(pre.at[:, their_half], pre2, 5)
    gains = jnp.sum(mid_grad[...] * normed2[...], axis=0, keepdims=True)
    first, second = stats_end(stat_copies, 2)
    resid_grad[...] = og_ref[...].reshape(tokens, width) + scaler2 * (
        mid_grad[...] * gain2[...] - first - normed2[...] * second
    )

    value_grad[...] = (resid_grad[...] * gate[...]).astype(bf16)
    gate_grad[...] = (resid_grad[...] * val[...] * gate[...] * (1.0 - gate[...])).astype(bf16)
    scatter_fill(
        lambda rows: dot(value_grad[...], gluv[rows, :], NT) + dot(gate_grad[...], glug[rows, :], NT), val, 2
    )
    act_parts = scatter_start(2, base + 5)
    wanted["value"] = swap_factor(value_grad.at[:, their_glu], value2, 6)
    wanted["gate"] = swap_factor(gate_grad.at[:, their_glu], gate2, 7)
    pump(2, 2)
    act_grad = scatter_end(act_parts, val, 2)
    mixer_grad[...] = act_grad.reshape(streams, length, width) * gelu_parts(y_ref[...])[1]

    out_parts = scatter_start(1, base + 3)

    backward = [Carry(adj, 1, True, k) for k in range(tiles)]
    for k in range(tiles):
        edges(mixer_grad, first_mask, True, k)
        backward[k].start()
        if k == 0:
            pump(1, 2)
    pump(1, 2)
    for k in range(tiles):
        backward[k].line()
    wanted["mid_near"] = swap_factor(mid_full.at[core_half, :], mid2.at[core_half, :], 2)
    pump(1, 2)
    total = scatter_end(out_parts, result_own, 1)
    block_out[...] = (resid[...] + total).reshape(streams, length, width)
    for k in range(tiles):
        backward[k].home()
    need("act_far")
    transposed(act2, act_t2, n_chan)
    ready.append("act")
    pump(2)
    zero = jnp.zeros((group // 8, 8, LANES), f32)
    q = 0

    def tables(**steps):
        for act, i in steps.items():
            if 0 <= i < quarters:
                getattr(table_line, act)(i)

    for k in range(width // LANES):
        backward[k].end()
        cols = pl.ds(k * LANES, LANES)
        row_b[...] = mixer_grad[:, :, cols]
        for h in range(n_states // group):
            rows = pl.ds(h * group, group)
            lr, li = tile(lam, (0,), rows, cols), tile(lam, (1,), rows, cols)
            cr, ci = tile(coef, (0,), rows, cols), tile(coef, (1,), rows, cols)

            if q > 1:
                again_pass(q)
            pump(2, 3)
            if q == 0:
                wanted["mid_near"].wait_recv()
                wanted["mid_far"] = swap_factor(mid2.at[core_half, :], mid2.at[core_half, :], 3, beside)
            tables(begin=q - 1, join=q - 2, relay=q - 3)
            held = states.at[q % 2]

            def back(i, carry, h=h, held=held, lr=lr, li=li, cr=cr, ci=ci):
                glr, gli, gcr, gci = carry[:4]
                adjoint = carry[4:]
                p = length - 1 - i
                new = []
                for b in range(streams):
                    ar, ai = adjoint[2 * b], adjoint[2 * b + 1]
                    g = row(row_b, b, p)
                    m = row(keep, b, p)
                    nr = (lr * ar + li * ai) + cr * g
                    ni = (lr * ai - li * ar) - ci * g
                    spot = pl.ds(pl.multiple_of((b * length + p) * 8, 8), 8)
                    if h == 0:
                        part[spot, :] = nr.sum(0)
                    else:
                        part[spot, :] += nr.sum(0)
                    gcr = gcr + g * held[p + 1, b, 0]
                    gci = gci - g * held[p + 1, b, 1]
                    nr = nr * m
                    ni = ni * m
                    sr, si = held[p, b, 0], held[p, b, 1]
                    glr = glr + (nr * sr + ni * si)
                    gli = gli + (ni * sr - nr * si)
                    new += [nr, ni]
                return (glr, gli, gcr, gci, *new)

            begin = []
            for b in range(streams):
                begin += [tile(adj, (b, 0), rows, cols), tile(adj, (b, 1), rows, cols)]
            sums = lax.fori_loop(0, length, back, (zero, zero, zero, zero, *begin), unroll=2)
            glr, gli, gcr, gci = [item.reshape(-1, LANES) for item in sums[:4]]
            share = factor[rows, cols]
            ratio = (1.0 - share * share) / share
            spots = [pl.ds(i * group, group) for i in range(4)]
            table[q, spots[0], :] = (gcr * real_ref[rows, cols] + gci * imag_ref[rows, cols]) * ratio - (
                glr * lam[0, rows, cols] + gli * lam[1, rows, cols]
            )
            table[q, spots[1], :] = gli * lam[0, rows, cols] - glr * lam[1, rows, cols]
            table[q, spots[2], :] = share * gcr
            table[q, spots[3], :] = share * gci
            wanted["table", q] = swap_factor(table.at[q], table2.at[q], 10 + q)
            if q == 0:
                need("mid_far")
                transposed(mid2, mid_t2, n_chan)
                ready.append("mid")
            pump(2, 3)
            tables(settle=q - 2)
            q += 1
        for b in range(streams):
            total = part[pl.ds(b * length * 8, length, stride=8), :]
            for j in range(1, 8):
                total = total + part[pl.ds(b * length * 8 + j, length, stride=8), :]
            u_grad = total + skip_ref[:, cols] * row_b[b]
            part_own[b * length : (b + 1) * length, cols] = u_grad * valid[b]

    last = quarters - 1
    scaled = part_own[...] * gain1[...]
    stat_copies = stats_start(
        jnp.sum(scaled, axis=1, keepdims=True),
        jnp.sum(scaled * normed1[...], axis=1, keepdims=True), 3, base + 6,
    )
    gain_rows = [
        jnp.sum(part_own[...] * normed1[...], axis=0, keepdims=True),
        jnp.sum(jnp.sum(mixer_grad[...] * u_ref[...], axis=0), axis=0, keepdims=True),
        gains,
    ]
    gain_all[s] = jnp.concatenate([*gain_rows, jnp.zeros((5, width), f32)], axis=0)
    for d in range(1, n_seq):
        copy = pltpu.make_async_remote_copy(
            src_ref=gain_all.at[s], dst_ref=gain_all.at[s], send_sem=gain_send.at[d], recv_sem=gain_recv.at[s],
            device_id=(lax.rem(s + d, n_seq), c), device_id_type=MESH,
        )
        copy.start()
        sent.append(copy)
    pump(1)
    tables(join=last - 1, relay=last - 2)
    pump(1)
    tables(begin=last)
    pump(1)
    tables(settle=last - 1)
    first, second = stats_end(stat_copies, 3)
    in_grad[...] = (
        resid_grad[...] + scaler1 * (part_own[...] * gain1[...] - first - normed1[...] * second)
    ).reshape(streams, length, width)
    tables(join=last)
    pump(1)
    tables(relay=last - 1)
    pump(1)
    tables(settle=last)
    pump(1)
    tables(relay=last)
    while tick[0] < len(pieces) + STORE:
        pump(1)
    for k in range(width // LANES):
        for h in range(n_states // group):
            for i in range(4):
                tables_out[i, h * group : (h + 1) * group, k * LANES : (k + 1) * LANES] = table_sum[
                    k * (n_states // group) + h, i * group : (i + 1) * group, :
                ]
    for d in range(1, n_seq):
        source = lax.rem(s + d, n_seq)
        pltpu.make_async_remote_copy(
            src_ref=gain_all.at[s], dst_ref=gain_all.at[source], send_sem=gain_send.at[d], recv_sem=gain_recv.at[source],
            device_id=(source, c), device_id_type=MESH,
        ).wait_recv()
    total = gain_all[0]
    for k in range(1, n_seq):
        total = total + gain_all[k]
    gains_out[...] = total
    for entry in lines:
        entry.finish()
    for copy in factors:
        copy.wait_send()
    for copy in sent:
        copy.wait_send()
    for carry in (*forward, *backward):
        carry.finish()


def rows_in_of(ref, tokens, width):
    return ref[...].reshape(tokens, width)


def cast_kernel(
    steps, gin, gout, gv, gg, block, grad, tables, gains,
    gin_hbm, gout_hbm, gv_hbm, gg_hbm, block_out, grad_out, dec_out, ang_out, real_out, imag_out, gain_a, gain_b, gain_c,
    gin_low, gout_low, gv_low, gg_low, gin_out, gout_out, gv_out, gg_out, table_low, gain_low, block_low, grad_low, load_sem, save_sem, small_sem,
):
    whole = [
        pltpu.make_async_copy(src, dst, small_sem.at[i])
        for i, (src, dst) in enumerate(
            [(tables, table_low), (gains, gain_low), (block, block_low), (grad, grad_low)]
        )
    ]
    full, units = gin_out.shape
    rows, tall = full // steps, units // steps
    loads, saves = [], []
    for p in range(steps):
        here, tall_here = pl.ds(p * rows, rows), pl.ds(p * tall, tall)
        loads.append(
            [
                pltpu.make_async_copy(gin.at[:, p], gin_low.at[:, p], load_sem.at[0, p]),
                pltpu.make_async_copy(gout.at[p // 2, p % 2], gout_low.at[p // 2, p % 2], load_sem.at[1, p]),
                pltpu.make_async_copy(gv.at[:, p], gv_low.at[:, p], load_sem.at[2, p]),
                pltpu.make_async_copy(gg.at[:, p], gg_low.at[:, p], load_sem.at[3, p]),
            ]
        )
        saves.append(
            [
                pltpu.make_async_copy(gin_out.at[here], gin_hbm.at[here], save_sem.at[0, p]),
                pltpu.make_async_copy(gout_out.at[tall_here], gout_hbm.at[tall_here], save_sem.at[1, p]),
                pltpu.make_async_copy(gv_out.at[here], gv_hbm.at[here], save_sem.at[2, p]),
                pltpu.make_async_copy(gg_out.at[here], gg_hbm.at[here], save_sem.at[3, p]),
            ]
        )
    for copies in loads:
        for copy in copies:
            copy.start()
    for copy in whole:
        copy.start()
    for p in range(steps):
        here, tall_here = slice(p * rows, (p + 1) * rows), slice(p * tall, (p + 1) * tall)
        for copy in loads[p]:
            copy.wait()
        for i in range(4):
            cols = slice(i * tall, (i + 1) * tall)
            gin_out[here, cols] = gin_low[i // 2, p, i % 2].astype(f32)
        for i in range(4):
            cols = slice(i * rows, (i + 1) * rows)
            gout_out[tall_here, cols] = gout_low[p // 2, p % 2, i].astype(f32)
        for x in range(2):
            cols = slice(x * gv.shape[-1], (x + 1) * gv.shape[-1])
            gv_out[here, cols] = gv_low[x, p].astype(f32)
            gg_out[here, cols] = gg_low[x, p].astype(f32)
        for copy in saves[p]:
            copy.start()
    for copy in whole:
        copy.wait()
    passed_on = [
        pltpu.make_async_copy(block_low, block_out, small_sem.at[4]),
        pltpu.make_async_copy(grad_low, grad_out, small_sem.at[5]),
    ]
    for copy in passed_on:
        copy.start()
    for k, out in enumerate((dec_out, ang_out, real_out, imag_out)):
        out[...] = table_low[k]
    for k, out in enumerate((gain_a, gain_b, gain_c)):
        out[...] = gain_low[k : k + 1, :]
    for copies in (*saves, passed_on):
        for copy in copies:
            copy.wait()


def per_device(
    sizes, block_in, doc_lengths, out_grad, first_gain, decay_rate, turn_angle, out_real, out_imag,
    skip_gain, glu_value, glu_gate, second_gain, ffn_in, ffn_out,
):
    n_seq, n_chan = sizes
    pairs = n_seq // 2
    streams, length, width = block_in.shape
    n_states = decay_rate.shape[1]
    tokens = streams * length
    full = width * n_chan
    units = ffn_in.shape[1]
    glu_cols = glu_value.shape[1]
    group = min(32, n_states)
    like = jax.ShapeDtypeStruct
    quarters = (width // LANES) * (n_states // group)
    phases = 10 + streams * (width // LANES)
    act = (streams, length, width)
    flat = (tokens, width)
    mask = (streams, length, LANES)
    tab, lane_tab = (2, n_states, width), (2, n_states, LANES)
    tiles = width // LANES
    V = pltpu.VMEM
    scratch = [
        V((2, 4, 2, full // 4, units // 4), bf16), V((2, 2, 4, units // 4, full // 4), bf16), *[V((2, 4, full // 4, glu_cols // 2), bf16)] * 2,
        V((full, glu_cols), bf16), V((full, glu_cols), bf16), V((full, units), bf16), V((units, full), bf16),
        V(act, f32), V(act, f32), *[V((n_states, width), f32)] * 4,
        V(mask, f32), V(mask, f32), V(mask, f32), V(mask, f32),
        V(tab, f32), V(tab, f32), V(tab, f32), V((n_states, width), f32),
        V((8, full), f32), V(flat, f32), V(act, f32), V(act, f32), V((tiles, streams, 2, n_states, LANES), f32), V((streams, *tab), f32), V((streams, *tab), f32),
        V((tokens, full), bf16), V((tokens, full), bf16), V((tokens, glu_cols), f32), V((tokens, glu_cols), f32), V(flat, f32), V(flat, f32),
        V((tokens, full), bf16), V((tokens, full), bf16), V((tokens, units), f32), V((tokens, units), bf16), V((tokens, units), bf16),
        V((full, tokens), bf16), V((full, tokens), bf16), V((units, tokens), bf16),
        V(flat, f32), V(flat, f32), V(flat, f32), V(flat, f32), V((tokens, glu_cols), bf16), V((tokens, glu_cols), bf16),
        V(act, f32),
        V(mask, f32), V(mask, f32), V((tiles, *mask), f32), V((streams, length // 4, LANES), f32), V((streams, 4, length // 4, LANES), f32), V((tokens * 8, LANES), f32), V((2, length + 1, streams, 2, group // 8, 8, LANES), f32),
        V((4, 8, tokens), f32), V((4, n_chan - 1, 8, tokens), f32), V((3, n_chan - 1, *flat), bf16), V((3, n_chan - 1, *flat), bf16),
        *[V((2, tiles, streams, *lane_tab), bf16)] * 2, V((2, tiles, *lane_tab), bf16), V((2, tiles, pairs - 1, *lane_tab), bf16),
        V(lane_tab, f32), *[V((2, tiles, *lane_tab), bf16)] * 2,
        *[V((quarters, 4 * group, LANES), f32)] * 6,
        V((n_seq, 8, width), f32),
        *[V((tokens, full), bf16)] * 3, V((full, tokens), bf16), V((full, tokens), bf16), V((units // 2, tokens), bf16),
        V((tokens, units // 2), bf16), V((tokens, glu_cols // 2), bf16), V((tokens, glu_cols // 2), bf16),
        *[V((8, full // 4, units // 4), bf16)] * 3, *[V((8, units // 4, full // 4), bf16)] * 3,
        *[V((4, full // 4, glu_cols // 2), bf16)] * 6,
        pltpu.SemaphoreType.DMA((10,)), pltpu.SemaphoreType.DMA((2, 24)),
        pltpu.SemaphoreType.DMA((phases, n_chan - 1)), pltpu.SemaphoreType.DMA((phases, n_chan - 1)),
        pltpu.SemaphoreType.DMA((2, tiles, pairs + 1)), pltpu.SemaphoreType.DMA((2, tiles, pairs + 1)),
        pltpu.SemaphoreType.DMA((11 + quarters,)), pltpu.SemaphoreType.DMA((11 + quarters,)),
        pltpu.SemaphoreType.DMA((n_seq,)), pltpu.SemaphoreType.DMA((n_seq,)),
        pltpu.SemaphoreType.DMA((3, 25 + quarters)), pltpu.SemaphoreType.DMA((4, 25 + quarters)),
    ]
    specs = [pl.BlockSpec(memory_space=pltpu.SMEM), ANY, ANY, VM, ANY, ANY, ANY, ANY, VM, ANY, ANY, VM, ANY, ANY]
    made = pl.pallas_call(
        functools.partial(block_kernel, sizes),
        out_shape=(
            like(act, f32), like(act, f32), like((4, n_states, width), f32), like((8, width), f32),
            like((2, 4, 2, full // 4, units // 4), bf16), like((2, 2, 4, units // 4, full // 4), bf16),
            like((2, 4, full // 4, glu_cols // 2), bf16), like((2, 4, full // 4, glu_cols // 2), bf16),
        ),
        in_specs=specs,
        out_specs=(VM,) * 4 + (ANY,) * 4,
        scratch_shapes=scratch,
        compiler_params=pltpu.CompilerParams(
            collective_id=0, has_side_effects=True, vmem_limit_bytes=60 * 1024 * 1024
        ),
        name="block",
    )(
        doc_lengths, block_in, out_grad, first_gain[None], decay_rate.T, turn_angle.T, out_real.T, out_imag.T, skip_gain[None],
        glu_value, glu_gate, second_gain[None], ffn_in, ffn_out,
    )
    block_out, in_grad, tables, gains, gin, gout, gv, gg = made
    steps = 4
    small = (n_states, width)
    cast = pl.pallas_call(
        functools.partial(cast_kernel, steps),
        out_shape=(
            like((full, units), f32), like((units, full), f32), like((full, glu_cols), f32), like((full, glu_cols), f32),
            like(act, f32), like(act, f32), like(small, f32), like(small, f32), like(small, f32), like(small, f32),
            *[like((1, width), f32)] * 3,
        ),
        in_specs=[ANY] * 8,
        out_specs=(ANY,) * 6 + (VM,) * 7,
        scratch_shapes=[
            V(gin.shape, bf16), V(gout.shape, bf16), V(gv.shape, bf16), V(gg.shape, bf16),
            V((full, units), f32), V((units, full), f32), V((full, glu_cols), f32), V((full, glu_cols), f32),
            V(tables.shape, f32), V(gains.shape, f32), V(act, f32), V(act, f32),
            pltpu.SemaphoreType.DMA((4, steps)), pltpu.SemaphoreType.DMA((4, steps)), pltpu.SemaphoreType.DMA((6,)),
        ],
        compiler_params=pltpu.CompilerParams(vmem_limit_bytes=58 * 1024 * 1024),
        name="cast",
    )(gin, gout, gv, gg, block_out, in_grad, tables, gains)
    gin, gout, gv, gg, block_out, in_grad, dec, ang, real, imag, *gains = cast
    return (
        block_out, in_grad, gains[0][0], dec.T, ang.T, real.T, imag.T, gains[1][0], gv, gg, gains[2][0], gin, gout,
    )


def solution(mesh):
    act = P(None, "seq", "chan")
    vec, mat = P("chan"), P("chan", None)
    col = P(None, "chan")
    sizes = (mesh.shape["seq"], mesh.shape["chan"])
    return jax.shard_map(
        functools.partial(per_device, sizes),
        mesh=mesh,
        in_specs=(act, P(), act, vec, mat, mat, mat, mat, vec, col, col, vec, col, mat),
        out_specs=(act, act, vec, mat, mat, mat, mat, vec, col, col, vec, col, mat),
        check_vma=False,
    )
```

```python
import functools

import jax
import jax.numpy as jnp
from jax import lax
from jax.experimental import pallas as pl
from jax.experimental.pallas import tpu as pltpu
from jax.sharding import PartitionSpec as P

epsilon = 1e-05
LANES = 128
MESH = pl.DeviceIdType.MESH
VM = pl.BlockSpec(memory_space=pltpu.VMEM)
ANY = pl.BlockSpec(memory_space=pl.ANY)
GELU_A = 0.7978845608028654
GELU_B = 0.044715
NN = (((1,), (0,)), ((), ()))
NT = (((1,), (1,)), ((), ()))
f32, bf16 = jnp.float32, jnp.bfloat16


def gelu_parts(x):
    inner = GELU_A * (x + GELU_B * (x * x * x))
    t = jnp.tanh(inner)
    half = 0.5 * (1.0 + t)
    slope = half + 0.5 * x * (1.0 - t * t) * (GELU_A * (1.0 + 3.0 * GELU_B * (x * x)))
    return x * half, slope


def dot(a, b, dims=NN):
    return lax.dot_general(a, b, dims, preferred_element_type=f32)


def cmul(ar, ai, br, bi):
    return ar * br - ai * bi, ar * bi + ai * br


def power(re, im, count):
    out = None
    while count:
        if count & 1:
            out = (re, im) if out is None else cmul(*out, re, im)
        re, im = cmul(re, im, re, im)
        count >>= 1
    return out


def row(ref, b, p):
    return jnp.broadcast_to(ref[b, pl.ds(p, 1), :], (8, LANES))


def tile(ref, lead, rows, cols):
    return ref[(*lead, rows, cols)].reshape(-1, 8, LANES)


TURNS = (8, 8, 8)


class Line:
    def __init__(self, own, count, at, send, inward, across, sems, where, hand_over, stores=None):
        self.own, self.count, self.at = own, count, at
        self.send, self.inward, self.across = send, inward, across
        self.sent, self.got = sems
        self.pairs, self.is_end, self.is_mid, self.toward, self.away, self.partner = where
        self.hand_over, self.stores = hand_over, stores

    def copy(self, src, dst, i, sent, got, to):
        return pltpu.make_async_remote_copy(
            src_ref=src, dst_ref=dst, send_sem=self.sent.at[sent, i % TURNS[sent]], recv_sem=self.got.at[got, i],
            device_id=to, device_id_type=MESH,
        )

    def free(self, i, kind):
        if i >= TURNS[kind]:
            self.gone(i - TURNS[kind], kind)

    def gone(self, i, kind):
        self.copy(self.send.at[i], self.send.at[i], i, kind, 0, self.toward).wait_send()

    def pass_in(self, i):
        self.free(i, 0)
        self.copy(self.send.at[i], self.inward.at[i], i, 0, 0, self.toward).start()

    def pass_across(self, i):
        self.free(i, 0)
        self.copy(self.send.at[i], self.across.at[i], i, 0, 1, self.toward).start()

    def pass_out(self, i):
        self.free(i, 1)
        self.copy(self.at(i), self.at(i), i, 1, 2, self.away).start()

    def pass_pair(self, i):
        self.free(i, 2)
        self.copy(self.at(i), self.at(i), i, 2, 3, self.partner).start()

    def arrived(self, i, kind):
        self.copy(self.send.at[i], self.send.at[i], i, 0, kind, self.toward).wait_recv()

    def begin(self, i):
        if self.pairs > 2:

            @pl.when(self.is_end)
            def _():
                self.send[i] = self.own(i).astype(self.send.dtype)
                self.pass_in(i)

    def join(self, i):
        if self.pairs == 2:
            self.send[i] = self.own(i).astype(self.send.dtype)
            self.pass_across(i)
            return

        @pl.when(jnp.logical_not(self.is_end))
        def _():
            total = self.own(i)
            self.arrived(i, 0)
            self.send[i] = (total + self.inward[i].astype(f32)).astype(self.send.dtype)
            if self.pairs == 4:
                self.pass_across(i)
                return

            @pl.when(self.is_mid)
            def _():
                self.pass_across(i)

            @pl.when(jnp.logical_not(self.is_mid))
            def _():
                self.pass_in(i)

    def settle(self, i):
        @pl.when(self.is_mid)
        def _():
            self.arrived(i, 1)
            total = self.send[i].astype(f32) + self.across[i].astype(f32)
            self.at(i)[...] = total.astype(self.send.dtype)
            if self.pairs > 2:
                self.pass_out(i)
            if self.hand_over:
                self.pass_pair(i)

    def relay(self, i):
        if self.pairs > 2:

            @pl.when(jnp.logical_not(self.is_mid))
            def _():
                self.arrived(i, 2)
                if self.pairs > 4:

                    @pl.when(jnp.logical_not(self.is_end))
                    def _():
                        self.pass_out(i)

                if self.hand_over:
                    self.pass_pair(i)

    def store(self, i):
        self.arrived(i, 3)
        self.stores(i)

    def finish(self):
        for i in range(max(0, self.count - TURNS[0]), self.count):
            self.gone(i, 0)
        for i in range(max(0, self.count - TURNS[1]), self.count):
            if self.pairs > 2:

                @pl.when(jnp.logical_not(self.is_end))
                def _(i=i):
                    self.gone(i, 1)

        if self.hand_over:
            for i in range(max(0, self.count - TURNS[2]), self.count):
                self.gone(i, 2)


def block_kernel(
    sizes,
    docs, x_hbm, og_hbm, gain1, dec_hbm, ang_hbm, real_hbm, imag_hbm, skip_ref, gluv_hbm, glug_hbm, gain2, win_hbm, wout_hbm,
    block_hbm, grad_hbm, tables_hbm, gains_hbm, gin_hbm, gout_hbm, gv_hbm, gg_hbm,
    block_out, in_grad, gains_out, gin_out, gout_out, gv_out, gg_out, gluv, glug, win, wout, x_ref, og_ref, dec_ref, ang_ref, real_ref, imag_ref,
    keep, first_mask, last_mask, valid,
    lam, coef, step_l, factor,
    gain_full, normed1, u_ref, y_ref, edge_sum, init, adj,
    act_full, val, gate, resid, normed2, grad_full, mid_full, hidden_grad, hidden, pre,
    act_t, mid_t, hidden_t, part_own, result_own, resid_grad, value_grad, gate_grad, mixer_grad,
    row_a, row_b, u_rows, keep4, tails, part, states,
    stat_send, stat_recv, rs_send, rs_recv,
    pair_send, pair_recv, line_send, line_recv, back_send, back_low, back_recv,
    table, table2, table_sum, table_send, table_in, table_across,
    gain_all,
    grad2, act2, mid2, act_t2, mid_t2, hidden_t2, pre2, value2, gate2,
    in_send, in_in, in_across, out_send, out_in, out_across, gv_send, gv_in, gv_across, gg_send, gg_in, gg_across,
    load_sem, save_sem, last_sem, chan_send, chan_recv, seq_send, seq_recv, fac_send, fac_recv, gain_send, gain_recv, line_sent, line_got,
):
    n_seq, n_chan = sizes
    pairs = n_seq // 2
    streams, length, width = x_hbm.shape
    n_states = lam.shape[1]
    tokens = streams * length
    full = width * n_chan
    units = win.shape[1]
    group = states.shape[4] * 8
    s, c = lax.axis_index("seq"), lax.axis_index("chan")
    odd = lax.rem(s, 2)
    level = lax.div(s, 2)
    partner = (s + 1 - 2 * odd, c)
    every = pl.ds(0, n_states)
    tiles = width // LANES

    def chan_peer(j):
        return lax.rem(c + j, n_chan)

    def chan_block(k, size):
        return pl.ds(pl.multiple_of(k * size, size), size)

    own_cols = chan_block(c, width)

    barrier = pltpu.get_barrier_semaphore()
    for j in range(1, n_chan):
        pl.semaphore_signal(barrier, inc=1, device_id=(s, chan_peer(j)), device_id_type=MESH)
    for d in range(1, n_seq):
        pl.semaphore_signal(barrier, inc=1, device_id=(lax.rem(s + d, n_seq), c), device_id_type=MESH)

    loads = [
        pltpu.make_async_copy(src, dst, load_sem.at[i])
        for i, (src, dst) in enumerate(
            (
                (wout_hbm, wout), (gluv_hbm, gluv), (glug_hbm, glug), (win_hbm, win), (x_hbm, x_ref), (og_hbm, og_ref),
                (dec_hbm, dec_ref), (ang_hbm, ang_ref), (real_hbm, real_ref), (imag_hbm, imag_ref),
            )
        )
    ]
    for i in (4, 5, 6, 7, 8, 9, 0, 1, 2, 3):
        loads[i].start()

    sent, saved = [], []

    def save(src, dst, i):
        copy = pltpu.make_async_copy(src, dst, last_sem.at[i])
        copy.start()
        saved.append(copy)

    chan_turns, chan_count = [], [0]

    def chan_copy(src, dst, phase, j, turn):
        return pltpu.make_async_remote_copy(
            src_ref=src, dst_ref=dst, send_sem=chan_send.at[turn, j - 1], recv_sem=chan_recv.at[phase, j - 1],
            device_id=(s, chan_peer(j)), device_id_type=MESH,
        )

    def chan_all(pick, phase):
        copies = []
        turn = chan_count[0] % 6
        chan_count[0] += 1
        if len(chan_turns) == 6:
            for copy in chan_turns.pop(0):
                copy.wait_send()
        for j in range(1, n_chan):
            copy = chan_copy(*pick(j), phase, j, turn)
            copy.start()
            copies.append(copy)
        chan_turns.append(copies)
        return copies

    def landed(copies):
        for copy in copies:
            copy.wait_recv()

    lane = lax.broadcasted_iota(jnp.int32, (tokens, LANES), 1)

    def stats_start(first, second, k, phase):
        packed = jnp.where(lane == 0, first, jnp.where(lane == 1, second, 0.0))
        stat_send[k] = packed.T[:8]
        return chan_all(lambda j: (stat_send.at[k], stat_recv.at[k, j - 1]), phase)

    def stats_end(copies, k):
        landed(copies)
        total = stat_send[k]
        for j in range(1, n_chan):
            total = total + stat_recv[k, j - 1]
        total = jnp.concatenate([total, jnp.zeros((LANES - 8, tokens), f32)], axis=0).T
        return total[:, 0:1] / full, total[:, 1:2] / full

    loads[4].wait()
    loads[5].wait()
    rows_in = x_ref[...].reshape(tokens, width)
    grad_full[:, own_cols] = og_ref[...].reshape(tokens, width).astype(bf16)
    sum1 = jnp.sum(rows_in, axis=1, keepdims=True)
    square1 = jnp.sum(rows_in * rows_in, axis=1, keepdims=True)
    pl.semaphore_wait(barrier, n_chan + n_seq - 2)
    stat_copies = stats_start(sum1, square1, 0, 0)
    grad_copies = chan_all(lambda j: (grad_full.at[:, own_cols], grad_full.at[:, own_cols]), 1)
    gain_full[:, own_cols] = jnp.broadcast_to(gain2[...], (8, width))
    gain_copies = chan_all(lambda j: (gain_full.at[:, own_cols], gain_full.at[:, own_cols]), 9 + streams * tiles)

    start = s * length
    ends = []
    for b in range(streams):
        total, stream = 0, []
        for k in range(docs.shape[1]):
            total = total + docs[b, k]
            stream.append(total)
        ends.append(stream)

    def passed(b, at):
        count = jnp.int32(0)
        for end in ends[b]:
            count = count + jnp.where(end <= at, 1, 0)
        return count

    def kept(block, b):
        return jnp.where(
            passed(b, block * length - 1) == passed(b, block * length + length - 1), 1.0, 0.0
        )

    pair_flags = [[kept(2 * level + x, b) for b in range(2)] for x in range(2)]

    def line_flag(source):
        both = [kept(2 * source, b) * kept(2 * source + 1, b) for b in range(2)]
        return jnp.where(odd == 1, both[1], both[0])

    line_flags = [[line_flag(level + (d if back else -d)) for d in range(1, pairs)] for back in (False, True)]
    position = lax.broadcasted_iota(jnp.int32, (length, LANES), 0) + start
    for b in range(streams):
        here = jnp.zeros((length, LANES), jnp.int32)
        prior = jnp.zeros((length, LANES), jnp.int32)
        for end in ends[b]:
            here = here + jnp.where(position >= end, 1, 0)
            prior = prior + jnp.where(position > end, 1, 0)
        keep[b] = jnp.where(here == prior, 1.0, 0.0)
        first_mask[b] = jnp.where(here == passed(b, start - 1), 1.0, 0.0)
        last_mask[b] = jnp.where(here == passed(b, start + length - 1), 1.0, 0.0)
        valid[b] = jnp.where(position < ends[b][-1], 1.0, 0.0)

    for load in loads[6:]:
        load.wait()
    decay, angle = dec_ref[...], ang_ref[...]
    magnitude = jnp.exp(-decay)
    a2 = angle * angle
    sine, cosine = jnp.ones_like(a2), jnp.ones_like(a2)
    for k in (13, 11, 9, 7, 5, 3):
        sine = 1.0 - sine * a2 * (1.0 / (k * (k - 1)))
    for k in (14, 12, 10, 8, 6, 4, 2):
        cosine = 1.0 - cosine * a2 * (1.0 / (k * (k - 1)))
    lam[0] = magnitude * cosine
    lam[1] = magnitude * (sine * angle)
    twice = 2.0 * decay
    series = jnp.ones_like(twice)
    for k in (9, 8, 7, 6, 5, 4, 3, 2):
        series = 1.0 - series * twice * (1.0 / k)
    factor[...] = jnp.sqrt(twice * series)
    coef[0] = real_ref[...] * factor[...]
    coef[1] = imag_ref[...] * factor[...]
    step_l[0], step_l[1] = power(lam[0], lam[1], length)

    average, square = stats_end(stat_copies, 0)
    scaler1 = lax.rsqrt(square - average * average + epsilon)
    normed1[...] = (rows_in - average) * scaler1
    for b in range(streams):
        rows = slice(b * length, (b + 1) * length)
        for k in range(width // LANES):
            cols = slice(k * LANES, (k + 1) * LANES)
            u_ref[b, :, cols] = normed1[rows, cols] * gain1[:, cols] * valid[b]

    def edges(values, mask, reverse, k):
            cols = pl.ds(k * LANES, LANES)
            row_a[...] = values[:, :, cols] * mask[...]
            for h in range(n_states // group):
                rows = pl.ds(h * group, group)
                l1r, l1i = tile(lam, (0,), rows, cols), tile(lam, (1,), rows, cols)
                l1i = -l1i if reverse else l1i
                l2r, l2i = cmul(l1r, l1i, l1r, l1i)
                l3r, l3i = cmul(l2r, l2i, l1r, l1i)
                l4r, l4i = cmul(l2r, l2i, l2r, l2i)

                def move(i, carry):
                    new = []
                    for b in range(streams):
                        sr, si = carry[2 * b], carry[2 * b + 1]
                        base = length - 4 - 4 * i if reverse else 4 * i
                        u = [row(row_a, b, base + (3 - j if reverse else j)) for j in range(4)]
                        nr = (l4r * sr - l4i * si) + (l3r * u[0] + l2r * u[1]) + (l1r * u[2] + u[3])
                        ni = (l4r * si + l4i * sr) + (l3i * u[0] + l2i * u[1]) + l1i * u[2]
                        new += [nr, ni]
                    return tuple(new)

                zero = jnp.zeros((group // 8, 8, LANES), f32)
                final = lax.fori_loop(0, length // 4, move, (zero,) * (2 * streams), unroll=2)
                cr, ci = tile(coef, (0,), rows, cols), tile(coef, (1,), rows, cols)
                for b in range(streams):
                    fr, fi = final[2 * b], final[2 * b + 1]
                    if reverse:
                        fr, fi = cmul(cr, -ci, fr, fi)
                    edge_sum[k, b, 0, rows] = fr.reshape(-1, LANES)
                    edge_sum[k, b, 1, rows] = fi.reshape(-1, LANES)

    class Carry:
        def __init__(self, target, which, reverse, k):
            self.target, self.which, self.reverse, self.k = target, which, reverse, k
            cols = pl.ds(k * LANES, LANES)
            self.sr = step_l[0, :, cols]
            self.si = -step_l[1, :, cols] if reverse else step_l[1, :, cols]
            self.leads = odd == (1 if reverse else 0)

        def copy(self, src, dst, i, to):
            return pltpu.make_async_remote_copy(
                src_ref=src.at[self.which, self.k], dst_ref=dst, send_sem=seq_send.at[self.which, self.k, i],
                recv_sem=seq_recv.at[self.which, self.k, i], device_id=to, device_id_type=MESH,
            )

        def advance(self, flag, vr, vi, ur, ui):
            r, i = cmul(ur, ui, vr, vi)
            return r * flag, i * flag

        def start(self):
            at = (self.which, self.k)
            pair_send[at] = edge_sum[self.k].astype(bf16)
            self.across = self.copy(pair_send, pair_recv.at[at], 0, partner)
            self.across.start()

        def line(self):
            at = (self.which, self.k)
            self.across.wait_recv()
            mine_r, mine_i = edge_sum[self.k, odd, 0], edge_sum[self.k, odd, 1]
            other_r, other_i = pair_recv[(*at, odd, 0)].astype(f32), pair_recv[(*at, odd, 1)].astype(f32)
            flag = jnp.where(odd == 1, *[pair_flags[0 if self.reverse else 1][b] for b in (1, 0)])
            lr, li = jnp.where(self.leads, mine_r, other_r), jnp.where(self.leads, mine_i, other_i)
            tr, ti = jnp.where(self.leads, other_r, mine_r), jnp.where(self.leads, other_i, mine_i)
            ar, ai = self.advance(flag, lr, li, self.sr, self.si)
            line_send[(*at, 0)] = (ar + tr).astype(bf16)
            line_send[(*at, 1)] = (ai + ti).astype(bf16)
            for d in range(1, pairs):
                to = level - d if self.reverse else level + d

                @pl.when(to >= 0 if self.reverse else to < pairs)
                def _(d=d, to=to):
                    self.onward(d, (2 * to + odd, c)).start()

        def onward(self, d, to=partner):
            return self.copy(line_send, line_recv.at[self.which, self.k, d - 1], 1 + d, to)

        def home(self):
            at = (self.which, self.k)
            dr, di = cmul(self.sr, self.si, self.sr, self.si)
            back_send[...] = jnp.zeros(back_send.shape, f32)
            for d in range(pairs - 1, 0, -1):
                source = level + d if self.reverse else level - d

                @pl.when(source < pairs if self.reverse else source >= 0)
                def _(d=d):
                    self.onward(d).wait_recv()
                    flag = line_flags[self.reverse][d - 1]
                    vr, vi = self.advance(flag, back_send[0], back_send[1], dr, di)
                    back_send[0] = vr + line_recv[(*at, d - 1, 0)].astype(f32)
                    back_send[1] = vi + line_recv[(*at, d - 1, 1)].astype(f32)

            back_low[at] = back_send[...].astype(bf16)
            self.back = self.copy(back_low, back_recv.at[at], 1, partner)
            self.back.start()

        def end(self):
            at = (self.which, self.k)
            cols = pl.ds(self.k * LANES, LANES)
            self.back.wait_recv()
            for b in range(streams):
                flag = pair_flags[1 if self.reverse else 0][b]
                near = [
                    jnp.where(odd == b, back_low[(*at, i)], back_recv[(*at, i)]).astype(f32) for i in range(2)
                ]
                far = self.advance(flag, *near, self.sr, self.si)
                for i in range(2):
                    other = far[i] + pair_recv[(*at, b, i)].astype(f32)
                    self.target[b, i, :, cols] = jnp.where(self.leads, near[i], other)

        def finish(self):
            self.across.wait_send()
            self.back.wait_send()

            for d in range(1, pairs):
                to = level - d if self.reverse else level + d

                @pl.when(to >= 0 if self.reverse else to < pairs)
                def _(d=d):
                    self.onward(d).wait_send()

    low_side = level < pairs // 2
    toward = (s + jnp.where(low_side, 2, -2), c)
    away = (s + jnp.where(low_side, -2, 2), c)
    where = (
        pairs,
        jnp.logical_or(level == 0, level == pairs - 1),
        jnp.logical_or(level == pairs // 2 - 1, level == pairs // 2),
        toward, away, partner,
    )
    factors = []

    def swap_factor(src, dst, k, to=partner):
        copy = pltpu.make_async_remote_copy(
            src_ref=src, dst_ref=dst, send_sem=fac_send.at[k], recv_sem=fac_recv.at[k], device_id=to, device_id_type=MESH
        )
        copy.start()
        factors.append(copy)
        return copy

    half_units = units // 2
    my_half = chan_block(odd, half_units)
    their_half = chan_block(1 - odd, half_units)
    wanted = {}

    def need(*names):
        for name in names:
            wanted[name].wait_recv()

    in_rows, in_cols = full // 4, units // 4
    out_rows, out_cols = units // 4, full // 4
    glu_rows, glu_half = full // 4, width // 2
    my_glu, their_glu = chan_block(odd, glu_half), chan_block(1 - odd, glu_half)

    ready = []

    def in_own(i):
        assert "mid" in ready
        if i == 0:
            need("pre")
        rows, cols = pl.ds((i // 2) * in_rows, in_rows), (i % 2) * in_cols
        mine = pl.ds(pl.multiple_of(odd * half_units + cols, in_cols), in_cols)
        return dot(mid_t[rows, :], pre[:, mine]) + dot(mid_t2[rows, :], pre2[:, pl.ds(cols, in_cols)])

    def in_at(i):
        return gin_out.at[odd, i // 2, i % 2]

    def out_own(i):
        if i == 0:
            need("grad", ("hidden", 0))
        if i == 4:
            need(("hidden", 1))
        rows, cols = (i // 4) * out_rows, pl.ds((i % 4) * out_cols, out_cols)
        mine = pl.ds(pl.multiple_of(odd * half_units + rows, out_rows), out_rows)
        return dot(hidden_t[mine, :], grad_full[:, cols]) + dot(hidden_t2[pl.ds(rows, out_rows), :], grad2[:, cols])

    def out_at(i):
        return gout_out.at[odd, i // 4, i % 4]

    def glu_own(near, far, names):
        def own(i):
            if i == 0:
                need(*names)
            assert "act" in ready
            rows = pl.ds(i * glu_rows, glu_rows)
            return dot(act_t[rows, :], near[:, my_glu]) + dot(act_t2[rows, :], far[...])

        return own

    def glu_at(out):
        def at(i):
            return out.at[odd, i]

        return at

    def table_own(q):
        need(("table", q))
        return table[q] + table2[q]

    sem_at = [0, 0]

    storing, stored = [], [0]

    def line(own, count, at, bufs, hand_over, kept_at=None):
        spot = pl.ds(sem_at[0], count)
        turns = pl.ds(sem_at[1], min(count, TURNS[0]))
        stores = None
        if kept_at:
            held, final, place = kept_at

            def stores(i):
                turn = stored[0] % 4
                stored[0] += 1
                if len(storing) == 4:
                    for copy in storing.pop(0):
                        copy.wait()
                copies = [
                    pltpu.make_async_copy(held.at[(x, *place(i))], final.at[(x, *place(i))], save_sem.at[x, turn]) for x in range(2)
                ]
                for copy in copies:
                    copy.start()
                storing.append(copies)

        sem_at[0] += count
        sem_at[1] += min(count, TURNS[0])
        return Line(own, count, at, *bufs, (line_sent.at[:, turns], line_got.at[:, spot]), where, hand_over, stores)

    quarters = (width // LANES) * (n_states // group)
    in_line = line(in_own, 8, in_at, (in_send, in_in, in_across), True, (gin_out, gin_hbm, lambda i: (i // 2, i % 2)))
    out_line = line(out_own, 8, out_at, (out_send, out_in, out_across), True, (gout_out, gout_hbm, lambda i: (i // 4, i % 4)))
    gv_line = line(glu_own(value_grad, value2, ("value",)), 4, glu_at(gv_out), (gv_send, gv_in, gv_across), True, (gv_out, gv_hbm, lambda i: (i,)))
    gg_line = line(glu_own(gate_grad, gate2, ("gate",)), 4, glu_at(gg_out), (gg_send, gg_in, gg_across), True, (gg_out, gg_hbm, lambda i: (i,)))
    table_line = line(table_own, quarters, lambda q: table_sum.at[q], (table_send, table_in, table_across), False)
    lines = [out_line, gv_line, in_line, gg_line, table_line]
    pieces = [(entry, i) for entry in lines[:4] for i in range(entry.count)]
    tick, begun = [0], [0]
    MID, LAST, STORE = 2, 4, 8

    def launch(count):
        for _ in range(count):
            if begun[0] < len(pieces):
                entry, i = pieces[begun[0]]
                entry.begin(i)
            begun[0] += 1

    def pump(count, lead=4):
        for _ in range(count):
            t = tick[0]
            tick[0] += 1
            launch(t + 1 + lead - begun[0])
            for ahead, act in ((0, "join"), (-MID, "settle"), (-LAST, "relay"), (-STORE, "store")):
                if 0 <= t + ahead < len(pieces):
                    entry, i = pieces[t + ahead]
                    getattr(entry, act)(i)

    forward = [Carry(init, 0, False, k) for k in range(tiles)]
    for k in range(tiles):
        edges(u_ref, last_mask, False, k)
        forward[k].start()
    unit_block = min(units, 256)

    def hidden_grad_part(i):
        cols = pl.ds(i * unit_block, unit_block)
        hidden_grad[:, cols] = dot(grad_full[...], wout[cols, :], NT)

    loads[0].wait()
    landed(grad_copies)
    blocks = units // unit_block
    for k in range(blocks // 2):
        hidden_grad_part(k)
    for k in range(tiles):
        forward[k].line()
    for k in range(blocks // 2, blocks):
        hidden_grad_part(k)
    for k in range(tiles):
        forward[k].home()
    wanted["grad"] = swap_factor(grad_full, grad2, 0)
    act_copies = []
    for k in range(tiles):
        forward[k].end()
        cols = pl.ds(k * LANES, LANES)
        u_rows[k] = u_ref[:, :, cols]
        near = [jnp.sum(coef[0, :, cols], axis=0, keepdims=True)]
        qr, qi = coef[0, :, cols], coef[1, :, cols]
        for _ in range(3):
            qr, qi = cmul(qr, qi, lam[0, :, cols], lam[1, :, cols])
            near.append(jnp.sum(qr, axis=0, keepdims=True))
        fours = length // 4
        local, through = [], []
        for b in range(streams):
            us = [u_rows[k, b, pl.ds(j, fours, stride=4), :] for j in range(4)]
            ks = [keep[b, pl.ds(j, fours, stride=4), :] for j in range(4)]
            reach = ks[0]
            passed_by = [reach]
            for j in range(1, 4):
                reach = reach * ks[j]
                passed_by.append(reach)
            through.append(passed_by)
            keep4[b] = reach
            terms, outs = [], []
            for j in range(4):
                terms = [term * ks[j] for term in terms] + [us[j]]
                out = skip_ref[:, cols] * us[j]
                for i, term in enumerate(terms):
                    out = out + near[j - i] * term
                outs.append(out)
            local.append(outs)
            for j in range(4):
                tails[b, j] = terms[j]
        for h in range(n_states // group):
            rows = pl.ds(h * group, group)
            l1r, l1i = tile(lam, (0,), rows, cols), tile(lam, (1,), rows, cols)
            l2r, l2i = cmul(l1r, l1i, l1r, l1i)
            l3r, l3i = cmul(l2r, l2i, l1r, l1i)
            l4r, l4i = cmul(l2r, l2i, l2r, l2i)
            cr, ci = tile(coef, (0,), rows, cols), tile(coef, (1,), rows, cols)
            taps = [cmul(cr, ci, *power_of) for power_of in ((l1r, l1i), (l2r, l2i), (l3r, l3i), (l4r, l4i))]

            def move(i, carry, h=h, l1=(l1r, l1i), l2=(l2r, l2i), l3=(l3r, l3i), l4=(l4r, l4i), taps=taps):
                new = []
                for b in range(streams):
                    sr, si = carry[2 * b], carry[2 * b + 1]
                    for j in range(4):
                        spot = pl.ds(pl.multiple_of(((b * 4 + j) * fours + i) * 8, 8), 8)
                        out = (taps[j][0] * sr - taps[j][1] * si).sum(0)
                        if h == 0:
                            part[spot, :] = out
                        else:
                            part[spot, :] += out
                    m = row(keep4, b, i)
                    t = [row(tails.at[b], j, i) for j in range(4)]
                    sr = sr * m
                    si = si * m
                    nr = (l4[0] * sr - l4[1] * si) + (l3[0] * t[0] + l2[0] * t[1]) + (l1[0] * t[2] + t[3])
                    ni = (l4[0] * si + l4[1] * sr) + (l3[1] * t[0] + l2[1] * t[1]) + l1[1] * t[2]
                    new += [nr, ni]
                return tuple(new)

            begin = []
            for b in range(streams):
                begin += [tile(init, (b, 0), rows, cols), tile(init, (b, 1), rows, cols)]
            lax.fori_loop(0, fours, move, tuple(begin), unroll=2)
        for b in range(streams):
            for j in range(4):
                first = (b * 4 + j) * fours * 8
                total = part[pl.ds(first, fours, stride=8), :]
                for i in range(1, 8):
                    total = total + part[pl.ds(first + i, fours, stride=8), :]
                row_a[b, pl.ds(j, fours, stride=4), :] = through[b][j] * total + local[b][j]
            y = row_a[b]
            y_ref[b, :, cols] = y
            to = pl.ds(pl.multiple_of(c * width + k * LANES, LANES), LANES)
            here = pl.ds(b * length, length)
            act_full[here, to] = gelu_parts(y)[0].astype(bf16)
            act_copies.append(
                chan_all(lambda j: (act_full.at[here, to], act_full.at[here, to]), 2 + streams * k + b)
            )
    base = 2 + streams * tiles

    def again_pass(q):
        k, h = q // (n_states // group), q % (n_states // group)
        rows, cols = pl.ds(h * group, group), pl.ds(k * LANES, LANES)
        lr, li = tile(lam, (0,), rows, cols), tile(lam, (1,), rows, cols)
        held = states.at[q % 2]

        def again(p, carry):
            new = []
            for b in range(streams):
                sr, si = carry[2 * b], carry[2 * b + 1]
                u = row(u_rows.at[k], b, p)
                m = row(keep, b, p)
                sr = sr * m
                si = si * m
                nr = (lr * sr - li * si) + u
                ni = lr * si + li * sr
                held[p + 1, b, 0] = nr
                held[p + 1, b, 1] = ni
                new += [nr, ni]
            return tuple(new)

        begin = []
        for b in range(streams):
            begin += [tile(init, (b, 0), rows, cols), tile(init, (b, 1), rows, cols)]
            held[0, b, 0] = begin[-2]
            held[0, b, 1] = begin[-1]
        lax.fori_loop(0, length, again, tuple(begin), unroll=2)

    loads[1].wait()
    loads[2].wait()
    for copies in act_copies:
        landed(copies)
    beside = (s, c + 1 - 2 * lax.rem(c, 2))
    core_half = chan_block(lax.rem(c, 2), tokens // 2)
    wanted["act_near"] = swap_factor(act_full.at[core_half, :], act2.at[core_half, :], 1)
    val[...] = dot(act_full[...], gluv[...])
    gate[...] = jax.nn.sigmoid(dot(act_full[...], glug[...]))
    resid[...] = rows_in_of(x_ref, tokens, width) + val[...] * gate[...]

    sum2 = jnp.sum(resid[...], axis=1, keepdims=True)
    square2 = jnp.sum(resid[...] * resid[...], axis=1, keepdims=True)
    mid2[:, own_cols] = (resid[...] - sum2 / width).astype(bf16)
    stat_copies = stats_start(sum2, square2, 1, base)
    mid_copies = chan_all(lambda j: (mid2.at[:, own_cols], mid2.at[:, own_cols]), base + 1)
    landed(gain_copies)
    landed(stat_copies)
    shares = [stat_send[1], *[stat_recv[1, j - 1] for j in range(1, n_chan)]]
    shares = jnp.concatenate([*shares, jnp.zeros((LANES - 8 * n_chan, tokens), f32)], axis=0).T
    average, square = 0.0, 0.0
    for j in range(n_chan):
        average = average + shares[:, 8 * j : 8 * j + 1] / full
        square = square + shares[:, 8 * j + 1 : 8 * j + 2] / full
    scaler2 = lax.rsqrt(square - average * average + epsilon)
    normed2[...] = (resid[...] - average) * scaler2
    mid_full[:, own_cols] = (normed2[...] * gain2[...]).astype(bf16)
    landed(mid_copies)
    for j in range(1, n_chan):
        cols = chan_block(lax.rem(c - j + n_chan, n_chan), width)
        shift = shares[:, 8 * j : 8 * j + 1] / width - average
        mid_full[:, cols] = ((mid2[:, cols].astype(f32) + shift) * scaler2 * gain_full[0:1, cols]).astype(bf16)
    loads[3].wait()

    for k in range(4):
        cols = pl.ds(k * out_rows, out_rows)
        value, slope = gelu_parts(dot(mid_full[...], win[:, cols]))
        hidden[:, cols] = value.astype(bf16)
        pre[:, cols] = (hidden_grad[:, cols] * slope).astype(bf16)
        hidden_t[cols, :] = hidden[:, cols].T
    for k in range(2):
        theirs = pl.ds(pl.multiple_of((1 - odd) * half_units + k * out_rows, out_rows), out_rows)
        wanted["hidden", k] = swap_factor(
            hidden_t.at[theirs, :], hidden_t2.at[pl.ds(k * out_rows, out_rows), :], 4 if k == 0 else 10 + quarters
        )

    def scatter_fill(piece, own, k):
        for j in range(1, n_chan):
            rs_send[k, j - 1] = piece(chan_block(chan_peer(j), width)).astype(bf16)
        own[...] = piece(own_cols)

    def scatter_start(k, phase):
        return chan_all(lambda j: (rs_send.at[k, j - 1], rs_recv.at[k, j - 1]), phase)

    def transposed(source, target, count):
        for k in range(count):
            target[pl.ds(k * width, width), :] = source[:, k * width : (k + 1) * width].T

    def scatter_end(copies, own, k):
        landed(copies)
        total = own[...]
        for j in range(1, n_chan):
            total = total + rs_recv[k, j - 1].astype(f32)
        return total

    scatter_fill(lambda rows: dot(pre[...], win[rows, :], NT), part_own, 0)
    grad_parts = scatter_start(0, base + 2)
    for copy in mid_copies:
        copy.wait_send()
    mid_copies.clear()
    first, second = 0.0, 0.0
    for j in range(n_chan):
        cols = chan_block(chan_peer(j), width) if j else own_cols
        values = rs_send[0, j - 1].astype(f32) if j else part_own[...]
        first = first + jnp.sum(values * gain_full[0:1, cols], axis=1, keepdims=True)
        second = second + jnp.sum(values * mid_full[:, cols].astype(f32), axis=1, keepdims=True)
    stat_copies = stats_start(first, second, 2, base + 4)
    scatter_fill(lambda cols: dot(hidden[...], wout[:, cols]), result_own, 1)
    transposed(act_full, act_t, n_chan)
    transposed(mid_full, mid_t, n_chan)
    wanted["act_near"].wait_recv()
    wanted["act_far"] = swap_factor(act2.at[core_half, :], act2.at[core_half, :], 9, beside)
    for q in range(min(2, quarters)):
        again_pass(q)
    launch(4)
    resid_grad[...] = scatter_end(grad_parts, part_own, 0)
    wanted["pre"] = swap_factor(pre.at[:, their_half], pre2, 5)
    gains = jnp.sum(resid_grad[...] * normed2[...], axis=0, keepdims=True)
    first, second = stats_end(stat_copies, 2)
    resid_grad[...] = og_ref[...].reshape(tokens, width) + scaler2 * (
        resid_grad[...] * gain2[...] - first - normed2[...] * second
    )

    value_grad[...] = (resid_grad[...] * gate[...]).astype(bf16)
    gate_grad[...] = (resid_grad[...] * val[...] * gate[...] * (1.0 - gate[...])).astype(bf16)
    scatter_fill(
        lambda rows: dot(value_grad[...], gluv[rows, :], NT) + dot(gate_grad[...], glug[rows, :], NT), val, 2
    )
    act_parts = scatter_start(2, base + 5)
    wanted["value"] = swap_factor(value_grad.at[:, their_glu], value2, 6)
    wanted["gate"] = swap_factor(gate_grad.at[:, their_glu], gate2, 7)
    pump(2, 2)
    act_grad = scatter_end(act_parts, val, 2)
    mixer_grad[...] = act_grad.reshape(streams, length, width) * gelu_parts(y_ref[...])[1]

    out_parts = scatter_start(1, base + 3)

    backward = [Carry(adj, 1, True, k) for k in range(tiles)]
    for k in range(tiles):
        edges(mixer_grad, first_mask, True, k)
        backward[k].start()
        if k == 0:
            pump(1, 2)
    pump(1, 2)
    for k in range(tiles):
        backward[k].line()
    wanted["mid_near"] = swap_factor(mid_full.at[core_half, :], mid2.at[core_half, :], 2)
    pump(1, 2)
    total = scatter_end(out_parts, result_own, 1)
    block_out[...] = (resid[...] + total).reshape(streams, length, width)
    save(block_out, block_hbm, 0)
    for k in range(tiles):
        backward[k].home()
    need("act_far")
    transposed(act2, act_t2, n_chan)
    ready.append("act")
    pump(2)
    zero = jnp.zeros((group // 8, 8, LANES), f32)
    q = 0

    def tables(**steps):
        for act, i in steps.items():
            if 0 <= i < quarters:
                getattr(table_line, act)(i)

    for k in range(width // LANES):
        backward[k].end()
        cols = pl.ds(k * LANES, LANES)
        row_b[...] = mixer_grad[:, :, cols]
        for h in range(n_states // group):
            rows = pl.ds(h * group, group)
            lr, li = tile(lam, (0,), rows, cols), tile(lam, (1,), rows, cols)
            cr, ci = tile(coef, (0,), rows, cols), tile(coef, (1,), rows, cols)

            if q > 1:
                again_pass(q)
            pump(2, 3)
            if q == 0:
                wanted["mid_near"].wait_recv()
                wanted["mid_far"] = swap_factor(mid2.at[core_half, :], mid2.at[core_half, :], 3, beside)
            tables(begin=q - 1, join=q - 2, relay=q - 3)
            held = states.at[q % 2]

            def back(i, carry, h=h, held=held, lr=lr, li=li, cr=cr, ci=ci):
                glr, gli, gcr, gci = carry[:4]
                adjoint = carry[4:]
                p = length - 1 - i
                new = []
                for b in range(streams):
                    ar, ai = adjoint[2 * b], adjoint[2 * b + 1]
                    g = row(row_b, b, p)
                    m = row(keep, b, p)
                    nr = (lr * ar + li * ai) + cr * g
                    ni = (lr * ai - li * ar) - ci * g
                    spot = pl.ds(pl.multiple_of((b * length + p) * 8, 8), 8)
                    if h == 0:
                        part[spot, :] = nr.sum(0)
                    else:
                        part[spot, :] += nr.sum(0)
                    gcr = gcr + g * held[p + 1, b, 0]
                    gci = gci - g * held[p + 1, b, 1]
                    nr = nr * m
                    ni = ni * m
                    sr, si = held[p, b, 0], held[p, b, 1]
                    glr = glr + (nr * sr + ni * si)
                    gli = gli + (ni * sr - nr * si)
                    new += [nr, ni]
                return (glr, gli, gcr, gci, *new)

            begin = []
            for b in range(streams):
                begin += [tile(adj, (b, 0), rows, cols), tile(adj, (b, 1), rows, cols)]
            sums = lax.fori_loop(0, length, back, (zero, zero, zero, zero, *begin), unroll=2)
            glr, gli, gcr, gci = [item.reshape(-1, LANES) for item in sums[:4]]
            share = factor[rows, cols]
            ratio = (1.0 - share * share) / share
            spots = [pl.ds(i * group, group) for i in range(4)]
            table[q, spots[0], :] = (gcr * real_ref[rows, cols] + gci * imag_ref[rows, cols]) * ratio - (
                glr * lam[0, rows, cols] + gli * lam[1, rows, cols]
            )
            table[q, spots[1], :] = gli * lam[0, rows, cols] - glr * lam[1, rows, cols]
            table[q, spots[2], :] = share * gcr
            table[q, spots[3], :] = share * gci
            wanted["table", q] = swap_factor(table.at[q], table2.at[q], 10 + q)
            if q == 0:
                need("mid_far")
                transposed(mid2, mid_t2, n_chan)
                ready.append("mid")
            pump(2, 3)
            tables(settle=q - 2)
            q += 1
        for b in range(streams):
            total = part[pl.ds(b * length * 8, length, stride=8), :]
            for j in range(1, 8):
                total = total + part[pl.ds(b * length * 8 + j, length, stride=8), :]
            u_grad = total + skip_ref[:, cols] * row_b[b]
            part_own[b * length : (b + 1) * length, cols] = u_grad * valid[b]

    last = quarters - 1
    scaled = part_own[...] * gain1[...]
    stat_copies = stats_start(
        jnp.sum(scaled, axis=1, keepdims=True),
        jnp.sum(scaled * normed1[...], axis=1, keepdims=True), 3, base + 6,
    )
    gain_rows = [
        jnp.sum(part_own[...] * normed1[...], axis=0, keepdims=True),
        jnp.sum(jnp.sum(mixer_grad[...] * u_ref[...], axis=0), axis=0, keepdims=True),
        gains,
    ]
    gain_all[s] = jnp.concatenate([*gain_rows, jnp.zeros((5, width), f32)], axis=0)
    for d in range(1, n_seq):
        copy = pltpu.make_async_remote_copy(
            src_ref=gain_all.at[s], dst_ref=gain_all.at[s], send_sem=gain_send.at[d], recv_sem=gain_recv.at[s],
            device_id=(lax.rem(s + d, n_seq), c), device_id_type=MESH,
        )
        copy.start()
        sent.append(copy)
    pump(1)
    tables(join=last - 1, relay=last - 2)
    pump(1)
    tables(begin=last)
    pump(1)
    tables(settle=last - 1)
    first, second = stats_end(stat_copies, 3)
    in_grad[...] = (
        resid_grad[...] + scaler1 * (part_own[...] * gain1[...] - first - normed1[...] * second)
    ).reshape(streams, length, width)
    save(in_grad, grad_hbm, 1)
    tables(join=last)
    pump(1)
    tables(relay=last - 1)
    pump(1)
    tables(settle=last)
    pump(1)
    tables(relay=last)
    while tick[0] < len(pieces) + STORE:
        pump(1)
    for q in range(quarters):
        save(table_sum.at[q], tables_hbm.at[q], 3 + q)
    for d in range(1, n_seq):
        source = lax.rem(s + d, n_seq)
        pltpu.make_async_remote_copy(
            src_ref=gain_all.at[s], dst_ref=gain_all.at[source], send_sem=gain_send.at[d], recv_sem=gain_recv.at[source],
            device_id=(source, c), device_id_type=MESH,
        ).wait_recv()
    total = gain_all[0]
    for k in range(1, n_seq):
        total = total + gain_all[k]
    gains_out[...] = total
    save(gains_out, gains_hbm, 2)
    for entry in lines:
        entry.finish()
    for copy in factors:
        copy.wait_send()
    for copy in (*saved, *sum(storing, [])):
        copy.wait()
    for copy in (*sent, *sum(chan_turns, [])):
        copy.wait_send()
    for carry in (*forward, *backward):
        carry.finish()


def rows_in_of(ref, tokens, width):
    return ref[...].reshape(tokens, width)


def cast_kernel(
    steps, gin, gout, gv, gg, block, grad, tables, gains,
    gin_hbm, gout_hbm, gv_hbm, gg_hbm, block_out, grad_out, dec_out, ang_out, real_out, imag_out, gain_a, gain_b, gain_c,
    gin_low, gout_low, gv_low, gg_low, gin_out, gout_out, gv_out, gg_out, table_low, gain_low, block_low, grad_low, load_sem, save_sem, small_sem,
):
    whole = [
        pltpu.make_async_copy(src, dst, small_sem.at[i])
        for i, (src, dst) in enumerate(
            [(tables, table_low), (gains, gain_low), (block, block_low), (grad, grad_low)]
        )
    ]
    full, units = gin_out.shape
    rows, tall = full // steps, units // steps
    loads, saves = [], []
    for p in range(steps):
        here, tall_here = pl.ds(p * rows, rows), pl.ds(p * tall, tall)
        loads.append(
            [
                pltpu.make_async_copy(gin.at[:, p], gin_low.at[:, p], load_sem.at[0, p]),
                pltpu.make_async_copy(gout.at[p // 2, p % 2], gout_low.at[p // 2, p % 2], load_sem.at[1, p]),
                pltpu.make_async_copy(gv.at[:, p], gv_low.at[:, p], load_sem.at[2, p]),
                pltpu.make_async_copy(gg.at[:, p], gg_low.at[:, p], load_sem.at[3, p]),
            ]
        )
        saves.append(
            [
                pltpu.make_async_copy(gin_out.at[here], gin_hbm.at[here], save_sem.at[0, p]),
                pltpu.make_async_copy(gout_out.at[tall_here], gout_hbm.at[tall_here], save_sem.at[1, p]),
                pltpu.make_async_copy(gv_out.at[here], gv_hbm.at[here], save_sem.at[2, p]),
                pltpu.make_async_copy(gg_out.at[here], gg_hbm.at[here], save_sem.at[3, p]),
            ]
        )
    for copies in loads:
        for copy in copies:
            copy.start()
    for copy in whole:
        copy.start()
    for p in range(steps):
        here, tall_here = slice(p * rows, (p + 1) * rows), slice(p * tall, (p + 1) * tall)
        for copy in loads[p]:
            copy.wait()
        for i in range(4):
            cols = slice(i * tall, (i + 1) * tall)
            gin_out[here, cols] = gin_low[i // 2, p, i % 2].astype(f32)
        for i in range(4):
            cols = slice(i * rows, (i + 1) * rows)
            gout_out[tall_here, cols] = gout_low[p // 2, p % 2, i].astype(f32)
        for x in range(2):
            cols = slice(x * gv.shape[-1], (x + 1) * gv.shape[-1])
            gv_out[here, cols] = gv_low[x, p].astype(f32)
            gg_out[here, cols] = gg_low[x, p].astype(f32)
        for copy in saves[p]:
            copy.start()
    for copy in whole:
        copy.wait()
    passed_on = [
        pltpu.make_async_copy(block_low, block_out, small_sem.at[4]),
        pltpu.make_async_copy(grad_low, grad_out, small_sem.at[5]),
    ]
    for copy in passed_on:
        copy.start()
    group, lanes = table_low.shape[1] // 4, table_low.shape[2]
    halves = dec_out.shape[0] // group
    for q in range(table_low.shape[0]):
        rows = slice(q % halves * group, (q % halves + 1) * group)
        cols = slice(q // halves * lanes, (q // halves + 1) * lanes)
        for k, out in enumerate((dec_out, ang_out, real_out, imag_out)):
            out[rows, cols] = table_low[q, k * group : (k + 1) * group, :]
    for k, out in enumerate((gain_a, gain_b, gain_c)):
        out[...] = gain_low[k : k + 1, :]
    for copies in (*saves, passed_on):
        for copy in copies:
            copy.wait()


def per_device(
    sizes, block_in, doc_lengths, out_grad, first_gain, decay_rate, turn_angle, out_real, out_imag,
    skip_gain, glu_value, glu_gate, second_gain, ffn_in, ffn_out,
):
    n_seq, n_chan = sizes
    pairs = n_seq // 2
    streams, length, width = block_in.shape
    n_states = decay_rate.shape[1]
    tokens = streams * length
    full = width * n_chan
    units = ffn_in.shape[1]
    glu_cols = glu_value.shape[1]
    group = min(32, n_states)
    like = jax.ShapeDtypeStruct
    quarters = (width // LANES) * (n_states // group)
    phases = 10 + streams * (width // LANES)
    act = (streams, length, width)
    flat = (tokens, width)
    mask = (streams, length, LANES)
    tab, lane_tab = (2, n_states, width), (2, n_states, LANES)
    tiles = width // LANES
    V = pltpu.VMEM
    scratch = [
        V(act, f32), V(act, f32), V((8, width), f32),
        V((2, 4, 2, full // 4, units // 4), bf16), V((2, 2, 4, units // 4, full // 4), bf16), *[V((2, 4, full // 4, glu_cols // 2), bf16)] * 2,
        V((full, glu_cols), bf16), V((full, glu_cols), bf16), V((full, units), bf16), V((units, full), bf16),
        V(act, f32), V(act, f32), *[V((n_states, width), f32)] * 4,
        V(mask, f32), V(mask, f32), V(mask, f32), V(mask, f32),
        V(tab, f32), V(tab, f32), V(tab, f32), V((n_states, width), f32),
        V((8, full), f32), V(flat, f32), V(act, f32), V(act, f32), V((tiles, streams, 2, n_states, LANES), f32), V((streams, *tab), f32), V((streams, *tab), f32),
        V((tokens, full), bf16), V((tokens, glu_cols), f32), V((tokens, glu_cols), f32), V(flat, f32), V(flat, f32),
        V((tokens, full), bf16), V((tokens, full), bf16), V((tokens, units), f32), V((tokens, units), bf16), V((tokens, units), bf16),
        V((full, tokens), bf16), V((full, tokens), bf16), V((units, tokens), bf16),
        V(flat, f32), V(flat, f32), V(flat, f32), V((tokens, glu_cols), bf16), V((tokens, glu_cols), bf16),
        V(act, f32),
        V(mask, f32), V(mask, f32), V((tiles, *mask), f32), V((streams, length // 4, LANES), f32), V((streams, 4, length // 4, LANES), f32), V((tokens * 8, LANES), f32), V((2, length + 1, streams, 2, group // 8, 8, LANES), f32),
        V((4, 8, tokens), f32), V((4, n_chan - 1, 8, tokens), f32), V((3, n_chan - 1, *flat), bf16), V((3, n_chan - 1, *flat), bf16),
        *[V((2, tiles, streams, *lane_tab), bf16)] * 2, V((2, tiles, *lane_tab), bf16), V((2, tiles, pairs - 1, *lane_tab), bf16),
        V(lane_tab, f32), *[V((2, tiles, *lane_tab), bf16)] * 2,
        *[V((quarters, 4 * group, LANES), f32)] * 6,
        V((n_seq, 8, width), f32),
        *[V((tokens, full), bf16)] * 3, V((full, tokens), bf16), V((full, tokens), bf16), V((units // 2, tokens), bf16),
        V((tokens, units // 2), bf16), V((tokens, glu_cols // 2), bf16), V((tokens, glu_cols // 2), bf16),
        *[V((8, full // 4, units // 4), bf16)] * 3, *[V((8, units // 4, full // 4), bf16)] * 3,
        *[V((4, full // 4, glu_cols // 2), bf16)] * 6,
        pltpu.SemaphoreType.DMA((10,)), pltpu.SemaphoreType.DMA((2, 4)), pltpu.SemaphoreType.DMA((3 + quarters,)),
        pltpu.SemaphoreType.DMA((6, n_chan - 1)), pltpu.SemaphoreType.DMA((phases, n_chan - 1)),
        pltpu.SemaphoreType.DMA((2, tiles, pairs + 1)), pltpu.SemaphoreType.DMA((2, tiles, pairs + 1)),
        pltpu.SemaphoreType.DMA((11 + quarters,)), pltpu.SemaphoreType.DMA((11 + quarters,)),
        pltpu.SemaphoreType.DMA((n_seq,)), pltpu.SemaphoreType.DMA((n_seq,)),
        pltpu.SemaphoreType.DMA((3, 24 + quarters)), pltpu.SemaphoreType.DMA((4, 24 + quarters)),
    ]
    specs = [pl.BlockSpec(memory_space=pltpu.SMEM), ANY, ANY, VM, ANY, ANY, ANY, ANY, VM, ANY, ANY, VM, ANY, ANY]
    made = pl.pallas_call(
        functools.partial(block_kernel, sizes),
        out_shape=(
            like(act, f32), like(act, f32), like((quarters, 4 * group, LANES), f32), like((8, width), f32),
            like((2, 4, 2, full // 4, units // 4), bf16), like((2, 2, 4, units // 4, full // 4), bf16),
            like((2, 4, full // 4, glu_cols // 2), bf16), like((2, 4, full // 4, glu_cols // 2), bf16),
        ),
        in_specs=specs,
        out_specs=(ANY,) * 8,
        scratch_shapes=scratch,
        compiler_params=pltpu.CompilerParams(
            collective_id=0, has_side_effects=True, vmem_limit_bytes=60 * 1024 * 1024
        ),
        name="block",
    )(
        doc_lengths, block_in, out_grad, first_gain[None], decay_rate.T, turn_angle.T, out_real.T, out_imag.T, skip_gain[None],
        glu_value, glu_gate, second_gain[None], ffn_in, ffn_out,
    )
    block_out, in_grad, tables, gains, gin, gout, gv, gg = made
    steps = 4
    small = (n_states, width)
    cast = pl.pallas_call(
        functools.partial(cast_kernel, steps),
        out_shape=(
            like((full, units), f32), like((units, full), f32), like((full, glu_cols), f32), like((full, glu_cols), f32),
            like(act, f32), like(act, f32), like(small, f32), like(small, f32), like(small, f32), like(small, f32),
            *[like((1, width), f32)] * 3,
        ),
        in_specs=[ANY] * 8,
        out_specs=(ANY,) * 6 + (VM,) * 7,
        scratch_shapes=[
            V(gin.shape, bf16), V(gout.shape, bf16), V(gv.shape, bf16), V(gg.shape, bf16),
            V((full, units), f32), V((units, full), f32), V((full, glu_cols), f32), V((full, glu_cols), f32),
            V(tables.shape, f32), V(gains.shape, f32), V(act, f32), V(act, f32),
            pltpu.SemaphoreType.DMA((4, steps)), pltpu.SemaphoreType.DMA((4, steps)), pltpu.SemaphoreType.DMA((6,)),
        ],
        compiler_params=pltpu.CompilerParams(vmem_limit_bytes=58 * 1024 * 1024),
        name="cast",
    )(gin, gout, gv, gg, block_out, in_grad, tables, gains)
    gin, gout, gv, gg, block_out, in_grad, dec, ang, real, imag, *gains = cast
    return (
        block_out, in_grad, gains[0][0], dec.T, ang.T, real.T, imag.T, gains[1][0], gv, gg, gains[2][0], gin, gout,
    )


def solution(mesh):
    act = P(None, "seq", "chan")
    vec, mat = P("chan"), P("chan", None)
    col = P(None, "chan")
    sizes = (mesh.shape["seq"], mesh.shape["chan"])
    return jax.shard_map(
        functools.partial(per_device, sizes),
        mesh=mesh,
        in_specs=(act, P(), act, vec, mat, mat, mat, mat, vec, col, col, vec, col, mat),
        out_specs=(act, act, vec, mat, mat, mat, mat, vec, col, col, vec, col, mat),
        check_vma=False,
    )
```
